32 devices in a mesh: group: 2 (over y), sess: 4 (over z), head: 2 (over x), dp: 2 (over core).
Axes of the slice: x: 2, y: 2, z: 4, core: 2. Of those that a mesh axis runs over, the one named last changes fastest.
Arguments:
- x_rows: bfloat16 [32, 128, 2048], P(('group', 'sess', 'dp'), None, 'head'), parts along dimension 0, may hold values from -6 to 6
- z_rows: bfloat16 [32, 128, 2048], P(('group', 'sess', 'dp'), None, 'head'), parts along dimension 0, may hold values from -6 to 6
- input_projection_matrix: bfloat16 [32, 128, 256], P(('group', 'sess', 'dp')), parts along dimension 0, may hold values from -6 to 6
- c_rows: bfloat16 [32, 128, 256], P(('group', 'sess', 'dp')), parts along dimension 0, may hold values from -0.375 to 0.375
- dt_raw: float32 [32, 32, 128], P(('group', 'sess', 'dp'), 'head'), parts along dimension 0
- a_log: float32 [32], P('head'), may hold values from -5.8 to -2.3
- dt_bias: float32 [32], P('head'), may hold values from -1 to 1
- d_skip: float32 [32], P('head'), may hold values from 0.5 to 2
- norm_gain: bfloat16 [2048], P('head'), may hold values from 0.25 to 1.75
- cache_state: bfloat16 [16, 32, 64, 256], P(('group', 'sess', 'dp'), 'head'), parts along dimension 0, may hold values from -12 to 12
- lengths: int32 [16], P(('group', 'sess', 'dp')), parts along dimension 0, may hold values from 16 to 192
- slot_owner: int32 [4, 8], P('group'), parts along dimension 0, may hold values from 0 to 3, as said below
- slot_task: int32 [4, 8], P('group'), parts along dimension 0, may hold values from 0 to 1, as said below
Outputs:
- mixed_rows: bfloat16 [32, 128, 2048], P(('group', 'sess', 'dp'), None, 'head'), parts along dimension 0
- final_state: bfloat16 [16, 32, 64, 256], P(('group', 'sess', 'dp'), 'head'), parts along dimension 0
The draws below stay inside these ranges and needn't reach their ends.
There are 2 independent parts, one for each index of `group`. The reference program is written for one: setup_inputs(seed, part) draws one part's arguments, and reference() takes and returns one part's arrays. A program takes and returns all parts, laid end to end along the dimension named above; an argument that names none is the same for every part. Nothing has to cross between parts.
Inputs may be any that keep to these rules, and one draw needn't show every extreme that they name: `slot_owner`: in each dp index, the slots of one device belong to 2 different owners, and the 2 tasks of one owner lie on 2 different devices. `slot_task`: every task of every owner stands in exactly one slot of its dp index.
All inputs are finite; a program needn't handle non-finite values.
Results may differ from the reference program's by a relative error of at most 0.0063.
Values may be sent and summed in bfloat16 or wider, within the bound.
No kernel may reach another device: no remote copies, remote signals or barrier semaphores. Data moves between devices by JAX's collectives and lax.ppermute only.
A program may use at most 64 MiB of HBM per device.

```python
import jax
import jax.numpy as jnp
from jax import lax

HEAD_SIZE = 64
STATE = 256
BLOCK = 128
SESSIONS_PER_UNIT = 1
GROUP_HEADS = 32
HEADS = 32
GROUPS = 1
SLOTS_DEV = 2
SESSIONS = 8
SLOTS = 16
N_SESS = 4
N_DP = 2


def slot_tables(key):
    key_a = jax.random.fold_in(jax.random.fold_in(key, 77), 0)

    def column(key_col):
        key_shift, random_seed_ordering = jax.random.split(key_col)
        shift_values = jax.random.permutation(key_shift, N_SESS)[:SLOTS_DEV]
        orders = jax.vmap(lambda key_one: jax.random.permutation(key_one, SLOTS_DEV))(jax.random.split(random_seed_ordering, N_SESS))
        helper = jnp.arange(N_SESS)[:, None]
        owner_ids = (helper + shift_values[None, :]) % N_SESS
        job_identifiers = orders[owner_ids, jnp.arange(SLOTS_DEV)[None, :]]
        return (owner_ids.reshape(-1), job_identifiers.reshape(-1))
    owner_all, task_all = jax.vmap(column)(jax.random.split(key_a, N_DP))
    return (owner_all.astype(jnp.int32), task_all.astype(jnp.int32))


def draw_slot_owner(key, part):
    return slot_tables(key)[0]


def draw_slot_task(key, part):
    return slot_tables(key)[1]


def draw_lengths(key, part):
    key = jax.random.fold_in(key, 5)
    key_a, random_seed_later_sample, key_c = jax.random.split(key, 3)
    values = jax.random.randint(key_a, (SESSIONS,), BLOCK // 8, BLOCK + BLOCK // 2 + 1)
    top_index = jax.random.randint(random_seed_later_sample, (), 0, SESSIONS)
    low_index = (top_index + 1 + jax.random.randint(key_c, (), 0, SESSIONS - 1)) % SESSIONS
    values = values.at[top_index].set(BLOCK + BLOCK // 2).at[low_index].set(BLOCK // 8)
    return values.astype(jnp.int32)


def draw_dt_raw(key, part):
    key = jax.random.fold_in(key, 11)
    key_a, random_seed_later_sample = jax.random.split(key)
    tensor_dimensions = (SLOTS, HEADS, BLOCK)
    starting_level = jax.random.normal(key_a, tensor_dimensions, jnp.float32)
    spike_magnitude = jax.random.uniform(random_seed_later_sample, tensor_dimensions, jnp.float32) < 0.02
    return jnp.where(spike_magnitude, starting_level + 5.0, starting_level).astype(jnp.float32)


def level_of(key, dims, cuts, least, largest):
    def one(position, shards_of):
        steps = jax.random.uniform(jax.random.fold_in(jax.random.fold_in(key, 6), position), (shards_of,), jnp.float32, least / len(cuts), largest / len(cuts))
        return jnp.repeat(jnp.exp(steps), dims[position] // shards_of).reshape((-1,) + (1,) * (len(dims) - position - 1))

    loudness = one(*cuts[0])
    for cut in cuts[1:]:
        loudness = loudness * one(*cut)
    return loudness


def noise(stream_key, shape, width, reach, cuts=(), kind=jnp.bfloat16):
    values = width * jax.random.normal(stream_key, shape, jnp.float32)
    if cuts:
        values = values * level_of(stream_key, shape, cuts, -0.22, 0.18)
    return jnp.clip(values, -reach, reach).astype(kind)


def setup_inputs(seed: int = 0, part: int = 0) -> dict:
    key_of = jax.random.split(jax.random.key(seed), 14)
    part_splits = jax.random.split(jax.random.fold_in(key_of[13], part), 14)
    return {
        "x_rows": noise(part_splits[0], (SLOTS, BLOCK, HEADS * HEAD_SIZE), 1.0, 6.0, ((0, 8), (2, 2))),
        "z_rows": noise(part_splits[1], (SLOTS, BLOCK, HEADS * HEAD_SIZE), 1.0, 6.0, ((0, 8), (2, 2))),
        "input_projection_matrix": noise(part_splits[2], (SLOTS, BLOCK, GROUPS * STATE), 1.0, 6.0, ((0, 8),)),
        "c_rows": noise(part_splits[3], (SLOTS, BLOCK, GROUPS * STATE), STATE ** -0.5, 0.375, ((0, 8),)),
        "dt_raw": draw_dt_raw(jax.random.fold_in(jax.random.fold_in(key_of[13], part), 71), part),
        "a_log": jnp.clip(-5.8 + 3.5000002 * jax.random.uniform(key_of[5], (HEADS,), jnp.float32) ** level_of(key_of[5], (HEADS,), ((0, 2),), -0.2, 0.2), -5.8, -2.3),
        "dt_bias": jnp.clip(jax.random.uniform(key_of[6], (HEADS,), jnp.float32, -1.0, 1.0) * level_of(key_of[6], (HEADS,), ((0, 2),), -0.4, 0.0), -1.0, 1.0),
        "d_skip": jnp.clip(0.5 + 1.5 * jax.random.uniform(key_of[7], (HEADS,), jnp.float32) ** level_of(key_of[7], (HEADS,), ((0, 2),), -0.2, 0.2), 0.5, 2.0),
        "norm_gain": jnp.clip(1.0 + 0.15 * jax.random.normal(key_of[8], (HEADS * HEAD_SIZE,), jnp.float32), 0.25, 1.75).astype(jnp.bfloat16),
        "cache_state": noise(part_splits[9], (SESSIONS, HEADS, HEAD_SIZE, STATE), 2.0, 12.0, ((0, 8), (1, 2))),
        "lengths": draw_lengths(jax.random.fold_in(jax.random.fold_in(key_of[13], part), 71), part),
        "slot_owner": draw_slot_owner(jax.random.fold_in(jax.random.fold_in(key_of[13], part), 71), part),
        "slot_task": draw_slot_task(jax.random.fold_in(jax.random.fold_in(key_of[13], part), 71), part),
    }


def block_work(x_slot, b_slot, c_slot, unscaled_steps, valid, a_log, dt_bias):
    row_index = jnp.arange(BLOCK)
    live_rows = row_index < valid
    step_lengths = jnp.where(live_rows[None, :], jax.nn.softplus(unscaled_steps + dt_bias[:, None]), 0.0)
    log_decay = jnp.cumsum(-jnp.exp(a_log)[:, None] * step_lengths, axis=1)
    group_of = jnp.arange(HEADS) // GROUP_HEADS
    b_group = b_slot.reshape(BLOCK, GROUPS, STATE).astype(jnp.float32)
    c_group = c_slot.reshape(BLOCK, GROUPS, STATE).astype(jnp.float32)
    scores = jnp.einsum('rgn,ugn->gru', c_group, b_group)[group_of]
    lower = row_index[:, None] >= row_index[None, :]
    gap_log = jnp.where(lower[None], log_decay[:, :, None] - log_decay[:, None, :], -jnp.inf)
    weights = (jnp.exp(gap_log) * step_lengths[:, None, :] * scores).astype(jnp.bfloat16)
    x_heads = x_slot.reshape(BLOCK, HEADS, HEAD_SIZE).astype(jnp.float32)
    in_block = jnp.einsum('hru,uhp->rhp', weights.astype(jnp.float32), x_heads)
    trailing_share = jnp.exp(log_decay[:, -1:] - log_decay) * step_lengths
    scaled = (x_heads * trailing_share.T[:, :, None]).astype(jnp.bfloat16)
    b_heads = b_group[:, group_of, :]
    local_state = jnp.einsum('uhp,uhn->hpn', scaled.astype(jnp.float32), b_heads).astype(jnp.bfloat16)
    block_decay = jnp.exp(log_decay[:, -1]).astype(jnp.bfloat16)
    return (in_block, log_decay, local_state, block_decay, live_rows)

def finish_rows(in_block, log_decay, start, x_slot, z_slot, c_slot, live_rows, d_skip, norm_gain):
    group_of = jnp.arange(HEADS) // GROUP_HEADS
    c_heads = c_slot.reshape(BLOCK, GROUPS, STATE).astype(jnp.float32)[:, group_of, :]
    carried = jnp.einsum('rhn,hpn->rhp', c_heads, start.astype(jnp.float32)) * jnp.exp(log_decay).T[:, :, None]
    x_heads = x_slot.reshape(BLOCK, HEADS, HEAD_SIZE).astype(jnp.float32)
    y_total = in_block + carried + d_skip[None, :, None] * x_heads
    gate_rows = jax.nn.silu(z_slot.astype(jnp.float32)).reshape(BLOCK, GROUPS, -1)
    gated_rows = y_total.reshape(BLOCK, GROUPS, -1) * gate_rows
    inv_rms = lax.rsqrt(lax.optimization_barrier(jnp.mean(gated_rows * gated_rows, axis=2, keepdims=True)) + 1e-05)
    normed = (gated_rows * inv_rms).reshape(BLOCK, -1) * norm_gain.astype(jnp.float32)
    return jnp.where(live_rows[:, None], normed, 0.0).astype(jnp.bfloat16)

def reference(x_rows, z_rows, input_projection_matrix, c_rows, dt_raw, a_log, dt_bias, d_skip, norm_gain, cache_state, lengths, slot_owner, slot_task):
    owner_ids = slot_owner.reshape(N_DP, N_SESS, SLOTS_DEV).transpose(1, 0, 2).reshape(-1)
    job_identifiers = slot_task.reshape(N_DP, N_SESS, SLOTS_DEV).transpose(1, 0, 2).reshape(-1)
    dp_index = jnp.arange(SLOTS, dtype=jnp.int32) // SLOTS_DEV % N_DP
    session = ((owner_ids * N_DP + dp_index) * SESSIONS_PER_UNIT + job_identifiers // 2).astype(jnp.int32)
    block_part = (job_identifiers % 2).astype(jnp.int32)
    valid = jnp.clip(lengths[session] - block_part * BLOCK, 0, BLOCK)

    def first_pass(item_args):
        x_slot, b_slot, c_slot, unscaled_steps, valid_one = item_args
        result = block_work(x_slot, b_slot, c_slot, unscaled_steps, valid_one, a_log, dt_bias)
        return (result[2], result[3])
    local_state, block_decay = lax.map(first_pass, (x_rows, input_projection_matrix, c_rows, dt_raw, valid))
    slot_of = jnp.zeros((SESSIONS, 2), jnp.int32).at[session, block_part].set(jnp.arange(SLOTS, dtype=jnp.int32))
    slot_first = slot_of[:, 0]
    slot_second = slot_of[:, 1]
    start_late = (block_decay[slot_first].astype(jnp.float32)[:, :, None, None] * cache_state.astype(jnp.float32) + local_state[slot_first].astype(jnp.float32)).astype(jnp.bfloat16)
    final_state = (block_decay[slot_second].astype(jnp.float32)[:, :, None, None] * start_late.astype(jnp.float32) + local_state[slot_second].astype(jnp.float32)).astype(jnp.bfloat16)
    starts = jnp.where((block_part == 0)[:, None, None, None], cache_state[session], start_late[session])

    def second_pass(item_args):
        x_slot, z_slot, b_slot, c_slot, unscaled_steps, valid_one, start = item_args
        in_block, log_decay, unused_state, unused_decay, live_rows = block_work(x_slot, b_slot, c_slot, unscaled_steps, valid_one, a_log, dt_bias)
        return finish_rows(in_block, log_decay, start, x_slot, z_slot, c_slot, live_rows, d_skip, norm_gain)
    mixed_rows = lax.map(second_pass, (x_rows, z_rows, input_projection_matrix, c_rows, dt_raw, valid, starts))
    return (mixed_rows, final_state)
```

```python
import functools

import jax
import jax.numpy as jnp
from jax import lax
from jax.experimental import pallas as pl
from jax.experimental.pallas import tpu as pltpu
from jax.sharding import PartitionSpec as P

F32 = jnp.float32
BF16 = jnp.bfloat16
HALF = 64
VMEM = pl.BlockSpec(memory_space=pltpu.VMEM)
SMEM = pl.BlockSpec(memory_space=pltpu.SMEM)
ANY = pl.BlockSpec(memory_space=pl.ANY)
PARAMS = pltpu.CompilerParams(vmem_limit_bytes=24 * 1024 * 1024)


def dot(a, b, dims, precision=None):
    return lax.dot_general(
        a, b, ((dims[:1], dims[1:]), ((), ())), precision=precision, preferred_element_type=F32
    )


def iota(shape, dim):
    return lax.broadcasted_iota(jnp.int32, shape, dim)


def softplus(v):
    return jnp.maximum(v, 0.0) + jnp.log1p(jnp.exp(-jnp.abs(v)))


def running(v):
    rows = v.shape[1]
    upto = jnp.where(iota((rows, rows), 0) <= iota((rows, rows), 1), 1.0, 0.0).astype(F32)
    return dot(v, upto, (1, 0), lax.Precision.HIGHEST)


def silu(v):
    return v * (1.0 / (1.0 + jnp.exp(-v)))


def choose(index, values):
    out = values[0]
    for k in range(1, len(values)):
        out = jnp.where(index == k, values[k], out)
    return out


def slot_for(ids, owner, k, slots):
    me, dp = ids[0], ids[1]
    pick = jnp.int32(0)
    for j in range(1, slots):
        pick = jnp.where(owner[dp, me * slots + j] == me ^ k, j, pick)
    return pick


def sources(ids, owner, task, slots):
    me, dp = ids[0], ids[1]
    first = jnp.int32(0)
    second = jnp.int32(0)
    for i in range(owner.shape[1]):
        mine = owner[dp, i] == me
        late = task[dp, i] % 2 == 1
        first = jnp.where(mine & ~late, me ^ (i // slots), first)
        second = jnp.where(mine & late, me ^ (i // slots), second)
    return first, second


def small_send(peers, ids, owner, lens, dt, b, c, *outs):
    slots, heads = dt.shape[:2]
    dtls, bcs = outs[:peers], outs[peers:]
    own_len = lens[0].astype(F32)
    for k in range(peers):
        j = slot_for(ids, owner, k, slots)
        dtls[k][:heads] = dt[j]
        dtls[k][heads:] = jnp.full((8, dt.shape[2]), own_len, F32)

        @pl.when(ids[2] == 0)
        def _():
            bcs[k][...] = b[j]

        @pl.when(ids[2] != 0)
        def _():
            bcs[k][...] = c[j]


def x_send(peers, ids, owner, x, *rest):
    outs, sem = rest[:peers], rest[peers]
    slots = x.shape[0]
    copies = []
    for k in range(peers):
        j = slot_for(ids, owner, k, slots)
        copies.append(pltpu.make_async_copy(x.at[j], outs[k], sem.at[k]))
        copies[-1].start()
    for copy in copies:
        copy.wait()


def bc_pick(peers, slots, ids, owner, task, *rest):
    bcs, out = rest[:peers], rest[peers]
    k0, k1 = sources(ids, owner, task, slots)
    rows = bcs[0].shape[0]
    for k in range(peers):

        @pl.when(k0 == k)
        def _():
            out[:rows] = bcs[k][...]

        @pl.when(k1 == k)
        def _():
            out[rows:] = bcs[k][:HALF]


def block_part(ids, x, z, b, c, dt, alog, bias, skip, yz, ez):
    slots, rows, width = x.shape
    heads = dt.shape[1]
    size = width // heads
    per = 128 // size
    causal = iota((rows, rows), 0) >= iota((rows, rows), 1)
    lane = iota((rows, 128), 1) // size
    rate = -jnp.exp(alog[...])
    for s in range(slots):
        step = softplus(dt[s] + bias[...])
        log_decay = running(rate * step)
        log_col = jnp.transpose(log_decay)
        decay_col = jnp.exp(log_col)
        scores = jnp.where(causal, dot(c[s], b[s], (1, 1)), 0.0)
        for p in range(width // 128):
            lanes = slice(p * 128, (p + 1) * 128)
            xp = x[s, :, lanes]
            weights = []
            blocks = []
            decay = decay_col[:, p * per : p * per + 1]
            own_skip = skip[p * per : p * per + 1]
            for q in range(per):
                h = p * per + q
                gap = jnp.minimum(log_col[:, h : h + 1] - log_decay[h : h + 1], 0.0)
                weights.append((jnp.exp(gap) * step[h : h + 1] * scores).astype(BF16))
                blocks.append(jnp.where(lane == q, xp, jnp.zeros_like(xp)))
                if q:
                    decay = jnp.where(lane == q, decay_col[:, h : h + 1], decay)
                    own_skip = jnp.where(lane[:1] == q, skip[h : h + 1], own_skip)
            inner = dot(
                jnp.concatenate(weights, axis=1), jnp.concatenate(blocks, axis=0), (1, 0)
            )
            gate = silu(z[s, :, lanes].astype(F32))
            yz[s, :, lanes] = (inner + own_skip * xp.astype(F32)) * gate
            ez[s, :, lanes] = decay * gate


def owner_part(peers, slots, ids, owner, task, lens, cache, alog, bias, mine, other, *rest):
    dtls, xs = rest[:peers], rest[peers : 2 * peers]
    final = rest[2 * peers]
    cars = rest[2 * peers + 1 : 3 * peers + 1]
    x0, x1, car0, car1, bs, cs, sem = rest[3 * peers + 1 :]
    rows, width = x0.shape
    heads = alog.shape[0]
    size = width // heads
    k0, k1 = sources(ids, owner, task, slots)

    def load(k):
        return (
            (k0 == k, pltpu.make_async_copy(xs[k], x0, sem.at[0])),
            (k1 == k, pltpu.make_async_copy(xs[k].at[:HALF], x1, sem.at[1])),
        )

    for k in range(peers):
        for pred, copy in load(k):
            pl.when(pred)(copy.start)

    @pl.when(ids[2] == 0)
    def _():
        bs[...] = mine[...]
        cs[...] = other[...]

    @pl.when(ids[2] != 0)
    def _():
        bs[...] = other[...]
        cs[...] = mine[...]

    length = lens[0]
    rate = -jnp.exp(alog[...])
    col = iota((heads, rows), 1)

    def shares(dt, valid):
        step = jnp.where(col < valid, softplus(dt + bias[...]), 0.0)
        log_decay = running(rate * step)
        total = log_decay[:, rows - 1 :]
        share = jnp.exp(total - log_decay) * step
        return jnp.transpose(share), jnp.exp(total).astype(BF16).astype(F32)

    share0, decay0 = shares(choose(k0, [d[:heads] for d in dtls]), length)
    share1, decay1 = shares(choose(k1, [d[:heads] for d in dtls]), length - rows)
    per = 128 // size
    lane = iota((rows, 128), 1) // size

    def scaled(xv, share, p):
        factor = share[:, p * per : p * per + 1]
        for q in range(1, per):
            factor = jnp.where(lane[: xv.shape[0]] == q, share[:, p * per + q : p * per + q + 1], factor)
        return (xv.astype(F32) * factor).astype(BF16)

    for k in range(peers):
        for pred, copy in load(k):
            pl.when(pred)(copy.wait)

    for g in range(width // 256):
        lanes = slice(g * 256, (g + 1) * 256)
        old = cache[lanes]
        car0[:, lanes] = dot(cs[:rows], old, (1, 1)).astype(BF16)
        s0 = jnp.concatenate(
            [scaled(x0[:, p * 128 : (p + 1) * 128], share0, p) for p in (2 * g, 2 * g + 1)], axis=1
        )
        s1 = jnp.concatenate(
            [scaled(x1[:, p * 128 : (p + 1) * 128], share1[:HALF], p) for p in (2 * g, 2 * g + 1)],
            axis=1,
        )
        local0 = dot(s0, bs[:rows], (0, 0)).astype(BF16).astype(F32)
        local1 = dot(s1, bs[rows:], (0, 0)).astype(BF16).astype(F32)
        late = []
        for q in range(256 // size):
            h = g * (256 // size) + q
            part = slice(q * size, (q + 1) * size)
            start = decay0[h : h + 1] * old[part].astype(F32) + local0[part]
            late.append(start.astype(BF16))
            final[h * size : (h + 1) * size] = (
                decay1[h : h + 1] * late[-1].astype(F32) + local1[part]
            ).astype(BF16)
        late = jnp.concatenate(late, axis=0)
        car1[:, lanes] = dot(cs[rows:], late, (1, 1)).astype(BF16)

    def store(k):
        return (
            (k0 == k, pltpu.make_async_copy(car0, cars[k], sem.at[0])),
            (k1 == k, pltpu.make_async_copy(car1, cars[k].at[:HALF], sem.at[1])),
        )

    for k in range(peers):
        for pred, copy in store(k):
            pl.when(pred)(copy.start)
    for k in range(peers):
        for pred, copy in store(k):
            pl.when(pred)(copy.wait)


def gate_part(peers, ids, owner, yz, ez, *rest):
    cars = rest[:peers]
    gated, squares, got, sem = rest[peers:]
    slots, rows, width = yz.shape
    me, dp = ids[0], ids[1]

    def load(j, k):
        far = me ^ owner[dp, me * slots + j]
        return far == k, pltpu.make_async_copy(cars[k], got.at[j], sem.at[j])

    for j in range(slots):
        for k in range(peers):
            pred, copy = load(j, k)
            pl.when(pred)(copy.start)
    for j in range(slots):
        for k in range(peers):
            pred, copy = load(j, k)
            pl.when(pred)(copy.wait)
        total = jnp.zeros((rows, 128), F32)
        for p in range(width // 128):
            lanes = slice(p * 128, (p + 1) * 128)
            value = yz[j, :, lanes] + ez[j, :, lanes] * got[j, :, lanes].astype(F32)
            gated[j, :, lanes] = value
            total = total + value * value
        squares[j : j + 1] = jnp.sum(jnp.transpose(total), axis=0, keepdims=True)


def norm_part(peers, ids, owner, task, gated, own, other, gain, *rest):
    dtls, mixed = rest[:peers], rest[peers]
    slots, rows, width = gated.shape
    heads = dtls[0].shape[0] - 8
    me, dp = ids[0], ids[1]
    row = iota((rows, 128), 0).astype(F32)
    for j in range(slots):
        far = me ^ owner[dp, me * slots + j]
        late = task[dp, me * slots + j] % 2
        length = choose(far, [d[heads : heads + 1] for d in dtls])
        live = row + (late * rows).astype(F32) < length
        mean = (own[j : j + 1] + other[j : j + 1]) / (2.0 * width)
        inverse = jnp.transpose(jnp.broadcast_to(lax.rsqrt(mean + 1e-05), (rows, rows)))
        for p in range(width // 128):
            lanes = slice(p * 128, (p + 1) * 128)
            value = gated[j, :, lanes] * inverse * gain[:, lanes].astype(F32)
            mixed[j, :, lanes] = jnp.where(live, value, 0.0).astype(BF16)


def call(kernel, outs, in_specs, out_specs=None, scratch=(), flops=0, moved=0):
    return pl.pallas_call(
        kernel,
        out_shape=outs,
        in_specs=in_specs,
        out_specs=out_specs if out_specs is not None else jax.tree.map(lambda _: VMEM, outs),
        scratch_shapes=scratch,
        compiler_params=PARAMS,
        cost_estimate=pl.CostEstimate(flops=flops, bytes_accessed=moved, transcendentals=0),
    )


def per_device(
    x_rows,
    z_rows,
    input_projection_matrix,
    c_rows,
    dt_raw,
    a_log,
    dt_bias,
    d_skip,
    norm_gain,
    cache_state,
    lengths,
    slot_owner,
    slot_task,
):
    slots, rows, width = x_rows.shape
    heads = dt_raw.shape[1]
    state = cache_state.shape[3]
    peers = lax.axis_size("sess")
    head = lax.axis_index("head")
    groups = input_projection_matrix.shape[2] // state
    if groups > 1:
        at = head // 2 * state
        b = lax.dynamic_slice_in_dim(input_projection_matrix, at, state, 2)
        c = lax.dynamic_slice_in_dim(c_rows, at, state, 2)
    else:
        b, c = input_projection_matrix, c_rows
    ids = jnp.stack([lax.axis_index("sess"), lax.axis_index("dp"), head % 2]).astype(jnp.int32)
    alog = a_log[:, None]
    bias = dt_bias[:, None]
    skip = d_skip[:, None]
    gain = norm_gain[None]
    cache = cache_state.reshape(width, state)

    def exchange(values):
        return [values[0]] + [
            lax.ppermute(values[k], "sess", [(i, i ^ k) for i in range(peers)])
            for k in range(1, peers)
        ]

    def swapped(value):
        count = lax.axis_size("head")
        return lax.ppermute(value, "head", [(i, i ^ 1) for i in range(count)])

    shape = jax.ShapeDtypeStruct
    small = call(
        functools.partial(small_send, peers),
        [shape((heads + 8, rows), F32)] * peers + [shape((rows, state), BF16)] * peers,
        [SMEM, SMEM, SMEM, VMEM, VMEM, VMEM],
    )(ids, slot_owner, lengths, dt_raw, b, c)
    dtls = exchange(small[:peers])
    bcs = exchange(small[peers:])
    xs = exchange(
        call(
            functools.partial(x_send, peers),
            [shape((rows, width), BF16)] * peers,
            [SMEM, SMEM, ANY],
            [ANY] * peers,
            [pltpu.SemaphoreType.DMA((peers,))],
        )(ids, slot_owner, x_rows)
    )
    mine = call(
        functools.partial(bc_pick, peers, slots),
        shape((rows + HALF, state), BF16),
        [SMEM, SMEM, SMEM] + [VMEM] * peers,
    )(ids, slot_owner, slot_task, *bcs)
    other = swapped(mine)
    yz, ez = call(
        block_part,
        [shape(x_rows.shape, F32)] * 2,
        [SMEM] + [VMEM] * 8,
        flops=2 * slots * rows * rows * width * 2,
        moved=16 * 1024 * 1024,
    )(ids, x_rows, z_rows, b, c, dt_raw, alog, bias, skip)
    out = call(
        functools.partial(owner_part, peers, slots),
        [shape((width, state), BF16)] + [shape((rows, width), BF16)] * peers,
        [SMEM] * 4 + [VMEM] * 5 + [VMEM] * peers + [ANY] * peers,
        [VMEM] + [ANY] * peers,
        [
            pltpu.VMEM((rows, width), BF16),
            pltpu.VMEM((HALF, width), BF16),
            pltpu.VMEM((rows, width), BF16),
            pltpu.VMEM((HALF, width), BF16),
            pltpu.VMEM((rows + HALF, state), BF16),
            pltpu.VMEM((rows + HALF, state), BF16),
            pltpu.SemaphoreType.DMA((2,)),
        ],
    )(ids, slot_owner, slot_task, lengths, cache, alog, bias, mine, other, *dtls, *xs)
    final_state = out[0].reshape(cache_state.shape)
    cars = exchange(out[1:])
    gated, own = call(
        functools.partial(gate_part, peers),
        [shape(x_rows.shape, F32), shape((slots, rows), F32)],
        [SMEM, SMEM, VMEM, VMEM] + [ANY] * peers,
        scratch=[pltpu.VMEM((slots, rows, width), BF16), pltpu.SemaphoreType.DMA((slots,))],
    )(ids, slot_owner, yz, ez, *cars)
    mixed_rows = call(
        functools.partial(norm_part, peers),
        shape(x_rows.shape, BF16),
        [SMEM] * 3 + [VMEM] * 4 + [VMEM] * peers,
    )(ids, slot_owner, slot_task, gated, own, swapped(own), gain, *dtls)
    return (mixed_rows, final_state)


def solution(mesh):
    in_specs = (
        P(("group", "sess", "dp"), None, "head"),
        P(("group", "sess", "dp"), None, "head"),
        P(("group", "sess", "dp"), None, None),
        P(("group", "sess", "dp"), None, None),
        P(("group", "sess", "dp"), "head", None),
        P("head"),
        P("head"),
        P("head"),
        P("head"),
        P(("group", "sess", "dp"), "head", None, None),
        P(("group", "sess", "dp")),
        P("group", None),
        P("group", None),
    )
    out_specs = (
        P(("group", "sess", "dp"), None, "head"),
        P(("group", "sess", "dp"), "head", None, None),
    )
    return jax.shard_map(
        per_device, mesh=mesh, in_specs=in_specs, out_specs=out_specs, check_vma=False
    )
```

```python
import functools

import jax
import jax.numpy as jnp
from jax import lax
from jax.experimental import pallas as pl
from jax.experimental.pallas import tpu as pltpu
from jax.sharding import PartitionSpec as P

F32 = jnp.float32
BF16 = jnp.bfloat16
HALF = 64
VMEM = pl.BlockSpec(memory_space=pltpu.VMEM)
SMEM = pl.BlockSpec(memory_space=pltpu.SMEM)
ANY = pl.BlockSpec(memory_space=pl.ANY)
PARAMS = pltpu.CompilerParams(vmem_limit_bytes=24 * 1024 * 1024)


def dot(a, b, dims, precision=None):
    return lax.dot_general(
        a, b, ((dims[:1], dims[1:]), ((), ())), precision=precision, preferred_element_type=F32
    )


def iota(shape, dim):
    return lax.broadcasted_iota(jnp.int32, shape, dim)


def softplus(v):
    return jnp.maximum(v, 0.0) + jnp.log1p(jnp.exp(-jnp.abs(v)))


def running(v):
    rows = v.shape[1]
    upto = jnp.where(iota((rows, rows), 0) <= iota((rows, rows), 1), 1.0, 0.0).astype(F32)
    return dot(v, upto, (1, 0), lax.Precision.HIGHEST)


def silu(v):
    return v * (1.0 / (1.0 + jnp.exp(-v)))


def choose(index, values):
    out = values[0]
    for k in range(1, len(values)):
        out = jnp.where(index == k, values[k], out)
    return out


def slot_for(ids, owner, k, slots):
    me, dp = ids[0], ids[1]
    pick = jnp.int32(0)
    for j in range(1, slots):
        pick = jnp.where(owner[dp, me * slots + j] == me ^ k, j, pick)
    return pick


def holder(ids, owner, task, slots, k, part):
    me, dp = ids[0], ids[1]
    found = jnp.int32(0)
    for i in range(owner.shape[1]):
        hit = (owner[dp, i] == me ^ k) & (task[dp, i] % 2 == part)
        found = jnp.where(hit, me ^ (i // slots), found)
    return found


def run(choices):
    for pred, copy in choices:
        pl.when(pred)(copy.start)

    def finish():
        for pred, copy in choices:
            pl.when(pred)(copy.wait)

    return finish


def small_send(peers, ids, owner, lens, dt, b, c, *outs):
    slots, heads, rows = dt.shape
    size = jnp.full((heads, rows), lens[0].astype(F32)).astype(BF16)
    for k in range(peers):
        j = slot_for(ids, owner, k, slots)
        out = outs[k]

        @pl.when(ids[2] == 0)
        def _():
            out[:rows] = b[j]

        @pl.when(ids[2] != 0)
        def _():
            out[:rows] = c[j]

        rest = dt[j]
        high = rest.astype(BF16)
        rest = rest - high.astype(F32)
        middle = rest.astype(BF16)
        low = (rest - middle.astype(F32)).astype(BF16)
        out[rows : rows + heads, :rows] = high
        out[rows : rows + heads, rows:] = middle
        out[rows + heads :, :rows] = low
        out[rows + heads :, rows:] = size


def x_send(peers, ids, owner, x, near, *rest):
    far, sem = rest[:-1], rest[-1]
    slots = x.shape[0]
    copies = []

    def move(k, start, out):
        j = slot_for(ids, owner, k, slots)
        copy = pltpu.make_async_copy(x.at[j, pl.ds(start, HALF)], out, sem.at[len(copies)])
        copy.start()
        copies.append(copy)

    for m in range(peers // 2):
        move(1 ^ 2 * m, HALF, near.at[pl.ds((m + 1) * HALF, HALF)])
    for k in range(2, peers):
        move(k, 0, far[k - 2])
    move(1, 0, near.at[pl.ds(0, HALF)])
    for copy in copies:
        copy.wait()


def x_forward(peers, ids, owner, task, x, near, *rest):
    outs, sem = rest[:-1], rest[-1]
    slots = x.shape[0]
    choices = []
    for m in range(1, peers // 2):
        at = holder(ids, owner, task, slots, 2 * m, 0)
        j = slot_for(ids, owner, 2 * m, slots)
        upper = x.at[j, pl.ds(HALF, HALF)]
        passing = near.at[pl.ds((m + 1) * HALF, HALF)]
        for pred, src in ((at == 0, upper), (at == 1, passing)):
            choices.append((pred, pltpu.make_async_copy(src, outs[m - 1], sem.at[m - 1])))
    run(choices)()


def small_pick(peers, slots, heads, ids, owner, task, *rest):
    got = rest[:peers]
    mine, dts, lens = rest[peers:]
    rows = got[0].shape[0] - 2 * heads
    me, dp = ids[0], ids[1]
    for part, count in ((0, rows), (1, HALF)):
        at = holder(ids, owner, task, slots, 0, part)
        for k in range(peers):

            @pl.when(at == k)
            def _():
                mine[part * rows : part * rows + count] = got[k][:count]
                high = got[k][rows : rows + heads, :rows].astype(F32)
                middle = got[k][rows : rows + heads, rows:].astype(F32)
                low = got[k][rows + heads :, :rows].astype(F32)
                dts[part] = high + (middle + low)

    for j in range(slots):
        far = me ^ owner[dp, me * slots + j]
        for k in range(peers):

            @pl.when(far == k)
            def _():
                lens[j] = got[k][rows + heads :, rows:].astype(F32)


def block_part(ids, x, z, b, c, dt, alog, bias, skip, yz, ez):
    slots, rows, width = x.shape
    heads = dt.shape[1]
    size = width // heads
    per = 128 // size
    causal = iota((rows, rows), 0) >= iota((rows, rows), 1)
    lane = iota((rows, 128), 1) // size
    rate = -jnp.exp(alog[...])
    for s in range(slots):
        step = softplus(dt[s] + bias[...])
        log_decay = running(rate * step)
        log_col = jnp.transpose(log_decay)
        decay_col = jnp.exp(log_col)
        scores = jnp.where(causal, dot(c[s], b[s], (1, 1)), 0.0)
        for p in range(width // 128):
            lanes = slice(p * 128, (p + 1) * 128)
            xp = x[s, :, lanes]
            weights = []
            blocks = []
            decay = decay_col[:, p * per : p * per + 1]
            own_skip = skip[p * per : p * per + 1]
            for q in range(per):
                h = p * per + q
                gap = jnp.minimum(log_col[:, h : h + 1] - log_decay[h : h + 1], 0.0)
                weights.append((jnp.exp(gap) * step[h : h + 1] * scores).astype(BF16))
                blocks.append(jnp.where(lane == q, xp, jnp.zeros_like(xp)))
                if q:
                    decay = jnp.where(lane == q, decay_col[:, h : h + 1], decay)
                    own_skip = jnp.where(lane[:1] == q, skip[h : h + 1], own_skip)
            inner = dot(
                jnp.concatenate(weights, axis=1), jnp.concatenate(blocks, axis=0), (1, 0)
            )
            gate = silu(z[s, :, lanes].astype(F32))
            yz[s, :, lanes] = (inner + own_skip * xp.astype(F32)) * gate
            ez[s, :, lanes] = decay * gate


def early_part(ids, cache, mine, other, lower, upper):
    rows = lower.shape[0] + upper.shape[0]

    def work(cs):
        for g in range(cache.shape[0] // 256):
            lanes = slice(g * 256, (g + 1) * 256)
            value = dot(cs[:rows], cache[lanes], (1, 1)).astype(BF16)
            lower[:, lanes] = value[:HALF]
            upper[:, lanes] = value[HALF:]

    @pl.when(ids[2] == 0)
    def _():
        work(other)

    @pl.when(ids[2] != 0)
    def _():
        work(mine)


def owner_part(
    peers, slots, ids, owner, task, lens, cache, alog, bias, mine, other, dts, lower, x, near, *rest
):
    half = peers // 2
    far, onward = rest[: peers - 2], rest[peers - 2 : peers - 3 + half]
    rest = rest[peers - 3 + half :]
    final, cars = rest[0], rest[1 : peers + 1]
    x0, x1, car1, bs, cs, sem = rest[peers + 1 :]
    rows, width = x0.shape
    heads = alog.shape[0]
    size = width // heads
    k0 = holder(ids, owner, task, slots, 0, 0)
    k1 = holder(ids, owner, task, slots, 0, 1)
    j = slot_for(ids, owner, 0, slots)
    loads = []
    for at, out, flag in ((k0, x0.at[pl.ds(0, HALF)], 0), (k1, x1, 1)):
        for k in range(peers):
            src = far[k - 2] if k > 1 else near.at[pl.ds(0, HALF)] if k else x.at[j, pl.ds(0, HALF)]
            loads.append((at == k, pltpu.make_async_copy(src, out, sem.at[flag])))
    out = x0.at[pl.ds(HALF, HALF)]
    for pred, src in [
        (k0 == 0, x.at[j, pl.ds(HALF, HALF)]),
        (k0 == 1, near.at[pl.ds(HALF, HALF)]),
    ] + [(k0 // 2 == m, onward[m - 1]) for m in range(1, half)]:
        loads.append((pred, pltpu.make_async_copy(src, out, sem.at[2])))
    loaded = run(loads)

    @pl.when(ids[2] == 0)
    def _():
        bs[...] = mine[...]
        cs[...] = other[rows:]

    @pl.when(ids[2] != 0)
    def _():
        bs[...] = other[...]
        cs[...] = mine[rows:]

    length = lens[0]
    rate = -jnp.exp(alog[...])
    col = iota((heads, rows), 1)

    def shares(dt, valid):
        step = jnp.where(col < valid, softplus(dt + bias[...]), 0.0)
        log_decay = running(rate * step)
        total = log_decay[:, rows - 1 :]
        share = jnp.exp(total - log_decay) * step
        return jnp.transpose(share), jnp.exp(total).astype(BF16).astype(F32)

    share0, decay0 = shares(dts[0], length)
    share1, decay1 = shares(dts[1], length - rows)
    per = 128 // size
    lane = iota((rows, 128), 1) // size

    def scaled(xv, share, p):
        factor = share[:, p * per : p * per + 1]
        for q in range(1, per):
            factor = jnp.where(
                lane[: xv.shape[0]] == q, share[:, p * per + q : p * per + q + 1], factor
            )
        return (xv.astype(F32) * factor).astype(BF16)

    loaded()
    for g in range(width // 256):
        lanes = slice(g * 256, (g + 1) * 256)
        old = cache[lanes]
        pairs = [(p, slice(p * 128, (p + 1) * 128)) for p in (2 * g, 2 * g + 1)]
        s0 = jnp.concatenate([scaled(x0[:, at], share0, p) for p, at in pairs], axis=1)
        s1 = jnp.concatenate([scaled(x1[:, at], share1[:HALF], p) for p, at in pairs], axis=1)
        local0 = dot(s0, bs[:rows], (0, 0)).astype(BF16).astype(F32)
        local1 = dot(s1, bs[rows:], (0, 0)).astype(BF16).astype(F32)
        late = []
        for q in range(256 // size):
            h = g * (256 // size) + q
            part = slice(q * size, (q + 1) * size)
            start = decay0[h : h + 1] * old[part].astype(F32) + local0[part]
            late.append(start.astype(BF16))
            final[h * size : (h + 1) * size] = (
                decay1[h : h + 1] * late[-1].astype(F32) + local1[part]
            ).astype(BF16)
        late = jnp.concatenate(late, axis=0)
        car1[:, lanes] = dot(cs[...], late, (1, 1)).astype(BF16)

    stores = []
    for k in range(peers):
        stores.append((k0 == k, pltpu.make_async_copy(lower, cars[k], sem.at[0])))
        stores.append((k1 == k, pltpu.make_async_copy(car1, cars[k], sem.at[1])))
    run(stores)()


def gate_part(peers, ids, owner, task, yz, ez, *rest):
    cars, uppers = rest[:peers], rest[peers : 2 * peers]
    gated, squares, got, sem = rest[2 * peers :]
    slots, rows, width = yz.shape
    me, dp = ids[0], ids[1]
    waits = []
    for j in range(slots):
        far = me ^ owner[dp, me * slots + j]
        early = task[dp, me * slots + j] % 2 == 0
        loads = []
        for k in range(peers):
            low = got.at[j, pl.ds(0, HALF)]
            high = got.at[j, pl.ds(HALF, HALF)]
            loads.append((far == k, pltpu.make_async_copy(cars[k], low, sem.at[j, 0])))
            loads.append(
                ((far == k) & early, pltpu.make_async_copy(uppers[k], high, sem.at[j, 1]))
            )
        waits.append(run(loads))
    for j in range(slots):
        waits[j]()
        total = jnp.zeros((rows, 128), F32)
        for p in range(width // 128):
            lanes = slice(p * 128, (p + 1) * 128)
            value = yz[j, :, lanes] + ez[j, :, lanes] * got[j, :, lanes].astype(F32)
            gated[j, :, lanes] = value
            total = total + value * value
        squares[j : j + 1] = jnp.sum(jnp.transpose(total), axis=0, keepdims=True)


def norm_part(ids, task, gated, own, other, gain, lens, mixed):
    slots, rows, width = gated.shape
    me, dp = ids[0], ids[1]
    row = iota((rows, 128), 0).astype(F32)
    for j in range(slots):
        late = task[dp, me * slots + j] % 2
        live = row + (late * rows).astype(F32) < lens[j][:1]
        mean = (own[j : j + 1] + other[j : j + 1]) / (2.0 * width)
        inverse = jnp.transpose(jnp.broadcast_to(lax.rsqrt(mean + 1e-05), (rows, rows)))
        for p in range(width // 128):
            lanes = slice(p * 128, (p + 1) * 128)
            value = gated[j, :, lanes] * inverse * gain[:, lanes].astype(F32)
            mixed[j, :, lanes] = jnp.where(live, value, 0.0).astype(BF16)


def call(kernel, outs, in_specs, out_specs=None, scratch=(), flops=0, moved=0):
    return pl.pallas_call(
        kernel,
        out_shape=outs,
        in_specs=in_specs,
        out_specs=out_specs if out_specs is not None else jax.tree.map(lambda _: VMEM, outs),
        scratch_shapes=scratch,
        compiler_params=PARAMS,
        cost_estimate=pl.CostEstimate(flops=flops, bytes_accessed=moved, transcendentals=0),
    )


def per_device(
    x_rows,
    z_rows,
    input_projection_matrix,
    c_rows,
    dt_raw,
    a_log,
    dt_bias,
    d_skip,
    norm_gain,
    cache_state,
    lengths,
    slot_owner,
    slot_task,
):
    slots, rows, width = x_rows.shape
    heads = dt_raw.shape[1]
    state = cache_state.shape[3]
    peers = lax.axis_size("sess")
    head = lax.axis_index("head")
    groups = input_projection_matrix.shape[2] // state
    if groups > 1:
        at = head // 2 * state
        b = lax.dynamic_slice_in_dim(input_projection_matrix, at, state, 2)
        c = lax.dynamic_slice_in_dim(c_rows, at, state, 2)
    else:
        b, c = input_projection_matrix, c_rows
    ids = jnp.stack([lax.axis_index("sess"), lax.axis_index("dp"), head % 2]).astype(jnp.int32)
    alog = a_log[:, None]
    bias = dt_bias[:, None]
    skip = d_skip[:, None]
    gain = norm_gain[None]
    cache = cache_state.reshape(width, state)

    half = peers // 2

    def far(value, k):
        return lax.ppermute(value, "sess", [(i, i ^ k) for i in range(peers)])

    def swapped(value):
        count = lax.axis_size("head")
        return lax.ppermute(value, "head", [(i, i ^ 1) for i in range(count)])

    shape = jax.ShapeDtypeStruct
    rows_of = lambda count: shape((count, width), BF16)
    dma = lambda *sizes: pltpu.SemaphoreType.DMA(sizes)
    small = call(
        functools.partial(small_send, peers),
        [shape((rows + 2 * heads, state), BF16)] * peers,
        [SMEM, SMEM, SMEM, VMEM, VMEM, VMEM],
    )(ids, slot_owner, lengths, dt_raw, b, c)
    order = list(range(2, peers)) + [1]
    got = {k: far(small[k], k) for k in order}
    near, *sends = call(
        functools.partial(x_send, peers),
        [rows_of((1 + half) * HALF)] + [rows_of(HALF)] * (peers - 2),
        [SMEM, SMEM, ANY],
        [ANY] * (peers - 1),
        [dma(half + peers - 1)],
    )(ids, slot_owner, x_rows)
    near = far(near, 1)
    sends = [far(value, k + 2) for k, value in enumerate(sends)]
    mine, dts, lens = call(
        functools.partial(small_pick, peers, slots, heads),
        [
            shape((rows + HALF, state), BF16),
            shape((2, heads, rows), F32),
            shape((slots, heads, rows), F32),
        ],
        [SMEM, SMEM, SMEM] + [VMEM] * peers,
    )(ids, slot_owner, slot_task, small[0], *[got[k] for k in range(1, peers)])
    other = swapped(mine)
    onward = call(
        functools.partial(x_forward, peers),
        [rows_of(HALF)] * (half - 1),
        [SMEM, SMEM, SMEM, ANY, ANY],
        [ANY] * (half - 1),
        [dma(half - 1)],
    )(ids, slot_owner, slot_task, x_rows, near)
    onward = [far(value, 2 * (m + 1)) for m, value in enumerate(onward)]
    lower, upper = call(
        early_part,
        [rows_of(HALF)] * 2,
        [SMEM, VMEM, VMEM, VMEM],
        flops=2 * rows * width * state,
        moved=2 * 1024 * 1024,
    )(ids, cache, mine, other)
    uppers = {2 * m: far(upper, 2 * m) if m else upper for m in range(half)}
    yz, ez = call(
        block_part,
        [shape(x_rows.shape, F32)] * 2,
        [SMEM] + [VMEM] * 8,
        flops=2 * slots * rows * rows * width * 2,
        moved=9 * 1024 * 1024,
    )(ids, x_rows, z_rows, b, c, dt_raw, alog, bias, skip)
    final, *cars = call(
        functools.partial(owner_part, peers, slots),
        [shape((width, state), BF16)] + [rows_of(HALF)] * peers,
        [SMEM] * 4 + [VMEM] * 6 + [ANY] * (2 + peers - 2 + half),
        [VMEM] + [ANY] * peers,
        [
            pltpu.VMEM((rows, width), BF16),
            pltpu.VMEM((HALF, width), BF16),
            pltpu.VMEM((HALF, width), BF16),
            pltpu.VMEM((rows + HALF, state), BF16),
            pltpu.VMEM((HALF, state), BF16),
            dma(3),
        ],
        flops=4 * rows * width * state,
        moved=9 * 1024 * 1024,
    )(
        ids,
        slot_owner,
        slot_task,
        lengths,
        cache,
        alog,
        bias,
        mine,
        other,
        dts,
        lower,
        x_rows,
        near,
        *sends,
        *onward,
    )
    cars = {0: cars[0]} | {k: far(cars[k], k) for k in order}
    uppers |= {2 * m + 1: far(uppers[2 * m], 1) for m in range(half)}
    gated, own = call(
        functools.partial(gate_part, peers),
        [shape(x_rows.shape, F32), shape((slots, rows), F32)],
        [SMEM, SMEM, SMEM, VMEM, VMEM] + [ANY] * (2 * peers),
        scratch=[pltpu.VMEM((slots, rows, width), BF16), dma(slots, 2)],
    )(
        ids,
        slot_owner,
        slot_task,
        yz,
        ez,
        *[cars[k] for k in range(peers)],
        *[uppers[k] for k in range(peers)],
    )
    mixed_rows = call(
        norm_part,
        shape(x_rows.shape, BF16),
        [SMEM] * 2 + [VMEM] * 5,
    )(ids, slot_task, gated, own, swapped(own), gain, lens)
    return (mixed_rows, final.reshape(cache_state.shape))


def solution(mesh):
    in_specs = (
        P(("group", "sess", "dp"), None, "head"),
        P(("group", "sess", "dp"), None, "head"),
        P(("group", "sess", "dp"), None, None),
        P(("group", "sess", "dp"), None, None),
        P(("group", "sess", "dp"), "head", None),
        P("head"),
        P("head"),
        P("head"),
        P("head"),
        P(("group", "sess", "dp"), "head", None, None),
        P(("group", "sess", "dp")),
        P("group", None),
        P("group", None),
    )
    out_specs = (
        P(("group", "sess", "dp"), None, "head"),
        P(("group", "sess", "dp"), "head", None, None),
    )
    return jax.shard_map(
        per_device, mesh=mesh, in_specs=in_specs, out_specs=out_specs, check_vma=False
    )
```

```python
import functools

import jax
import jax.numpy as jnp
from jax import lax
from jax.experimental import pallas as pl
from jax.experimental.pallas import tpu as pltpu
from jax.sharding import PartitionSpec as P

F32 = jnp.float32
BF16 = jnp.bfloat16
HALF = 64
VMEM = pl.BlockSpec(memory_space=pltpu.VMEM)
SMEM = pl.BlockSpec(memory_space=pltpu.SMEM)
HBM = pl.BlockSpec(memory_space=pltpu.HBM)
ANY = pl.BlockSpec(memory_space=pl.ANY)


def dot(a, b, dims, precision=None):
    return lax.dot_general(
        a, b, ((dims[:1], dims[1:]), ((), ())), precision=precision, preferred_element_type=F32
    )


def iota(shape, dim):
    return lax.broadcasted_iota(jnp.int32, shape, dim)


def softplus(v):
    return jnp.maximum(v, 0.0) + jnp.log1p(jnp.exp(-jnp.abs(v)))


def running(v):
    rows = v.shape[1]
    upto = jnp.where(iota((rows, rows), 0) <= iota((rows, rows), 1), 1.0, 0.0).astype(F32)
    return dot(v, upto, (1, 0), lax.Precision.HIGHEST)


def silu(v):
    return v * (1.0 / (1.0 + jnp.exp(-v)))


def columns(params):
    heads = params.shape[1]
    eye = iota((heads, heads), 0) == iota((heads, heads), 1)
    return [
        jnp.sum(jnp.where(eye, params[i : i + 1], 0.0), axis=1, keepdims=True)
        for i in range(params.shape[0])
    ]


class Table:
    def __init__(self, tab, peers, slots):
        self.peers, self.slots = peers, slots
        self.me, self.odd, self.length = tab[0], tab[1], tab[2]
        count = peers * slots
        self.owner = lambda i: tab[3 + i]
        self.late = lambda i: tab[3 + count + i] % 2

    def far(self, j):
        return self.me ^ self.owner(self.me * self.slots + j)

    def slot(self, k):
        pick = jnp.int32(0)
        for j in range(1, self.slots):
            pick = jnp.where(self.far(j) == k, j, pick)
        return pick

    def holder(self, k, part):
        found = jnp.int32(0)
        for i in range(self.peers * self.slots):
            hit = (self.owner(i) == self.me ^ k) & (self.late(i) == part)
            found = jnp.where(hit, self.me ^ (i // self.slots), found)
        return found


class Copies:
    def __init__(self, sem):
        self.sem, self.count, self.started = sem, 0, []

    def __call__(self, src, dst, pred=None, again=False):
        self.count += not again
        copy = pltpu.make_async_copy(src, dst, self.sem.at[self.count - 1])
        if pred is None:
            copy.start()
        else:
            pl.when(pred)(copy.start)
        self.started.append((pred, copy))

    def wait(self):
        for pred, copy in self.started:
            if pred is None:
                copy.wait()
            else:
                pl.when(pred)(copy.wait)
        self.started = []


def spans(width):
    return [slice(g * 256, (g + 1) * 256) for g in range(width // 256)]


def chunk(ref, index, width):
    size = width // 256 * HALF
    return ref.at[pl.ds(index * size, size)]


def from_rows(x, j, start, out):
    return [
        (x.at[j, pl.ds(start, HALF), lanes], out.at[pl.ds(g * HALF, HALF)])
        for g, lanes in enumerate(spans(x.shape[2]))
    ]


def tail_of(ref, size, start=0, count=None):
    return ref.at[pl.ds(ref.shape[0] - size + start, size if count is None else count)]


def send_part(peers, tab, x_in, b, c, dt, own, near, *rest):
    far = rest[: peers - 2]
    dtv, packed, x, bc, sem, in_sem = rest[peers - 2 :]
    slots, rows, width = x.shape
    heads = dt.shape[1]
    t = Table(tab, peers, slots)
    copies = Copies(sem)
    first = Copies(in_sem.at[pl.ds(0, 1)])
    first(dt, dtv)
    second = Copies(in_sem.at[pl.ds(1, 2)])
    second(x_in, x)
    second(b, bc, t.odd == 0)
    second(c, bc, t.odd != 0, again=True)
    outs = [own, near] + list(far)
    size = rows + 2 * heads
    first.wait()
    length = jnp.full((heads, rows), t.length.astype(F32)).astype(BF16)
    for j in range(slots):
        value = dtv[j]
        high = value.astype(BF16)
        value = value - high.astype(F32)
        middle = value.astype(BF16)
        low = (value - middle.astype(F32)).astype(BF16)
        packed[j, :heads, :rows] = high
        packed[j, :heads, rows:] = middle
        packed[j, heads:, :rows] = low
        packed[j, heads:, rows:] = length
    second.wait()
    for m in range(peers // 2):
        for src, dst in from_rows(x, t.slot(1 ^ 2 * m), HALF, chunk(near, m + 1, width)):
            copies(src, dst)
    for k in range(peers):
        j = t.slot(k)
        copies(bc.at[j], tail_of(outs[k], size, 0, rows))
        if k:
            for src, dst in from_rows(x, j, 0, chunk(outs[k], 0, width)):
                copies(src, dst)
    for k in range(peers):
        copies(packed.at[t.slot(k)], tail_of(outs[k], size, rows, 2 * heads))
    copies.wait()


def forward_part(peers, slots, tab, x, near, after, *rest):
    outs, sem = rest[:-1], rest[-1]
    rows, width = x.shape[1:]
    t = Table(tab, peers, slots)
    copies = Copies(sem)
    for m in range(1, peers // 2):
        at = t.holder(2 * m, 0)
        copies(chunk(near, m + 1, width), outs[m - 1], at == 1)
        for g, (src, dst) in enumerate(from_rows(x, t.slot(2 * m), HALF, outs[m - 1])):
            copies(src, dst, at == 0, again=not g)
    copies.wait()


def pick_part(peers, slots, heads, tab, *rest):
    got = rest[:peers]
    mine, dts, lens, tails, counts, sem = rest[peers + 1 :]
    rows = mine.shape[0] - HALF
    size = rows + 2 * heads
    t = Table(tab, peers, slots)
    copies = Copies(sem)
    for part in range(2):
        at = t.holder(0, part)
        for k in range(peers):
            copies(tail_of(got[k], size), tails.at[part], at == k, again=k > 0)
    for j in range(slots):
        for k in range(peers):
            copies(
                tail_of(got[k], size, rows + heads, heads), counts.at[j], t.far(j) == k, again=k > 0
            )
    copies.wait()
    mine[:rows] = tails[0, :rows]
    mine[rows:] = tails[1, :HALF]
    for part in range(2):
        first = tails[part, rows : rows + heads].astype(F32)
        second = tails[part, rows + heads :].astype(F32)
        dts[part] = first[:, :rows] + (first[:, rows:] + second[:, :rows])
    for j in range(slots):
        lens[j] = counts[j, :, rows:].astype(F32)


def touch_part(value, out):
    out[...] = jnp.zeros(out.shape, out.dtype)


def share_part(peers, slots, tab, dts, params, share0, share1, decays):
    parts, heads, rows = dts.shape
    width = share0.shape[1]
    size = width // heads
    per = 128 // size
    length = Table(tab, peers, slots).length
    alog, bias, _ = columns(params)
    rate = -jnp.exp(alog)
    col = iota((heads, rows), 1)
    lane = iota((rows, 128), 1) // size
    for part, out in ((0, share0), (1, share1)):
        step = jnp.where(col < length - part * rows, softplus(dts[part] + bias), 0.0)
        log_decay = running(rate * step)
        total = log_decay[:, rows - 1 :]
        share = jnp.transpose(jnp.exp(total - log_decay) * step)
        decays[part] = jnp.broadcast_to(jnp.exp(total).astype(BF16).astype(F32), (heads, 256))
        for p in range(width // 128):
            factor = jnp.broadcast_to(share[:, p * per : p * per + 1], (rows, 128))
            for q in range(1, per):
                factor = jnp.where(lane == q, share[:, p * per + q : p * per + q + 1], factor)
            out[:, p * 128 : (p + 1) * 128] = factor[: out.shape[0]]


def block_part(x_in, z_in, b_in, c_in, dt_in, params, yz, ez, x, z, b, c, dt, sem):
    slots, rows, width = x.shape
    heads = dt.shape[1]
    size = width // heads
    per = 128 // size
    waits = []
    for s in range(slots):
        copies = Copies(sem.at[s])
        for src, dst in ((dt_in, dt), (b_in, b), (c_in, c), (x_in, x), (z_in, z)):
            copies(src.at[s], dst.at[s])
        waits.append(copies)
    causal = iota((rows, rows), 0) >= iota((rows, rows), 1)
    lane = iota((rows, 128), 1) // size
    alog, bias, skip = columns(params)
    rate = -jnp.exp(alog)
    for s in range(slots):
        waits[s].wait()
        step = softplus(dt[s] + bias)
        log_decay = running(rate * step)
        log_col = jnp.transpose(log_decay)
        decay_col = jnp.exp(log_col)
        scores = jnp.where(causal, dot(c[s], b[s], (1, 1)), 0.0)
        for p in range(width // 128):
            lanes = slice(p * 128, (p + 1) * 128)
            xp = x[s, :, lanes]
            weights = []
            parts = []
            decay = decay_col[:, p * per : p * per + 1]
            own_skip = skip[p * per : p * per + 1]
            for q in range(per):
                h = p * per + q
                gap = jnp.minimum(log_col[:, h : h + 1] - log_decay[h : h + 1], 0.0)
                weights.append((jnp.exp(gap) * step[h : h + 1] * scores).astype(BF16))
                parts.append(jnp.where(lane == q, xp, jnp.zeros_like(xp)))
                if q:
                    decay = jnp.where(lane == q, decay_col[:, h : h + 1], decay)
                    own_skip = jnp.where(lane[:1] == q, skip[h : h + 1], own_skip)
            inner = dot(jnp.concatenate(weights, axis=1), jnp.concatenate(parts, axis=0), (1, 0))
            gate = silu(z[s, :, lanes].astype(F32))
            yz[s, :, lanes] = (inner + own_skip * xp.astype(F32)) * gate
            ez[s, :, lanes] = decay * gate


def early_part(peers, slots, tab, cache, mine, other, token, decays, upper):
    def work(cs):
        for lanes in spans(cache.shape[0]):
            upper[:, lanes] = dot(cs[HALF : 2 * HALF], cache[lanes], (1, 1)).astype(BF16)

    odd = Table(tab, peers, slots).odd
    pl.when(odd == 0)(lambda: work(other))
    pl.when(odd != 0)(lambda: work(mine))


def late_part(peers, slots, tab, cache, mine, other, share, decays, x, near, *rest):
    half = peers // 2
    far, onward = rest[: peers - 2], rest[peers - 2 : peers - 3 + half]
    rest = rest[peers - 3 + half :]
    late, second, cars = rest[0], rest[1], rest[2 : peers + 2]
    low, high, car0, car1, bs, cs, sem = rest[peers + 2 :]
    rows, width = share.shape
    heads = decays.shape[1]
    size = width // heads
    t = Table(tab, peers, slots)
    k0, k1, j = t.holder(0, 0), t.holder(0, 1), t.slot(0)
    loads = Copies(sem)
    others = Copies(sem.at[pl.ds(2 * width // 256, width // 256 + 2)])
    straight = [(1, chunk(near, 0, width))] + [
        (k, chunk(far[k - 2], 0, width)) for k in range(2, peers)
    ]
    for g, (src, dst) in enumerate(from_rows(x, j, HALF, high)):
        loads(src, dst, k0 == 0)
    loads(chunk(near, 1, width), high, k0 == 1, again=True)
    for m in range(1, half):
        loads(onward[m - 1], high, k0 // 2 == m, again=True)
    for at, out, use in ((k0, low, loads), (k1, second, others)):
        for g, (src, dst) in enumerate(from_rows(x, j, 0, out)):
            use(src, dst, at == 0)
        for k, src in straight:
            use(src, out, at == k, again=True)

    @pl.when(t.odd == 0)
    def _():
        bs[...] = mine[:rows]
        cs[...] = other[...]

    @pl.when(t.odd != 0)
    def _():
        bs[...] = other[:rows]
        cs[...] = mine[...]

    for lanes in spans(width):
        car0[:, lanes] = dot(cs[:HALF], cache[lanes], (1, 1)).astype(BF16)
    loads.wait()
    for g, lanes in enumerate(spans(width)):
        at = slice(g * HALF, (g + 1) * HALF)
        xv = jnp.concatenate([low[at], high[at]], axis=0).astype(F32)
        local = dot((xv * share[:, lanes]).astype(BF16), bs[...], (0, 0)).astype(BF16).astype(F32)
        for q in range(256 // size):
            h = g * (256 // size) + q
            state = slice(h * size, (h + 1) * size)
            late[state] = (
                decays[0, h : h + 1] * cache[state].astype(F32)
                + local[q * size : (q + 1) * size]
            ).astype(BF16)
        car1[:, lanes] = dot(cs[rows:], late[lanes], (1, 1)).astype(BF16)
    others.wait()
    stores = Copies(sem)
    for at, src in ((k0, car0), (k1, car1)):
        for k in range(peers):
            stores(src, cars[k], at == k, again=k > 0)
    stores.wait()


def final_part(peers, slots, tab, mine, other, share, decays, late, second, final, bs):
    width = share.shape[1]
    heads = decays.shape[1]
    size = width // heads
    rows = mine.shape[0] - HALF
    odd = Table(tab, peers, slots).odd

    @pl.when(odd == 0)
    def _():
        bs[...] = mine[rows:]

    @pl.when(odd != 0)
    def _():
        bs[...] = other[rows:]

    for g, lanes in enumerate(spans(width)):
        xv = second[g * HALF : (g + 1) * HALF].astype(F32)
        local = dot((xv * share[:, lanes]).astype(BF16), bs[...], (0, 0)).astype(BF16).astype(F32)
        for q in range(256 // size):
            h = g * (256 // size) + q
            state = slice(h * size, (h + 1) * size)
            final[state] = (
                decays[1, h : h + 1] * late[state].astype(F32)
                + local[q * size : (q + 1) * size]
            ).astype(BF16)


def gate_part(peers, tab, yz, ez, *rest):
    cars, uppers = rest[:peers], rest[peers : 2 * peers]
    gated, squares, got, sem = rest[2 * peers :]
    slots, rows, width = yz.shape
    t = Table(tab, peers, slots)
    waits = []
    for j in range(slots):
        copies = Copies(sem.at[j])
        early = t.late(t.me * slots + j) == 0
        for k in range(peers):
            copies(cars[k], got.at[j, pl.ds(0, HALF)], t.far(j) == k, again=k > 0)
        for k in range(peers):
            copies(
                uppers[k], got.at[j, pl.ds(HALF, HALF)], (t.far(j) == k) & early, again=k > 0
            )
        waits.append(copies)
    for j in range(slots):
        waits[j].wait()
        total = jnp.zeros((rows, 128), F32)
        for p in range(width // 128):
            lanes = slice(p * 128, (p + 1) * 128)
            value = yz[j, :, lanes] + ez[j, :, lanes] * got[j, :, lanes].astype(F32)
            gated[j, :, lanes] = value
            total = total + value * value
        squares[j : j + 1] = jnp.sum(jnp.transpose(total), axis=0, keepdims=True)


def norm_part(peers, tab, gated, own, other, gain, lens, mixed):
    slots, rows, width = gated.shape
    t = Table(tab, peers, slots)
    row = iota((rows, 128), 0).astype(F32)
    for j in range(slots):
        late = t.late(t.me * slots + j)
        live = row + (late * rows).astype(F32) < lens[j][:1]
        mean = (own[j : j + 1] + other[j : j + 1]) / (2.0 * width)
        inverse = jnp.transpose(jnp.broadcast_to(lax.rsqrt(mean + 1e-05), (rows, rows)))
        for p in range(width // 128):
            lanes = slice(p * 128, (p + 1) * 128)
            value = gated[j, :, lanes] * inverse * gain[:, lanes].astype(F32)
            mixed[j, :, lanes] = jnp.where(live, value, 0.0).astype(BF16)


def call(kernel, outs, in_specs, out_specs=None, scratch=(), limit=24, cost=0):
    return pl.pallas_call(
        kernel,
        out_shape=outs,
        in_specs=in_specs,
        out_specs=out_specs if out_specs is not None else jax.tree.map(lambda _: VMEM, outs),
        scratch_shapes=scratch,
        compiler_params=pltpu.CompilerParams(vmem_limit_bytes=limit * 1024 * 1024),
        cost_estimate=pl.CostEstimate(flops=0, bytes_accessed=cost, transcendentals=0),
    )


def per_device(
    x_rows,
    z_rows,
    input_projection_matrix,
    c_rows,
    dt_raw,
    a_log,
    dt_bias,
    d_skip,
    norm_gain,
    cache_state,
    lengths,
    slot_owner,
    slot_task,
):
    slots, rows, width = x_rows.shape
    heads = dt_raw.shape[1]
    state = cache_state.shape[3]
    peers = lax.axis_size("sess")
    half = peers // 2
    head = lax.axis_index("head")
    groups = input_projection_matrix.shape[2] // state
    if groups > 1:
        at = head // 2 * state
        b = lax.dynamic_slice_in_dim(input_projection_matrix, at, state, 2)
        c = lax.dynamic_slice_in_dim(c_rows, at, state, 2)
    else:
        b, c = input_projection_matrix, c_rows

    def own_row(table):
        mine = iota(table.shape, 0) == lax.axis_index("dp")
        return jnp.sum(jnp.where(mine, table, 0), axis=0)

    ids = jnp.stack([lax.axis_index("sess"), head % 2]).astype(jnp.int32)
    tab = jnp.concatenate([ids, lengths, own_row(slot_owner), own_row(slot_task)])
    params = jnp.stack([a_log, dt_bias, d_skip])
    cache = cache_state.reshape(width, state)

    def far(value, k):
        return lax.ppermute(value, "sess", [(i, i ^ k) for i in range(peers)])

    def swapped(value):
        count = lax.axis_size("head")
        return lax.ppermute(value, "head", [(i, i ^ 1) for i in range(count)])

    def scratch(*sizes, dtype=BF16):
        return pltpu.VMEM(sizes, dtype)

    shape = jax.ShapeDtypeStruct
    dma = lambda *sizes: pltpu.SemaphoreType.DMA(sizes)
    bind = lambda kernel, *more: functools.partial(kernel, peers, *more)
    count = width // 256
    piece = count * HALF
    tail = rows + 2 * heads
    packed = lambda size: shape((size, 256), BF16)
    upper_rows = shape((HALF, width), BF16)
    own, near, *sends = call(
        bind(send_part),
        [packed(tail), packed((1 + half) * piece + tail)] + [packed(piece + tail)] * (peers - 2),
        [SMEM, HBM, HBM, HBM, HBM],
        [ANY] * peers,
        [
            scratch(*dt_raw.shape, dtype=F32),
            scratch(slots, 2 * heads, state),
            scratch(*x_rows.shape),
            scratch(*b.shape),
            dma((half + peers - 1) * count + 2 * peers),
            dma(3),
        ],
        limit=60,
    )(tab, x_rows, b, c, dt_raw)
    near = far(near, 1)
    sends = [far(value, k + 2) for k, value in enumerate(sends)]
    yz, ez = call(
        block_part,
        [shape(x_rows.shape, F32)] * 2,
        [HBM] * 5 + [VMEM],
        scratch=[
            scratch(*x_rows.shape),
            scratch(*x_rows.shape),
            scratch(*b.shape),
            scratch(*b.shape),
            scratch(*dt_raw.shape, dtype=F32),
            dma(slots, 5),
        ],
    )(x_rows, z_rows, b, c, dt_raw, params)
    passing = call(
        bind(forward_part, slots),
        [packed(piece)] * (half - 1),
        [SMEM, HBM, ANY, ANY],
        [ANY] * (half - 1),
        [dma((half - 1) * count)],
    )(tab, x_rows, near, ez)
    onward = [far(value, 2 * (m + 1)) for m, value in enumerate(passing)]
    mine, dts, lens = call(
        bind(pick_part, slots, heads),
        [
            shape((rows + HALF, state), BF16),
            shape((2, heads, rows), F32),
            shape((slots, heads, rows), F32),
        ],
        [SMEM] + [ANY] * (peers + 1),
        scratch=[scratch(2, tail, 256), scratch(slots, heads, 256), dma(2 + slots)],
    )(tab, own, near, *sends, passing[0])
    other = swapped(mine)
    share0, share1, decays = call(
        bind(share_part, slots),
        [shape((rows, width), F32), shape((HALF, width), F32), shape((2, heads, 256), F32)],
        [SMEM, VMEM, VMEM],
    )(tab, dts, params)
    token = call(touch_part, shape((8, 128), F32), [ANY], cost=40_000_000)(onward[0])
    upper = call(
        bind(early_part, slots), upper_rows, [SMEM, VMEM, VMEM, VMEM, ANY, ANY]
    )(tab, cache, mine, other, token, decays)
    uppers = {2 * m: far(upper, 2 * m) if m else upper for m in range(half)}
    late, second, *cars = call(
        bind(late_part, slots),
        [shape((width, state), BF16), packed(piece)] + [upper_rows] * peers,
        [SMEM] + [VMEM] * 5 + [HBM] + [ANY] * (peers + half - 2),
        [VMEM, VMEM] + [ANY] * peers,
        [
            scratch(piece, 256),
            scratch(piece, 256),
            scratch(HALF, width),
            scratch(HALF, width),
            scratch(rows, state),
            scratch(rows + HALF, state),
            dma(3 * count + 2),
        ],
    )(tab, cache, mine, other, share0, decays, x_rows, near, *sends, *onward)
    cars = {0: cars[0]} | {k: far(cars[k], k) for k in list(range(2, peers)) + [1]}
    uppers |= {2 * m + 1: far(uppers[2 * m], 1) for m in range(half)}
    final = call(
        bind(final_part, slots),
        shape((width, state), BF16),
        [SMEM] + [VMEM] * 6,
        scratch=[scratch(HALF, state)],
    )(tab, mine, other, share1, decays, late, second)
    gated, squares = call(
        bind(gate_part),
        [shape(x_rows.shape, F32), shape((slots, rows), F32)],
        [SMEM, VMEM, VMEM] + [ANY] * (2 * peers),
        scratch=[scratch(slots, rows, width), dma(slots, 2)],
    )(
        tab,
        yz,
        ez,
        *[cars[k] for k in range(peers)],
        *[uppers[k] for k in range(peers)],
    )
    mixed_rows = call(bind(norm_part), shape(x_rows.shape, BF16), [SMEM] + [VMEM] * 5)(
        tab, gated, squares, swapped(squares), norm_gain[None], lens
    )
    return (mixed_rows, final.reshape(cache_state.shape))


def solution(mesh):
    in_specs = (
        P(("group", "sess", "dp"), None, "head"),
        P(("group", "sess", "dp"), None, "head"),
        P(("group", "sess", "dp"), None, None),
        P(("group", "sess", "dp"), None, None),
        P(("group", "sess", "dp"), "head", None),
        P("head"),
        P("head"),
        P("head"),
        P("head"),
        P(("group", "sess", "dp"), "head", None, None),
        P(("group", "sess", "dp")),
        P("group", None),
        P("group", None),
    )
    out_specs = (
        P(("group", "sess", "dp"), None, "head"),
        P(("group", "sess", "dp"), "head", None, None),
    )
    return jax.shard_map(
        per_device, mesh=mesh, in_specs=in_specs, out_specs=out_specs, check_vma=False
    )
```

```python
import functools

import jax
import jax.numpy as jnp
from jax import lax
from jax.experimental import pallas as pl
from jax.experimental.pallas import tpu as pltpu
from jax.sharding import PartitionSpec as P

F32 = jnp.float32
BF16 = jnp.bfloat16
HALF = 64
VMEM = pl.BlockSpec(memory_space=pltpu.VMEM)
SMEM = pl.BlockSpec(memory_space=pltpu.SMEM)
HBM = pl.BlockSpec(memory_space=pltpu.HBM)
ANY = pl.BlockSpec(memory_space=pl.ANY)


def dot(a, b, dims, precision=None):
    return lax.dot_general(
        a, b, ((dims[:1], dims[1:]), ((), ())), precision=precision, preferred_element_type=F32
    )


def iota(shape, dim):
    return lax.broadcasted_iota(jnp.int32, shape, dim)


def softplus(v):
    return jnp.maximum(v, 0.0) + jnp.log1p(jnp.exp(-jnp.abs(v)))


def running(v):
    rows = v.shape[1]
    upto = jnp.where(iota((rows, rows), 0) <= iota((rows, rows), 1), 1.0, 0.0).astype(F32)
    return dot(v, upto, (1, 0), lax.Precision.HIGHEST)


def silu(v):
    return v * (1.0 / (1.0 + jnp.exp(-v)))


def columns(params):
    heads = params.shape[1]
    eye = iota((heads, heads), 0) == iota((heads, heads), 1)
    return [
        jnp.sum(jnp.where(eye, params[i : i + 1], 0.0), axis=1, keepdims=True)
        for i in range(params.shape[0])
    ]


class Table:
    def __init__(self, tab, peers, slots):
        self.peers, self.slots = peers, slots
        self.me, self.odd, self.length = tab[0], tab[1], tab[2]
        count = peers * slots
        self.owner = lambda i: tab[3 + i]
        self.late = lambda i: tab[3 + count + i] % 2

    def far(self, j):
        return self.me ^ self.owner(self.me * self.slots + j)

    def slot(self, k):
        pick = jnp.int32(0)
        for j in range(1, self.slots):
            pick = jnp.where(self.far(j) == k, j, pick)
        return pick

    def holder(self, k, part):
        found = jnp.int32(0)
        for i in range(self.peers * self.slots):
            hit = (self.owner(i) == self.me ^ k) & (self.late(i) == part)
            found = jnp.where(hit, self.me ^ (i // self.slots), found)
        return found


class Copies:
    def __init__(self, sem):
        self.sem, self.count, self.started = sem, 0, []

    def __call__(self, src, dst, pred=None, again=False):
        self.count += not again
        copy = pltpu.make_async_copy(src, dst, self.sem.at[self.count - 1])
        if pred is None:
            copy.start()
        else:
            pl.when(pred)(copy.start)
        self.started.append((pred, copy))

    def wait(self):
        for pred, copy in self.started:
            if pred is None:
                copy.wait()
            else:
                pl.when(pred)(copy.wait)
        self.started = []


def spans(width):
    return [slice(g * 256, (g + 1) * 256) for g in range(width // 256)]


def chunk(ref, index, width):
    size = width // 256 * HALF
    return ref.at[pl.ds(index * size, size)]


def from_rows(x, j, start, out):
    return [
        (x.at[j, pl.ds(start, HALF), lanes], out.at[pl.ds(g * HALF, HALF)])
        for g, lanes in enumerate(spans(x.shape[2]))
    ]


def tail_of(ref, size, start=0, count=None):
    return ref.at[pl.ds(ref.shape[0] - size + start, size if count is None else count)]


def send_part(peers, x_in, b, c, dt, owner, lens, own, near, *rest):
    outs = (own, near, *rest[: peers - 2])
    dtv, x, bc, table, length, sem = rest[peers - 2 :]
    slots, rows, width = x.shape
    heads = dt.shape[1]
    dp = lax.axis_index("dp")
    odd = lax.axis_index("head") % 2
    copies = Copies(sem)
    copies(owner, table)
    copies(lens, length)
    copies(dt, dtv)
    copies(x_in, x)
    copies(b, bc, odd == 0)
    copies(c, bc, odd != 0, again=True)
    copies.wait()
    t = Table([lax.axis_index("sess"), odd, length[0]], peers, slots)
    t.owner = lambda i: table[dp, i]
    count = jnp.full((heads, rows), t.length.astype(F32)).astype(BF16)
    picks = [t.slot(k) for k in range(peers)]

    def put(out, index, j, start):
        for g, lanes in enumerate(spans(width)):
            at = (index * (width // 256) + g) * HALF
            out[at : at + HALF] = x[j, start : start + HALF, lanes]

    for k in list(range(2, peers)) + [1, 0]:
        out, j = outs[k], picks[k]
        at = out.shape[0] - rows - 2 * heads
        out[at : at + rows] = bc[j]
        value = dtv[j]
        high = value.astype(BF16)
        value = value - high.astype(F32)
        middle = value.astype(BF16)
        low = (value - middle.astype(F32)).astype(BF16)
        out[at + rows : at + rows + heads] = jnp.concatenate([high, middle], axis=1)
        out[at + rows + heads :] = jnp.concatenate([low, count], axis=1)
        if k:
            put(out, 0, j, 0)
    for m in range(peers // 2):
        put(near, m + 1, picks[1 ^ 2 * m], HALF)


def forward_part(peers, slots, tab, x, near, after, *rest):
    outs, sem = rest[:-1], rest[-1]
    rows, width = x.shape[1:]
    t = Table(tab, peers, slots)
    copies = Copies(sem)
    for m in range(1, peers // 2):
        at = t.holder(2 * m, 0)
        copies(chunk(near, m + 1, width), outs[m - 1], at == 1)
        for g, (src, dst) in enumerate(from_rows(x, t.slot(2 * m), HALF, outs[m - 1])):
            copies(src, dst, at == 0, again=not g)
    copies.wait()


def pick_part(peers, slots, heads, tab, *rest):
    got = rest[:peers]
    mine, dts, lens, tails, counts, sem = rest[peers + 1 :]
    rows = mine.shape[0] - HALF
    size = rows + 2 * heads
    t = Table(tab, peers, slots)
    copies = Copies(sem)
    for part in range(2):
        at = t.holder(0, part)
        for k in range(peers):
            copies(tail_of(got[k], size), tails.at[part], at == k, again=k > 0)
    for j in range(slots):
        for k in range(peers):
            copies(
                tail_of(got[k], size, rows + heads, heads), counts.at[j], t.far(j) == k, again=k > 0
            )
    copies.wait()
    mine[:rows] = tails[0, :rows]
    mine[rows:] = tails[1, :HALF]
    for part in range(2):
        first = tails[part, rows : rows + heads].astype(F32)
        second = tails[part, rows + heads :].astype(F32)
        dts[part] = first[:, :rows] + (first[:, rows:] + second[:, :rows])
    for j in range(slots):
        lens[j] = counts[j, :, rows:].astype(F32)


def touch_part(value, out):
    out[...] = jnp.zeros(out.shape, out.dtype)


def share_part(peers, slots, tab, dts, params, share0, share1, decays):
    parts, heads, rows = dts.shape
    width = share0.shape[1]
    size = width // heads
    per = 128 // size
    length = Table(tab, peers, slots).length
    alog, bias, _ = columns(params)
    rate = -jnp.exp(alog)
    col = iota((heads, rows), 1)
    lane = iota((rows, 128), 1) // size
    for part, out in ((0, share0), (1, share1)):
        step = jnp.where(col < length - part * rows, softplus(dts[part] + bias), 0.0)
        log_decay = running(rate * step)
        total = log_decay[:, rows - 1 :]
        share = jnp.transpose(jnp.exp(total - log_decay) * step)
        decays[part] = jnp.broadcast_to(jnp.exp(total).astype(BF16).astype(F32), (heads, 256))
        for p in range(width // 128):
            factor = jnp.broadcast_to(share[:, p * per : p * per + 1], (rows, 128))
            for q in range(1, per):
                factor = jnp.where(lane == q, share[:, p * per + q : p * per + q + 1], factor)
            out[:, p * 128 : (p + 1) * 128] = factor[: out.shape[0]]


def block_part(x_in, z_in, b_in, c_in, dt_in, params, yz, ez, x, z, b, c, dt, sem):
    slots, rows, width = x.shape
    heads = dt.shape[1]
    size = width // heads
    per = 128 // size
    waits = []
    for s in range(slots):
        copies = Copies(sem.at[s])
        for src, dst in ((dt_in, dt), (b_in, b), (c_in, c), (x_in, x), (z_in, z)):
            copies(src.at[s], dst.at[s])
        waits.append(copies)
    causal = iota((rows, rows), 0) >= iota((rows, rows), 1)
    lane = iota((rows, 128), 1) // size
    alog, bias, skip = columns(params)
    rate = -jnp.exp(alog)
    for s in range(slots):
        waits[s].wait()
        step = softplus(dt[s] + bias)
        log_decay = running(rate * step)
        log_col = jnp.transpose(log_decay)
        decay_col = jnp.exp(log_col)
        scores = jnp.where(causal, dot(c[s], b[s], (1, 1)), 0.0)
        for p in range(width // 128):
            lanes = slice(p * 128, (p + 1) * 128)
            xp = x[s, :, lanes]
            weights = []
            parts = []
            decay = decay_col[:, p * per : p * per + 1]
            own_skip = skip[p * per : p * per + 1]
            for q in range(per):
                h = p * per + q
                gap = jnp.minimum(log_col[:, h : h + 1] - log_decay[h : h + 1], 0.0)
                weights.append((jnp.exp(gap) * step[h : h + 1] * scores).astype(BF16))
                parts.append(jnp.where(lane == q, xp, jnp.zeros_like(xp)))
                if q:
                    decay = jnp.where(lane == q, decay_col[:, h : h + 1], decay)
                    own_skip = jnp.where(lane[:1] == q, skip[h : h + 1], own_skip)
            inner = dot(jnp.concatenate(weights, axis=1), jnp.concatenate(parts, axis=0), (1, 0))
            gate = silu(z[s, :, lanes].astype(F32))
            yz[s, :, lanes] = (inner + own_skip * xp.astype(F32)) * gate
            ez[s, :, lanes] = decay * gate


def early_part(peers, slots, tab, cache, mine, other, token, decays, upper):
    def work(cs):
        for lanes in spans(cache.shape[0]):
            upper[:, lanes] = dot(cs[HALF : 2 * HALF], cache[lanes], (1, 1)).astype(BF16)

    odd = Table(tab, peers, slots).odd
    pl.when(odd == 0)(lambda: work(other))
    pl.when(odd != 0)(lambda: work(mine))


def late_part(peers, slots, tab, cache, mine, other, share, decays, x, near, *rest):
    half = peers // 2
    far, onward = rest[: peers - 2], rest[peers - 2 : peers - 3 + half]
    rest = rest[peers - 3 + half :]
    late, second, cars = rest[0], rest[1], rest[2 : peers + 2]
    low, high, car0, car1, bs, cs, sem = rest[peers + 2 :]
    rows, width = share.shape
    heads = decays.shape[1]
    size = width // heads
    t = Table(tab, peers, slots)
    k0, k1, j = t.holder(0, 0), t.holder(0, 1), t.slot(0)
    loads = Copies(sem)
    others = Copies(sem.at[pl.ds(2 * width // 256, width // 256 + 2)])
    straight = [(1, chunk(near, 0, width))] + [
        (k, chunk(far[k - 2], 0, width)) for k in range(2, peers)
    ]
    for g, (src, dst) in enumerate(from_rows(x, j, HALF, high)):
        loads(src, dst, k0 == 0)
    loads(chunk(near, 1, width), high, k0 == 1, again=True)
    for m in range(1, half):
        loads(onward[m - 1], high, k0 // 2 == m, again=True)
    for at, out, use in ((k0, low, loads), (k1, second, others)):
        for g, (src, dst) in enumerate(from_rows(x, j, 0, out)):
            use(src, dst, at == 0)
        for k, src in straight:
            use(src, out, at == k, again=True)

    @pl.when(t.odd == 0)
    def _():
        bs[...] = mine[:rows]
        cs[...] = other[...]

    @pl.when(t.odd != 0)
    def _():
        bs[...] = other[:rows]
        cs[...] = mine[...]

    for lanes in spans(width):
        car0[:, lanes] = dot(cs[:HALF], cache[lanes], (1, 1)).astype(BF16)
    loads.wait()
    for g, lanes in enumerate(spans(width)):
        at = slice(g * HALF, (g + 1) * HALF)
        xv = jnp.concatenate([low[at], high[at]], axis=0).astype(F32)
        local = dot((xv * share[:, lanes]).astype(BF16), bs[...], (0, 0)).astype(BF16).astype(F32)
        for q in range(256 // size):
            h = g * (256 // size) + q
            state = slice(h * size, (h + 1) * size)
            late[state] = (
                decays[0, h : h + 1] * cache[state].astype(F32)
                + local[q * size : (q + 1) * size]
            ).astype(BF16)
        car1[:, lanes] = dot(cs[rows:], late[lanes], (1, 1)).astype(BF16)
    others.wait()
    stores = Copies(sem)
    for at, src in ((k0, car0), (k1, car1)):
        for k in range(peers):
            stores(src, cars[k], at == k, again=k > 0)
    stores.wait()


def final_part(peers, slots, tab, mine, other, share, decays, late, second, final, bs):
    width = share.shape[1]
    heads = decays.shape[1]
    size = width // heads
    rows = mine.shape[0] - HALF
    odd = Table(tab, peers, slots).odd

    @pl.when(odd == 0)
    def _():
        bs[...] = mine[rows:]

    @pl.when(odd != 0)
    def _():
        bs[...] = other[rows:]

    for g, lanes in enumerate(spans(width)):
        xv = second[g * HALF : (g + 1) * HALF].astype(F32)
        local = dot((xv * share[:, lanes]).astype(BF16), bs[...], (0, 0)).astype(BF16).astype(F32)
        for q in range(256 // size):
            h = g * (256 // size) + q
            state = slice(h * size, (h + 1) * size)
            final[state] = (
                decays[1, h : h + 1] * late[state].astype(F32)
                + local[q * size : (q + 1) * size]
            ).astype(BF16)


def gate_part(peers, tab, yz, ez, *rest):
    cars, uppers = rest[:peers], rest[peers : 2 * peers]
    gated, squares, got, sem = rest[2 * peers :]
    slots, rows, width = yz.shape
    t = Table(tab, peers, slots)
    waits = []
    for j in range(slots):
        copies = Copies(sem.at[j])
        early = t.late(t.me * slots + j) == 0
        for k in range(peers):
            copies(cars[k], got.at[j, pl.ds(0, HALF)], t.far(j) == k, again=k > 0)
        for k in range(peers):
            copies(
                uppers[k], got.at[j, pl.ds(HALF, HALF)], (t.far(j) == k) & early, again=k > 0
            )
        waits.append(copies)
    for j in range(slots):
        waits[j].wait()
        total = jnp.zeros((rows, 128), F32)
        for p in range(width // 128):
            lanes = slice(p * 128, (p + 1) * 128)
            value = yz[j, :, lanes] + ez[j, :, lanes] * got[j, :, lanes].astype(F32)
            gated[j, :, lanes] = value
            total = total + value * value
        squares[j : j + 1] = jnp.sum(jnp.transpose(total), axis=0, keepdims=True)


def norm_part(peers, tab, gated, own, other, gain, lens, mixed):
    slots, rows, width = gated.shape
    t = Table(tab, peers, slots)
    row = iota((rows, 128), 0).astype(F32)
    for j in range(slots):
        late = t.late(t.me * slots + j)
        live = row + (late * rows).astype(F32) < lens[j][:1]
        mean = (own[j : j + 1] + other[j : j + 1]) / (2.0 * width)
        inverse = jnp.transpose(jnp.broadcast_to(lax.rsqrt(mean + 1e-05), (rows, rows)))
        for p in range(width // 128):
            lanes = slice(p * 128, (p + 1) * 128)
            value = gated[j, :, lanes] * inverse * gain[:, lanes].astype(F32)
            mixed[j, :, lanes] = jnp.where(live, value, 0.0).astype(BF16)


def call(kernel, outs, in_specs, out_specs=None, scratch=(), limit=24, cost=0):
    return pl.pallas_call(
        kernel,
        out_shape=outs,
        in_specs=in_specs,
        out_specs=out_specs if out_specs is not None else jax.tree.map(lambda _: VMEM, outs),
        scratch_shapes=scratch,
        compiler_params=pltpu.CompilerParams(vmem_limit_bytes=limit * 1024 * 1024),
        cost_estimate=pl.CostEstimate(flops=0, bytes_accessed=cost, transcendentals=0),
    )


def per_device(
    x_rows,
    z_rows,
    input_projection_matrix,
    c_rows,
    dt_raw,
    a_log,
    dt_bias,
    d_skip,
    norm_gain,
    cache_state,
    lengths,
    slot_owner,
    slot_task,
):
    slots, rows, width = x_rows.shape
    heads = dt_raw.shape[1]
    state = cache_state.shape[3]
    peers = lax.axis_size("sess")
    half = peers // 2
    head = lax.axis_index("head")
    groups = input_projection_matrix.shape[2] // state
    if groups > 1:
        at = head // 2 * state
        b = lax.dynamic_slice_in_dim(input_projection_matrix, at, state, 2)
        c = lax.dynamic_slice_in_dim(c_rows, at, state, 2)
    else:
        b, c = input_projection_matrix, c_rows

    def own_row(table):
        mine = iota(table.shape, 0) == lax.axis_index("dp")
        return jnp.sum(jnp.where(mine, table, 0), axis=0)

    ids = jnp.stack([lax.axis_index("sess"), head % 2]).astype(jnp.int32)
    tab = jnp.concatenate([ids, lengths, own_row(slot_owner), own_row(slot_task)])
    params = jnp.stack([a_log, dt_bias, d_skip])
    cache = cache_state.reshape(width, state)

    def far(value, k):
        return lax.ppermute(value, "sess", [(i, i ^ k) for i in range(peers)])

    def swapped(value):
        count = lax.axis_size("head")
        return lax.ppermute(value, "head", [(i, i ^ 1) for i in range(count)])

    def scratch(*sizes, dtype=BF16):
        return pltpu.VMEM(sizes, dtype)

    shape = jax.ShapeDtypeStruct
    dma = lambda *sizes: pltpu.SemaphoreType.DMA(sizes)
    bind = lambda kernel, *more: functools.partial(kernel, peers, *more)
    count = width // 256
    piece = count * HALF
    tail = rows + 2 * heads
    packed = lambda size: shape((size, 256), BF16)
    upper_rows = shape((HALF, width), BF16)
    own, near, *sends = call(
        bind(send_part),
        [packed(tail), packed((1 + half) * piece + tail)] + [packed(piece + tail)] * (peers - 2),
        [HBM] * 6,
        scratch=[
            scratch(*dt_raw.shape, dtype=F32),
            scratch(*x_rows.shape),
            scratch(*b.shape),
            pltpu.SMEM(slot_owner.shape, jnp.int32),
            pltpu.SMEM(lengths.shape, jnp.int32),
            dma(5),
        ],
        limit=60,
    )(x_rows, b, c, dt_raw, slot_owner, lengths)
    near = far(near, 1)
    sends = [far(value, k + 2) for k, value in enumerate(sends)]
    yz, ez = call(
        block_part,
        [shape(x_rows.shape, F32)] * 2,
        [HBM] * 5 + [VMEM],
        scratch=[
            scratch(*x_rows.shape),
            scratch(*x_rows.shape),
            scratch(*b.shape),
            scratch(*b.shape),
            scratch(*dt_raw.shape, dtype=F32),
            dma(slots, 5),
        ],
    )(x_rows, z_rows, b, c, dt_raw, params)
    passing = call(
        bind(forward_part, slots),
        [packed(piece)] * (half - 1),
        [SMEM, HBM, ANY, ANY],
        [ANY] * (half - 1),
        [dma((half - 1) * count)],
    )(tab, x_rows, near, ez)
    onward = [far(value, 2 * (m + 1)) for m, value in enumerate(passing)]
    mine, dts, lens = call(
        bind(pick_part, slots, heads),
        [
            shape((rows + HALF, state), BF16),
            shape((2, heads, rows), F32),
            shape((slots, heads, rows), F32),
        ],
        [SMEM] + [ANY] * (peers + 1),
        scratch=[scratch(2, tail, 256), scratch(slots, heads, 256), dma(2 + slots)],
    )(tab, own, near, *sends, passing[0])
    other = swapped(mine)
    share0, share1, decays = call(
        bind(share_part, slots),
        [shape((rows, width), F32), shape((HALF, width), F32), shape((2, heads, 256), F32)],
        [SMEM, VMEM, VMEM],
    )(tab, dts, params)
    token = call(touch_part, shape((8, 128), F32), [ANY], cost=40_000_000)(onward[0])
    upper = call(
        bind(early_part, slots), upper_rows, [SMEM, VMEM, VMEM, VMEM, ANY, ANY]
    )(tab, cache, mine, other, token, decays)
    uppers = {2 * m: far(upper, 2 * m) if m else upper for m in range(half)}
    late, second, *cars = call(
        bind(late_part, slots),
        [shape((width, state), BF16), packed(piece)] + [upper_rows] * peers,
        [SMEM] + [VMEM] * 5 + [HBM] + [ANY] * (peers + half - 2),
        [VMEM, VMEM] + [ANY] * peers,
        [
            scratch(piece, 256),
            scratch(piece, 256),
            scratch(HALF, width),
            scratch(HALF, width),
            scratch(rows, state),
            scratch(rows + HALF, state),
            dma(3 * count + 2),
        ],
    )(tab, cache, mine, other, share0, decays, x_rows, near, *sends, *onward)
    cars = {0: cars[0]} | {k: far(cars[k], k) for k in list(range(2, peers)) + [1]}
    uppers |= {2 * m + 1: far(uppers[2 * m], 1) for m in range(half)}
    final = call(
        bind(final_part, slots),
        shape((width, state), BF16),
        [SMEM] + [VMEM] * 6,
        scratch=[scratch(HALF, state)],
    )(tab, mine, other, share1, decays, late, second)
    gated, squares = call(
        bind(gate_part),
        [shape(x_rows.shape, F32), shape((slots, rows), F32)],
        [SMEM, VMEM, VMEM] + [ANY] * (2 * peers),
        scratch=[scratch(slots, rows, width), dma(slots, 2)],
    )(
        tab,
        yz,
        ez,
        *[cars[k] for k in range(peers)],
        *[uppers[k] for k in range(peers)],
    )
    mixed_rows = call(bind(norm_part), shape(x_rows.shape, BF16), [SMEM] + [VMEM] * 5)(
        tab, gated, squares, swapped(squares), norm_gain[None], lens
    )
    return (mixed_rows, final.reshape(cache_state.shape))


def solution(mesh):
    in_specs = (
        P(("group", "sess", "dp"), None, "head"),
        P(("group", "sess", "dp"), None, "head"),
        P(("group", "sess", "dp"), None, None),
        P(("group", "sess", "dp"), None, None),
        P(("group", "sess", "dp"), "head", None),
        P("head"),
        P("head"),
        P("head"),
        P("head"),
        P(("group", "sess", "dp"), "head", None, None),
        P(("group", "sess", "dp")),
        P("group", None),
        P("group", None),
    )
    out_specs = (
        P(("group", "sess", "dp"), None, "head"),
        P(("group", "sess", "dp"), "head", None, None),
    )
    return jax.shard_map(
        per_device, mesh=mesh, in_specs=in_specs, out_specs=out_specs, check_vma=False
    )
```

```python
import functools

import jax
import jax.numpy as jnp
from jax import lax
from jax.experimental import pallas as pl
from jax.experimental.pallas import tpu as pltpu
from jax.sharding import PartitionSpec as P

F32 = jnp.float32
BF16 = jnp.bfloat16
HALF = 64
VMEM = pl.BlockSpec(memory_space=pltpu.VMEM)
SMEM = pl.BlockSpec(memory_space=pltpu.SMEM)
HBM = pl.BlockSpec(memory_space=pltpu.HBM)
ANY = pl.BlockSpec(memory_space=pl.ANY)


def dot(a, b, dims, precision=None):
    return lax.dot_general(
        a, b, ((dims[:1], dims[1:]), ((), ())), precision=precision, preferred_element_type=F32
    )


def iota(shape, dim):
    return lax.broadcasted_iota(jnp.int32, shape, dim)


def softplus(v):
    return jnp.maximum(v, 0.0) + jnp.log1p(jnp.exp(-jnp.abs(v)))


def running(v):
    rows = v.shape[1]
    upto = jnp.where(iota((rows, rows), 0) <= iota((rows, rows), 1), 1.0, 0.0).astype(F32)
    return dot(v, upto, (1, 0), lax.Precision.HIGHEST)


def silu(v):
    return v * (1.0 / (1.0 + jnp.exp(-v)))


def columns(params):
    heads = params.shape[1]
    eye = iota((heads, heads), 0) == iota((heads, heads), 1)
    return [
        jnp.sum(jnp.where(eye, params[i : i + 1], 0.0), axis=1, keepdims=True)
        for i in range(params.shape[0])
    ]


class Table:
    def __init__(self, tab, peers, slots):
        self.peers, self.slots = peers, slots
        self.me, self.odd, self.length = tab[0], tab[1], tab[2]
        count = peers * slots
        self.owner = lambda i: tab[3 + i]
        self.late = lambda i: tab[3 + count + i] % 2

    def far(self, j):
        return self.me ^ self.owner(self.me * self.slots + j)

    def slot(self, k):
        pick = jnp.int32(0)
        for j in range(1, self.slots):
            pick = jnp.where(self.far(j) == k, j, pick)
        return pick

    def holder(self, k, part):
        found = jnp.int32(0)
        for i in range(self.peers * self.slots):
            hit = (self.owner(i) == self.me ^ k) & (self.late(i) == part)
            found = jnp.where(hit, self.me ^ (i // self.slots), found)
        return found


class Copies:
    def __init__(self, sem):
        self.sem, self.count, self.started = sem, 0, []

    def __call__(self, src, dst, pred=None, again=False):
        self.count += not again
        copy = pltpu.make_async_copy(src, dst, self.sem.at[self.count - 1])
        if pred is None:
            copy.start()
        else:
            pl.when(pred)(copy.start)
        self.started.append((pred, copy))

    def wait(self):
        for pred, copy in self.started:
            if pred is None:
                copy.wait()
            else:
                pl.when(pred)(copy.wait)
        self.started = []


def gather(sem, dst, choices):
    for pred, pairs in choices:

        @pl.when(pred)
        def _():
            for src, part in pairs:
                pltpu.make_async_copy(src, part, sem).start()

    return pltpu.make_async_copy(dst, dst, sem).wait


def spans(width):
    return [slice(g * 256, (g + 1) * 256) for g in range(width // 256)]


def chunk(ref, index, width):
    size = width // 256 * HALF
    return ref.at[pl.ds(index * size, size)]


def from_rows(x, j, start, out):
    return [
        (x.at[j, pl.ds(start, HALF), lanes], out.at[pl.ds(g * HALF, HALF)])
        for g, lanes in enumerate(spans(x.shape[2]))
    ]


def tail_of(ref, size, start=0, count=None):
    return ref.at[pl.ds(ref.shape[0] - size + start, size if count is None else count)]


def send_part(peers, x_in, b, c, dt, owner, lens, own, near, *rest):
    smalls = (own, near, *rest[: peers - 2])
    outs = (own, near, *rest[peers - 2 : 2 * peers - 4])
    dtv, x, bc, table, length, sem = rest[2 * peers - 4 :]
    slots, rows, width = x.shape
    heads = dt.shape[1]
    dp = lax.axis_index("dp")
    odd = lax.axis_index("head") % 2
    copies = Copies(sem)
    copies(owner, table)
    copies(lens, length)
    copies(dt, dtv)
    copies(x_in, x)
    copies(b, bc, odd == 0)
    copies(c, bc, odd != 0, again=True)
    copies.wait()
    t = Table([lax.axis_index("sess"), odd, length[0]], peers, slots)
    t.owner = lambda i: table[dp, i]
    count = jnp.full((heads, rows), t.length.astype(F32)).astype(BF16)
    picks = [t.slot(k) for k in range(peers)]

    def put(out, index, j, start):
        for g, lanes in enumerate(spans(width)):
            at = (index * (width // 256) + g) * HALF
            out[at : at + HALF] = x[j, start : start + HALF, lanes]

    for k in list(range(2, peers)) + [1, 0]:
        out, j = smalls[k], picks[k]
        at = out.shape[0] - rows - 2 * heads
        out[at : at + rows] = bc[j]
        value = dtv[j]
        high = value.astype(BF16)
        value = value - high.astype(F32)
        middle = value.astype(BF16)
        low = (value - middle.astype(F32)).astype(BF16)
        out[at + rows : at + rows + heads] = jnp.concatenate([high, middle], axis=1)
        out[at + rows + heads :] = jnp.concatenate([low, count], axis=1)
        if k:
            put(outs[k], 0, j, 0)
    for m in range(peers // 2):
        put(near, m + 1, picks[1 ^ 2 * m], HALF)


def forward_part(peers, slots, tab, x, near, after, *rest):
    outs, sem = rest[:-1], rest[-1]
    rows, width = x.shape[1:]
    t = Table(tab, peers, slots)
    for m in range(1, peers // 2):
        out, at = outs[m - 1], t.holder(2 * m, 0)
        wait = gather(
            sem.at[m - 1],
            out,
            [
                (at == 0, from_rows(x, t.slot(2 * m), HALF, out)),
                (at == 1, [(chunk(near, m + 1, width), out)]),
            ],
        )
        pl.when(at < 2)(wait)


def pick_part(peers, slots, heads, tab, *rest):
    got = rest[:peers]
    mine, dts, lens, tails, counts, sem = rest[peers + 1 :]
    rows = mine.shape[0] - HALF
    size = rows + 2 * heads
    t = Table(tab, peers, slots)
    waits = []
    for part in range(2):
        at, out = t.holder(0, part), tails.at[part]
        choices = [(at == k, [(tail_of(got[k], size), out)]) for k in range(peers)]
        waits.append(gather(sem.at[part], out, choices))
    for j in range(slots):
        at, out = t.far(j), counts.at[j]
        choices = [
            (at == k, [(tail_of(got[k], size, rows + heads, heads), out)]) for k in range(peers)
        ]
        waits.append(gather(sem.at[2 + j], out, choices))
    for wait in waits:
        wait()
    mine[:rows] = tails[0, :rows]
    mine[rows:] = tails[1, :HALF]
    for part in range(2):
        first = tails[part, rows : rows + heads].astype(F32)
        second = tails[part, rows + heads :].astype(F32)
        dts[part] = first[:, :rows] + (first[:, rows:] + second[:, :rows])
    for j in range(slots):
        lens[j] = counts[j, :, rows:].astype(F32)


def touch_part(*refs):
    out = refs[-1]
    out[...] = jnp.zeros(out.shape, out.dtype)


def share_part(peers, slots, tab, dts, params, share0, share1, decays):
    parts, heads, rows = dts.shape
    width = share0.shape[1]
    size = width // heads
    per = 128 // size
    length = Table(tab, peers, slots).length
    alog, bias, _ = columns(params)
    rate = -jnp.exp(alog)
    col = iota((heads, rows), 1)
    lane = iota((rows, 128), 1) // size
    for part, out in ((0, share0), (1, share1)):
        step = jnp.where(col < length - part * rows, softplus(dts[part] + bias), 0.0)
        log_decay = running(rate * step)
        total = log_decay[:, rows - 1 :]
        share = jnp.transpose(jnp.exp(total - log_decay) * step)
        decays[part] = jnp.broadcast_to(jnp.exp(total).astype(BF16).astype(F32), (heads, 256))
        for p in range(width // 128):
            factor = jnp.broadcast_to(share[:, p * per : p * per + 1], (rows, 128))
            for q in range(1, per):
                factor = jnp.where(lane == q, share[:, p * per + q : p * per + q + 1], factor)
            out[:, p * 128 : (p + 1) * 128] = factor[: out.shape[0]]


def block_part(x_in, z_in, b_in, c_in, dt_in, params, yz, ez, x, z, b, c, dt, sem):
    slots, rows, width = x.shape
    heads = dt.shape[1]
    size = width // heads
    per = 128 // size
    waits = []
    for s in range(slots):
        copies = Copies(sem.at[s])
        for src, dst in ((dt_in, dt), (b_in, b), (c_in, c), (x_in, x), (z_in, z)):
            copies(src.at[s], dst.at[s])
        waits.append(copies)
    causal = iota((rows, rows), 0) >= iota((rows, rows), 1)
    lane = iota((rows, 128), 1) // size
    alog, bias, skip = columns(params)
    rate = -jnp.exp(alog)
    for s in range(slots):
        waits[s].wait()
        step = softplus(dt[s] + bias)
        log_decay = running(rate * step)
        log_col = jnp.transpose(log_decay)
        decay_col = jnp.exp(log_col)
        scores = jnp.where(causal, dot(c[s], b[s], (1, 1)), 0.0)
        for p in range(width // 128):
            lanes = slice(p * 128, (p + 1) * 128)
            xp = x[s, :, lanes]
            weights = []
            parts = []
            decay = decay_col[:, p * per : p * per + 1]
            own_skip = skip[p * per : p * per + 1]
            for q in range(per):
                h = p * per + q
                gap = jnp.minimum(log_col[:, h : h + 1] - log_decay[h : h + 1], 0.0)
                weights.append((jnp.exp(gap) * step[h : h + 1] * scores).astype(BF16))
                parts.append(jnp.where(lane == q, xp, jnp.zeros_like(xp)))
                if q:
                    decay = jnp.where(lane == q, decay_col[:, h : h + 1], decay)
                    own_skip = jnp.where(lane[:1] == q, skip[h : h + 1], own_skip)
            inner = dot(jnp.concatenate(weights, axis=1), jnp.concatenate(parts, axis=0), (1, 0))
            gate = silu(z[s, :, lanes].astype(F32))
            yz[s, :, lanes] = (inner + own_skip * xp.astype(F32)) * gate
            ez[s, :, lanes] = decay * gate


def early_part(peers, slots, tab, cache, mine, other, token, decays, upper):
    def work(cs):
        for lanes in spans(cache.shape[0]):
            upper[:, lanes] = dot(cs[HALF : 2 * HALF], cache[lanes], (1, 1)).astype(BF16)

    odd = Table(tab, peers, slots).odd
    pl.when(odd == 0)(lambda: work(other))
    pl.when(odd != 0)(lambda: work(mine))


def late_part(peers, slots, tab, cache, mine, other, share, decays, x, near, *rest):
    half = peers // 2
    far, onward = rest[: peers - 2], rest[peers - 2 : peers - 3 + half]
    rest = rest[peers - 3 + half :]
    late, second, cars = rest[0], rest[1], rest[2 : peers + 2]
    low, high, car0, car1, bs, cs, sem = rest[peers + 2 :]
    rows, width = share.shape
    heads = decays.shape[1]
    size = width // heads
    t = Table(tab, peers, slots)
    k0, k1, j = t.holder(0, 0), t.holder(0, 1), t.slot(0)
    upper = (
        [(k0 == 0, from_rows(x, j, HALF, high)), (k0 == 1, [(chunk(near, 1, width), high)])]
        + [(k0 // 2 == m, [(onward[m - 1], high)]) for m in range(1, half)]
    )
    straight = [near] + list(far)

    def lower(at, out):
        return [(at == 0, from_rows(x, j, 0, out))] + [
            (at == k, [(chunk(straight[k - 1], 0, width), out)]) for k in range(1, peers)
        ]

    got_high = gather(sem.at[0], high, upper)
    got_low = gather(sem.at[1], low, lower(k0, low))
    got_second = gather(sem.at[2], second, lower(k1, second))

    @pl.when(t.odd == 0)
    def _():
        bs[...] = mine[:rows]
        cs[...] = other[...]

    @pl.when(t.odd != 0)
    def _():
        bs[...] = other[:rows]
        cs[...] = mine[...]

    for lanes in spans(width):
        car0[:, lanes] = dot(cs[:HALF], cache[lanes], (1, 1)).astype(BF16)
    got_low()
    got_high()
    for g, lanes in enumerate(spans(width)):
        at = slice(g * HALF, (g + 1) * HALF)
        xv = jnp.concatenate([low[at], high[at]], axis=0).astype(F32)
        local = dot((xv * share[:, lanes]).astype(BF16), bs[...], (0, 0)).astype(BF16).astype(F32)
        for q in range(256 // size):
            h = g * (256 // size) + q
            state = slice(h * size, (h + 1) * size)
            late[state] = (
                decays[0, h : h + 1] * cache[state].astype(F32)
                + local[q * size : (q + 1) * size]
            ).astype(BF16)
        car1[:, lanes] = dot(cs[rows:], late[lanes], (1, 1)).astype(BF16)
    got_second()
    waits = []
    for flag, at, src in ((0, k0, car0), (1, k1, car1)):
        choices = [(at == k, [(src, cars[k])]) for k in range(peers)]
        gather(sem.at[flag], src, choices)
        waits.append(pltpu.make_async_copy(src, cars[0], sem.at[flag]).wait)
    for wait in waits:
        wait()


def final_part(peers, slots, tab, mine, other, share, decays, late, second, final, bs):
    width = share.shape[1]
    heads = decays.shape[1]
    size = width // heads
    rows = mine.shape[0] - HALF
    odd = Table(tab, peers, slots).odd

    @pl.when(odd == 0)
    def _():
        bs[...] = mine[rows:]

    @pl.when(odd != 0)
    def _():
        bs[...] = other[rows:]

    for g, lanes in enumerate(spans(width)):
        xv = second[g * HALF : (g + 1) * HALF].astype(F32)
        local = dot((xv * share[:, lanes]).astype(BF16), bs[...], (0, 0)).astype(BF16).astype(F32)
        for q in range(256 // size):
            h = g * (256 // size) + q
            state = slice(h * size, (h + 1) * size)
            final[state] = (
                decays[1, h : h + 1] * late[state].astype(F32)
                + local[q * size : (q + 1) * size]
            ).astype(BF16)


def gate_part(peers, tab, yz, ez, *rest):
    cars, uppers = rest[:peers], rest[peers : 2 * peers]
    gated, squares, got, sem = rest[2 * peers :]
    slots, rows, width = yz.shape
    t = Table(tab, peers, slots)
    waits = []
    for j in range(slots):
        early = t.late(t.me * slots + j) == 0
        low, high = got.at[j, pl.ds(0, HALF)], got.at[j, pl.ds(HALF, HALF)]
        at = t.far(j)
        first = gather(sem.at[j, 0], low, [(at == k, [(cars[k], low)]) for k in range(peers)])
        second = gather(
            sem.at[j, 1],
            high,
            [((at == k) & early, [(uppers[k], high)]) for k in range(peers)],
        )
        waits.append((early, first, second))
    for j, (early, first, second) in enumerate(waits):
        first()
        pl.when(early)(second)
        total = jnp.zeros((rows, 128), F32)
        for p in range(width // 128):
            lanes = slice(p * 128, (p + 1) * 128)
            value = yz[j, :, lanes] + ez[j, :, lanes] * got[j, :, lanes].astype(F32)
            gated[j, :, lanes] = value
            total = total + value * value
        squares[j : j + 1] = jnp.sum(jnp.transpose(total), axis=0, keepdims=True)


def norm_part(peers, tab, gated, own, other, gain, lens, mixed, out, sem):
    slots, rows, width = gated.shape
    t = Table(tab, peers, slots)
    row = iota((rows, 128), 0).astype(F32)
    copies = Copies(sem)
    for j in range(slots):
        late = t.late(t.me * slots + j)
        live = row + (late * rows).astype(F32) < lens[j][:1]
        mean = (own[j : j + 1] + other[j : j + 1]) / (2.0 * width)
        inverse = jnp.transpose(jnp.broadcast_to(lax.rsqrt(mean + 1e-05), (rows, rows)))
        for p in range(width // 128):
            lanes = slice(p * 128, (p + 1) * 128)
            value = gated[j, :, lanes] * inverse * gain[:, lanes].astype(F32)
            out[j, :, lanes] = jnp.where(live, value, 0.0).astype(BF16)
        copies(out.at[j], mixed.at[j])
    copies.wait()


def call(kernel, outs, in_specs, out_specs=None, scratch=(), limit=24, cost=0):
    return pl.pallas_call(
        kernel,
        out_shape=outs,
        in_specs=in_specs,
        out_specs=out_specs if out_specs is not None else jax.tree.map(lambda _: VMEM, outs),
        scratch_shapes=scratch,
        compiler_params=pltpu.CompilerParams(vmem_limit_bytes=limit * 1024 * 1024),
        cost_estimate=pl.CostEstimate(flops=0, bytes_accessed=cost, transcendentals=0),
    )


def per_device(
    x_rows,
    z_rows,
    input_projection_matrix,
    c_rows,
    dt_raw,
    a_log,
    dt_bias,
    d_skip,
    norm_gain,
    cache_state,
    lengths,
    slot_owner,
    slot_task,
):
    slots, rows, width = x_rows.shape
    heads = dt_raw.shape[1]
    state = cache_state.shape[3]
    peers = lax.axis_size("sess")
    half = peers // 2
    head = lax.axis_index("head")
    groups = input_projection_matrix.shape[2] // state
    if groups > 1:
        at = head // 2 * state
        b = lax.dynamic_slice_in_dim(input_projection_matrix, at, state, 2)
        c = lax.dynamic_slice_in_dim(c_rows, at, state, 2)
    else:
        b, c = input_projection_matrix, c_rows

    def own_row(table):
        mine = iota(table.shape, 0) == lax.axis_index("dp")
        return jnp.sum(jnp.where(mine, table, 0), axis=0)

    ids = jnp.stack([lax.axis_index("sess"), head % 2]).astype(jnp.int32)
    tab = jnp.concatenate([ids, lengths, own_row(slot_owner), own_row(slot_task)])
    params = jnp.stack([a_log, dt_bias, d_skip])
    cache = cache_state.reshape(width, state)

    def far(value, k):
        return lax.ppermute(value, "sess", [(i, i ^ k) for i in range(peers)])

    def swapped(value):
        count = lax.axis_size("head")
        return lax.ppermute(value, "head", [(i, i ^ 1) for i in range(count)])

    def scratch(*sizes, dtype=BF16):
        return pltpu.VMEM(sizes, dtype)

    shape = jax.ShapeDtypeStruct
    dma = lambda *sizes: pltpu.SemaphoreType.DMA(sizes)
    bind = lambda kernel, *more: functools.partial(kernel, peers, *more)
    count = width // 256
    piece = count * HALF
    tail = rows + 2 * heads
    packed = lambda size: shape((size, 256), BF16)
    upper_rows = shape((HALF, width), BF16)
    own, near, *rest = call(
        bind(send_part),
        [packed(tail), packed((1 + half) * piece + tail)]
        + [packed(tail)] * (peers - 2)
        + [packed(piece)] * (peers - 2),
        [HBM] * 6,
        scratch=[
            scratch(*dt_raw.shape, dtype=F32),
            scratch(*x_rows.shape),
            scratch(*b.shape),
            pltpu.SMEM(slot_owner.shape, jnp.int32),
            pltpu.SMEM(lengths.shape, jnp.int32),
            dma(5),
        ],
        limit=60,
    )(x_rows, b, c, dt_raw, slot_owner, lengths)
    near = far(near, 1)
    smalls = [far(value, k + 2) for k, value in enumerate(rest[: peers - 2])]
    sends = [far(value, k + 2) for k, value in enumerate(rest[peers - 2 :])]
    yz, ez = call(
        block_part,
        [shape(x_rows.shape, F32)] * 2,
        [HBM] * 5 + [VMEM],
        scratch=[
            scratch(*x_rows.shape),
            scratch(*x_rows.shape),
            scratch(*b.shape),
            scratch(*b.shape),
            scratch(*dt_raw.shape, dtype=F32),
            dma(slots, 5),
        ],
    )(x_rows, z_rows, b, c, dt_raw, params)
    passing = call(
        bind(forward_part, slots),
        [packed(piece)] * (half - 1),
        [SMEM, HBM, ANY, ANY],
        [ANY] * (half - 1),
        [dma(half - 1)],
    )(tab, x_rows, near, ez)
    onward = [far(value, 2 * (m + 1)) for m, value in enumerate(passing)]
    mine, dts, lens = call(
        bind(pick_part, slots, heads),
        [
            shape((rows + HALF, state), BF16),
            shape((2, heads, rows), F32),
            shape((slots, heads, rows), F32),
        ],
        [SMEM] + [ANY] * (peers + 1),
        scratch=[scratch(2, tail, 256), scratch(slots, heads, 256), dma(2 + slots)],
    )(tab, own, near, *smalls, passing[0])
    other = swapped(mine)
    share0, share1, decays = call(
        bind(share_part, slots),
        [shape((rows, width), F32), shape((HALF, width), F32), shape((2, heads, 256), F32)],
        [SMEM, VMEM, VMEM],
    )(tab, dts, params)
    token = call(touch_part, shape((8, 128), F32), [ANY] * (peers - 2), cost=40_000_000)(*sends)
    upper = call(
        bind(early_part, slots), upper_rows, [SMEM, VMEM, VMEM, VMEM, ANY, ANY]
    )(tab, cache, mine, other, token, decays)
    uppers = {2 * m: far(upper, 2 * m) if m else upper for m in range(half)}
    late, second, *cars = call(
        bind(late_part, slots),
        [shape((width, state), BF16), packed(piece)] + [upper_rows] * peers,
        [SMEM] + [VMEM] * 5 + [HBM] + [ANY] * (peers + half - 2),
        [VMEM, VMEM] + [ANY] * peers,
        [
            scratch(piece, 256),
            scratch(piece, 256),
            scratch(HALF, width),
            scratch(HALF, width),
            scratch(rows, state),
            scratch(rows + HALF, state),
            dma(3),
        ],
    )(tab, cache, mine, other, share0, decays, x_rows, near, *sends, *onward)
    cars = {0: cars[0]} | {k: far(cars[k], k) for k in list(range(2, peers)) + [1]}
    uppers |= {2 * m + 1: far(uppers[2 * m], 1) for m in range(half)}
    final = call(
        bind(final_part, slots),
        shape((width, state), BF16),
        [SMEM] + [VMEM] * 6,
        scratch=[scratch(HALF, state)],
    )(tab, mine, other, share1, decays, late, second)
    gated, squares = call(
        bind(gate_part),
        [shape(x_rows.shape, F32), shape((slots, rows), F32)],
        [SMEM, VMEM, VMEM] + [ANY] * (2 * peers),
        scratch=[scratch(slots, rows, width), dma(slots, 2)],
    )(
        tab,
        yz,
        ez,
        *[cars[k] for k in range(peers)],
        *[uppers[k] for k in range(peers)],
    )
    mixed_rows = call(bind(norm_part), shape(x_rows.shape, BF16), [SMEM] + [VMEM] * 5, ANY, [scratch(*x_rows.shape), dma(slots)])(
        tab, gated, squares, swapped(squares), norm_gain[None], lens
    )
    return (mixed_rows, final.reshape(cache_state.shape))


def solution(mesh):
    in_specs = (
        P(("group", "sess", "dp"), None, "head"),
        P(("group", "sess", "dp"), None, "head"),
        P(("group", "sess", "dp"), None, None),
        P(("group", "sess", "dp"), None, None),
        P(("group", "sess", "dp"), "head", None),
        P("head"),
        P("head"),
        P("head"),
        P("head"),
        P(("group", "sess", "dp"), "head", None, None),
        P(("group", "sess", "dp")),
        P("group", None),
        P("group", None),
    )
    out_specs = (
        P(("group", "sess", "dp"), None, "head"),
        P(("group", "sess", "dp"), "head", None, None),
    )
    return jax.shard_map(
        per_device, mesh=mesh, in_specs=in_specs, out_specs=out_specs, check_vma=False
    )
```

```python
import functools

import jax
import jax.numpy as jnp
from jax import lax
from jax.experimental import pallas as pl
from jax.experimental.pallas import tpu as pltpu
from jax.sharding import PartitionSpec as P

F32 = jnp.float32
BF16 = jnp.bfloat16
HALF = 64
VMEM = pl.BlockSpec(memory_space=pltpu.VMEM)
SMEM = pl.BlockSpec(memory_space=pltpu.SMEM)
HBM = pl.BlockSpec(memory_space=pltpu.HBM)
ANY = pl.BlockSpec(memory_space=pl.ANY)


def dot(a, b, dims, precision=None):
    return lax.dot_general(
        a, b, ((dims[:1], dims[1:]), ((), ())), precision=precision, preferred_element_type=F32
    )


def iota(shape, dim):
    return lax.broadcasted_iota(jnp.int32, shape, dim)


def softplus(v):
    return jnp.maximum(v, 0.0) + jnp.log1p(jnp.exp(-jnp.abs(v)))


def running(v):
    rows = v.shape[1]
    upto = jnp.where(iota((rows, rows), 0) <= iota((rows, rows), 1), 1.0, 0.0).astype(F32)
    return dot(v, upto, (1, 0), lax.Precision.HIGHEST)


def silu(v):
    return v * (1.0 / (1.0 + jnp.exp(-v)))


def columns(params):
    heads = params.shape[1]
    eye = iota((heads, heads), 0) == iota((heads, heads), 1)
    return [
        jnp.sum(jnp.where(eye, params[i : i + 1], 0.0), axis=1, keepdims=True)
        for i in range(params.shape[0])
    ]


class Table:
    def __init__(self, tab, peers, slots):
        self.peers, self.slots = peers, slots
        self.me, self.odd, self.length = tab[0], tab[1], tab[2]
        count = peers * slots
        self.owner = lambda i: tab[3 + i]
        self.late = lambda i: tab[3 + count + i] % 2

    def far(self, j):
        return self.me ^ self.owner(self.me * self.slots + j)

    def slot(self, k):
        pick = jnp.int32(0)
        for j in range(1, self.slots):
            pick = jnp.where(self.far(j) == k, j, pick)
        return pick

    def holder(self, k, part):
        found = jnp.int32(0)
        for i in range(self.peers * self.slots):
            hit = (self.owner(i) == self.me ^ k) & (self.late(i) == part)
            found = jnp.where(hit, self.me ^ (i // self.slots), found)
        return found


class Copies:
    def __init__(self, sem):
        self.sem, self.count, self.started = sem, 0, []

    def __call__(self, src, dst, pred=None, again=False):
        self.count += not again
        copy = pltpu.make_async_copy(src, dst, self.sem.at[self.count - 1])
        if pred is None:
            copy.start()
        else:
            pl.when(pred)(copy.start)
        self.started.append((pred, copy))

    def wait(self):
        for pred, copy in self.started:
            if pred is None:
                copy.wait()
            else:
                pl.when(pred)(copy.wait)
        self.started = []


def gather(sem, dst, choices):
    for pred, pairs in choices:

        @pl.when(pred)
        def _():
            for src, part in pairs:
                pltpu.make_async_copy(src, part, sem).start()

    return pltpu.make_async_copy(dst, dst, sem).wait


def spans(width):
    return [slice(g * 256, (g + 1) * 256) for g in range(width // 256)]


def chunk(ref, index, width):
    size = width // 256 * HALF
    return ref.at[pl.ds(index * size, size)]


def from_rows(x, j, start, out):
    return [
        (x.at[j, pl.ds(start, HALF), lanes], out.at[pl.ds(g * HALF, HALF)])
        for g, lanes in enumerate(spans(x.shape[2]))
    ]


def tail_of(ref, size, start=0, count=None):
    return ref.at[pl.ds(ref.shape[0] - size + start, size if count is None else count)]


def send_part(peers, x_in, b, c, dt, owner, lens, own, near, *rest):
    smalls = (own, near, *rest[: peers - 2])
    outs = (own, near, *rest[peers - 2 : 2 * peers - 4])
    dtv, x, bc, table, length, sem = rest[2 * peers - 4 :]
    slots, rows, width = x.shape
    heads = dt.shape[1]
    dp = lax.axis_index("dp")
    odd = lax.axis_index("head") % 2
    copies = Copies(sem)
    copies(owner, table)
    copies(lens, length)
    copies(dt, dtv)
    copies(x_in, x)
    copies(b, bc, odd == 0)
    copies(c, bc, odd != 0, again=True)
    copies.wait()
    t = Table([lax.axis_index("sess"), odd, length[0]], peers, slots)
    t.owner = lambda i: table[dp, i]
    count = jnp.full((heads, rows), t.length.astype(F32)).astype(BF16)
    picks = [t.slot(k) for k in range(peers)]

    def put(out, index, j, start):
        for g, lanes in enumerate(spans(width)):
            at = (index * (width // 256) + g) * HALF
            out[at : at + HALF] = x[j, start : start + HALF, lanes]

    for k in list(range(2, peers)) + [1, 0]:
        out, j = smalls[k], picks[k]
        at = out.shape[0] - rows - 2 * heads
        out[at : at + rows] = bc[j]
        value = dtv[j]
        high = value.astype(BF16)
        value = value - high.astype(F32)
        middle = value.astype(BF16)
        low = (value - middle.astype(F32)).astype(BF16)
        out[at + rows : at + rows + heads] = jnp.concatenate([high, middle], axis=1)
        out[at + rows + heads :] = jnp.concatenate([low, count], axis=1)
        if k:
            put(outs[k], 0, j, 0)
    for m in range(peers // 2):
        put(near, m + 1, picks[1 ^ 2 * m], HALF)


def forward_part(peers, slots, tab, x, near, after, *rest):
    outs, sem = rest[:-1], rest[-1]
    rows, width = x.shape[1:]
    t = Table(tab, peers, slots)
    for m in range(1, peers // 2):
        out, at = outs[m - 1], t.holder(2 * m, 0)
        wait = gather(
            sem.at[m - 1],
            out,
            [
                (at == 0, from_rows(x, t.slot(2 * m), HALF, out)),
                (at == 1, [(chunk(near, m + 1, width), out)]),
            ],
        )
        pl.when(at < 2)(wait)


def pick_part(peers, slots, heads, tab, *rest):
    got = rest[:peers]
    mine, dts, lens, tails, counts, sem = rest[peers + 1 :]
    rows = mine.shape[0] - HALF
    size = rows + 2 * heads
    t = Table(tab, peers, slots)
    waits = []
    for part in range(2):
        at, out = t.holder(0, part), tails.at[part]
        choices = [(at == k, [(tail_of(got[k], size), out)]) for k in range(peers)]
        waits.append(gather(sem.at[part], out, choices))
    for j in range(slots):
        at, out = t.far(j), counts.at[j]
        choices = [
            (at == k, [(tail_of(got[k], size, rows + heads, heads), out)]) for k in range(peers)
        ]
        waits.append(gather(sem.at[2 + j], out, choices))
    for wait in waits:
        wait()
    mine[:rows] = tails[0, :rows]
    mine[rows:] = tails[1, :HALF]
    for part in range(2):
        first = tails[part, rows : rows + heads].astype(F32)
        second = tails[part, rows + heads :].astype(F32)
        dts[part] = first[:, :rows] + (first[:, rows:] + second[:, :rows])
    for j in range(slots):
        lens[j] = counts[j, :, rows:].astype(F32)


def touch_part(*refs):
    out = refs[-1]
    out[...] = jnp.zeros(out.shape, out.dtype)


def share_part(peers, slots, tab, dts, params, share0, share1, decays):
    parts, heads, rows = dts.shape
    width = share0.shape[1]
    size = width // heads
    per = 128 // size
    length = Table(tab, peers, slots).length
    alog, bias, _ = columns(params)
    rate = -jnp.exp(alog)
    col = iota((heads, rows), 1)
    lane = iota((rows, 128), 1) // size
    for part, out in ((0, share0), (1, share1)):
        step = jnp.where(col < length - part * rows, softplus(dts[part] + bias), 0.0)
        log_decay = running(rate * step)
        total = log_decay[:, rows - 1 :]
        share = jnp.transpose(jnp.exp(total - log_decay) * step)
        decays[part] = jnp.broadcast_to(jnp.exp(total).astype(BF16).astype(F32), (heads, 256))
        for p in range(width // 128):
            factor = jnp.broadcast_to(share[:, p * per : p * per + 1], (rows, 128))
            for q in range(1, per):
                factor = jnp.where(lane == q, share[:, p * per + q : p * per + q + 1], factor)
            out[:, p * 128 : (p + 1) * 128] = factor[: out.shape[0]]


def block_part(x_in, z_in, b_in, c_in, dt_in, params, yz, ez, x, z, b, c, dt, sem):
    slots, rows, width = x.shape
    heads = dt.shape[1]
    size = width // heads
    per = 128 // size
    waits = []
    for s in range(slots):
        copies = Copies(sem.at[s])
        for src, dst in ((dt_in, dt), (b_in, b), (c_in, c), (x_in, x), (z_in, z)):
            copies(src.at[s], dst.at[s])
        waits.append(copies)
    causal = iota((rows, rows), 0) >= iota((rows, rows), 1)
    lane = iota((rows, 128), 1) // size
    alog, bias, skip = columns(params)
    rate = -jnp.exp(alog)
    for s in range(slots):
        waits[s].wait()
        step = softplus(dt[s] + bias)
        log_decay = running(rate * step)
        log_col = jnp.transpose(log_decay)
        decay_col = jnp.exp(log_col)
        scores = jnp.where(causal, dot(c[s], b[s], (1, 1)), 0.0)
        for p in range(width // 128):
            lanes = slice(p * 128, (p + 1) * 128)
            xp = x[s, :, lanes]
            weights = []
            parts = []
            decay = decay_col[:, p * per : p * per + 1]
            own_skip = skip[p * per : p * per + 1]
            for q in range(per):
                h = p * per + q
                gap = jnp.minimum(log_col[:, h : h + 1] - log_decay[h : h + 1], 0.0)
                weights.append((jnp.exp(gap) * step[h : h + 1] * scores).astype(BF16))
                parts.append(jnp.where(lane == q, xp, jnp.zeros_like(xp)))
                if q:
                    decay = jnp.where(lane == q, decay_col[:, h : h + 1], decay)
                    own_skip = jnp.where(lane[:1] == q, skip[h : h + 1], own_skip)
            inner = dot(jnp.concatenate(weights, axis=1), jnp.concatenate(parts, axis=0), (1, 0))
            gate = silu(z[s, :, lanes].astype(F32))
            yz[s, :, lanes] = (inner + own_skip * xp.astype(F32)) * gate
            ez[s, :, lanes] = decay * gate


def early_part(peers, slots, tab, cache, mine, other, token, upper):
    def work(cs):
        for lanes in spans(cache.shape[0]):
            upper[:, lanes] = dot(cs[HALF : 2 * HALF], cache[lanes], (1, 1)).astype(BF16)

    odd = Table(tab, peers, slots).odd
    pl.when(odd == 0)(lambda: work(other))
    pl.when(odd != 0)(lambda: work(mine))


def late_part(peers, slots, tab, cache, mine, other, share, decays, x, near, *rest):
    half = peers // 2
    far, onward = rest[: peers - 2], rest[peers - 2 : peers - 3 + half]
    rest = rest[peers - 3 + half :]
    late, second, cars = rest[0], rest[1], rest[2 : peers + 2]
    low, high, car0, car1, bs, cs, sem = rest[peers + 2 :]
    rows, width = share.shape
    heads = decays.shape[1]
    size = width // heads
    t = Table(tab, peers, slots)
    k0, k1, j = t.holder(0, 0), t.holder(0, 1), t.slot(0)
    upper = (
        [(k0 == 0, from_rows(x, j, HALF, high)), (k0 == 1, [(chunk(near, 1, width), high)])]
        + [(k0 // 2 == m, [(onward[m - 1], high)]) for m in range(1, half)]
    )
    straight = [near] + list(far)

    def lower(at, out):
        return [(at == 0, from_rows(x, j, 0, out))] + [
            (at == k, [(chunk(straight[k - 1], 0, width), out)]) for k in range(1, peers)
        ]

    got_high = gather(sem.at[0], high, upper)
    got_low = gather(sem.at[1], low, lower(k0, low))
    got_second = gather(sem.at[2], second, lower(k1, second))

    @pl.when(t.odd == 0)
    def _():
        bs[...] = mine[:rows]
        cs[...] = other[...]

    @pl.when(t.odd != 0)
    def _():
        bs[...] = other[:rows]
        cs[...] = mine[...]

    for lanes in spans(width):
        car0[:, lanes] = dot(cs[:HALF], cache[lanes], (1, 1)).astype(BF16)
    got_low()
    got_high()
    for g, lanes in enumerate(spans(width)):
        at = slice(g * HALF, (g + 1) * HALF)
        xv = jnp.concatenate([low[at], high[at]], axis=0).astype(F32)
        local = dot((xv * share[:, lanes]).astype(BF16), bs[...], (0, 0)).astype(BF16).astype(F32)
        for q in range(256 // size):
            h = g * (256 // size) + q
            state = slice(h * size, (h + 1) * size)
            late[state] = (
                decays[0, h : h + 1] * cache[state].astype(F32)
                + local[q * size : (q + 1) * size]
            ).astype(BF16)
        car1[:, lanes] = dot(cs[rows:], late[lanes], (1, 1)).astype(BF16)
    got_second()
    waits = []
    for flag, at, src in ((0, k0, car0), (1, k1, car1)):
        choices = [(at == k, [(src, cars[k])]) for k in range(peers)]
        gather(sem.at[flag], src, choices)
        waits.append(pltpu.make_async_copy(src, cars[0], sem.at[flag]).wait)
    for wait in waits:
        wait()


def final_part(peers, slots, tab, mine, other, share, decays, late, second, final, bs):
    width = share.shape[1]
    heads = decays.shape[1]
    size = width // heads
    rows = mine.shape[0] - HALF
    odd = Table(tab, peers, slots).odd

    @pl.when(odd == 0)
    def _():
        bs[...] = mine[rows:]

    @pl.when(odd != 0)
    def _():
        bs[...] = other[rows:]

    for g, lanes in enumerate(spans(width)):
        xv = second[g * HALF : (g + 1) * HALF].astype(F32)
        local = dot((xv * share[:, lanes]).astype(BF16), bs[...], (0, 0)).astype(BF16).astype(F32)
        for q in range(256 // size):
            h = g * (256 // size) + q
            state = slice(h * size, (h + 1) * size)
            final[state] = (
                decays[1, h : h + 1] * late[state].astype(F32)
                + local[q * size : (q + 1) * size]
            ).astype(BF16)


def gate_part(peers, tab, yz, ez, *rest):
    cars, uppers = rest[:peers], rest[peers : 2 * peers]
    gated, squares, got, sem = rest[2 * peers :]
    slots, rows, width = yz.shape
    t = Table(tab, peers, slots)
    waits = []
    for j in range(slots):
        early = t.late(t.me * slots + j) == 0
        low, high = got.at[j, pl.ds(0, HALF)], got.at[j, pl.ds(HALF, HALF)]
        at = t.far(j)
        first = gather(sem.at[j, 0], low, [(at == k, [(cars[k], low)]) for k in range(peers)])
        second = gather(
            sem.at[j, 1],
            high,
            [((at == k) & early, [(uppers[k], high)]) for k in range(peers)],
        )
        waits.append((early, first, second))
    for j, (early, first, second) in enumerate(waits):
        first()
        pl.when(early)(second)
        total = jnp.zeros((rows, 128), F32)
        for p in range(width // 128):
            lanes = slice(p * 128, (p + 1) * 128)
            value = yz[j, :, lanes] + ez[j, :, lanes] * got[j, :, lanes].astype(F32)
            gated[j, :, lanes] = value
            total = total + value * value
        squares[j : j + 1] = jnp.sum(jnp.transpose(total), axis=0, keepdims=True)


def norm_part(peers, tab, gated, own, other, gain, lens, mixed, out, sem):
    slots, rows, width = gated.shape
    t = Table(tab, peers, slots)
    row = iota((rows, 128), 0).astype(F32)
    copies = Copies(sem)
    for j in range(slots):
        late = t.late(t.me * slots + j)
        live = row + (late * rows).astype(F32) < lens[j][:1]
        mean = (own[j : j + 1] + other[j : j + 1]) / (2.0 * width)
        inverse = jnp.transpose(jnp.broadcast_to(lax.rsqrt(mean + 1e-05), (rows, rows)))
        for p in range(width // 128):
            lanes = slice(p * 128, (p + 1) * 128)
            value = gated[j, :, lanes] * inverse * gain[:, lanes].astype(F32)
            out[j, :, lanes] = jnp.where(live, value, 0.0).astype(BF16)
        copies(out.at[j], mixed.at[j])
    copies.wait()


def call(kernel, outs, in_specs, out_specs=None, scratch=(), limit=24, cost=0):
    return pl.pallas_call(
        kernel,
        out_shape=outs,
        in_specs=in_specs,
        out_specs=out_specs if out_specs is not None else jax.tree.map(lambda _: VMEM, outs),
        scratch_shapes=scratch,
        compiler_params=pltpu.CompilerParams(vmem_limit_bytes=limit * 1024 * 1024),
        cost_estimate=pl.CostEstimate(flops=0, bytes_accessed=cost, transcendentals=0),
    )


def per_device(
    x_rows,
    z_rows,
    input_projection_matrix,
    c_rows,
    dt_raw,
    a_log,
    dt_bias,
    d_skip,
    norm_gain,
    cache_state,
    lengths,
    slot_owner,
    slot_task,
):
    slots, rows, width = x_rows.shape
    heads = dt_raw.shape[1]
    state = cache_state.shape[3]
    peers = lax.axis_size("sess")
    half = peers // 2
    head = lax.axis_index("head")
    groups = input_projection_matrix.shape[2] // state
    if groups > 1:
        at = head // 2 * state
        b = lax.dynamic_slice_in_dim(input_projection_matrix, at, state, 2)
        c = lax.dynamic_slice_in_dim(c_rows, at, state, 2)
    else:
        b, c = input_projection_matrix, c_rows

    def own_row(table):
        mine = iota(table.shape, 0) == lax.axis_index("dp")
        return jnp.sum(jnp.where(mine, table, 0), axis=0)

    ids = jnp.stack([lax.axis_index("sess"), head % 2]).astype(jnp.int32)
    tab = jnp.concatenate([ids, lengths, own_row(slot_owner), own_row(slot_task)])
    params = jnp.stack([a_log, dt_bias, d_skip])
    cache = cache_state.reshape(width, state)

    def far(value, k):
        return lax.ppermute(value, "sess", [(i, i ^ k) for i in range(peers)])

    def swapped(value):
        count = lax.axis_size("head")
        return lax.ppermute(value, "head", [(i, i ^ 1) for i in range(count)])

    def scratch(*sizes, dtype=BF16):
        return pltpu.VMEM(sizes, dtype)

    shape = jax.ShapeDtypeStruct
    dma = lambda *sizes: pltpu.SemaphoreType.DMA(sizes)
    bind = lambda kernel, *more: functools.partial(kernel, peers, *more)
    count = width // 256
    piece = count * HALF
    tail = rows + 2 * heads
    packed = lambda size: shape((size, 256), BF16)
    upper_rows = shape((HALF, width), BF16)
    own, near, *rest = call(
        bind(send_part),
        [packed(tail), packed((1 + half) * piece + tail)]
        + [packed(tail)] * (peers - 2)
        + [packed(piece)] * (peers - 2),
        [HBM] * 6,
        scratch=[
            scratch(*dt_raw.shape, dtype=F32),
            scratch(*x_rows.shape),
            scratch(*b.shape),
            pltpu.SMEM(slot_owner.shape, jnp.int32),
            pltpu.SMEM(lengths.shape, jnp.int32),
            dma(5),
        ],
        limit=60,
    )(x_rows, b, c, dt_raw, slot_owner, lengths)
    near = far(near, 1)
    smalls = [far(value, k + 2) for k, value in enumerate(rest[: peers - 2])]
    sends = [far(value, k + 2) for k, value in enumerate(rest[peers - 2 :])]
    yz, ez = call(
        block_part,
        [shape(x_rows.shape, F32)] * 2,
        [HBM] * 5 + [VMEM],
        scratch=[
            scratch(*x_rows.shape),
            scratch(*x_rows.shape),
            scratch(*b.shape),
            scratch(*b.shape),
            scratch(*dt_raw.shape, dtype=F32),
            dma(slots, 5),
        ],
    )(x_rows, z_rows, b, c, dt_raw, params)
    passing = call(
        bind(forward_part, slots),
        [packed(piece)] * (half - 1),
        [SMEM, HBM, ANY, ANY],
        [ANY] * (half - 1),
        [dma(half - 1)],
    )(tab, x_rows, near, ez)
    onward = [far(value, 2 * (m + 1)) for m, value in enumerate(passing)]
    mine, dts, lens = call(
        bind(pick_part, slots, heads),
        [
            shape((rows + HALF, state), BF16),
            shape((2, heads, rows), F32),
            shape((slots, heads, rows), F32),
        ],
        [SMEM] + [ANY] * (peers + 1),
        scratch=[scratch(2, tail, 256), scratch(slots, heads, 256), dma(2 + slots)],
    )(tab, own, near, *smalls, passing[0])
    other = swapped(mine)
    share0, share1, decays = call(
        bind(share_part, slots),
        [shape((rows, width), F32), shape((HALF, width), F32), shape((2, heads, 256), F32)],
        [SMEM, VMEM, VMEM],
    )(tab, dts, params)
    token = call(touch_part, shape((8, 128), F32), [ANY] * (peers - 2), cost=40_000_000)(*sends)
    upper = call(
        bind(early_part, slots), upper_rows, [SMEM, VMEM, VMEM, VMEM, ANY]
    )(tab, cache, mine, other, token)
    uppers = {2 * m: far(upper, 2 * m) if m else upper for m in range(half)}
    late, second, *cars = call(
        bind(late_part, slots),
        [shape((width, state), BF16), packed(piece)] + [upper_rows] * peers,
        [SMEM] + [VMEM] * 5 + [HBM] + [ANY] * (peers + half - 2),
        [VMEM, VMEM] + [ANY] * peers,
        [
            scratch(piece, 256),
            scratch(piece, 256),
            scratch(HALF, width),
            scratch(HALF, width),
            scratch(rows, state),
            scratch(rows + HALF, state),
            dma(3),
        ],
    )(tab, cache, mine, other, share0, decays, x_rows, near, *sends, *onward)
    cars = {0: cars[0]} | {k: far(cars[k], k) for k in list(range(2, peers)) + [1]}
    uppers |= {2 * m + 1: far(uppers[2 * m], 1) for m in range(half)}
    final = call(
        bind(final_part, slots),
        shape((width, state), BF16),
        [SMEM] + [VMEM] * 6,
        scratch=[scratch(HALF, state)],
    )(tab, mine, other, share1, decays, late, second)
    gated, squares = call(
        bind(gate_part),
        [shape(x_rows.shape, F32), shape((slots, rows), F32)],
        [SMEM, VMEM, VMEM] + [ANY] * (2 * peers),
        scratch=[scratch(slots, rows, width), dma(slots, 2)],
    )(
        tab,
        yz,
        ez,
        *[cars[k] for k in range(peers)],
        *[uppers[k] for k in range(peers)],
    )
    mixed_rows = call(bind(norm_part), shape(x_rows.shape, BF16), [SMEM] + [VMEM] * 5, ANY, [scratch(*x_rows.shape), dma(slots)])(
        tab, gated, squares, swapped(squares), norm_gain[None], lens
    )
    return (mixed_rows, final.reshape(cache_state.shape))


def solution(mesh):
    in_specs = (
        P(("group", "sess", "dp"), None, "head"),
        P(("group", "sess", "dp"), None, "head"),
        P(("group", "sess", "dp"), None, None),
        P(("group", "sess", "dp"), None, None),
        P(("group", "sess", "dp"), "head", None),
        P("head"),
        P("head"),
        P("head"),
        P("head"),
        P(("group", "sess", "dp"), "head", None, None),
        P(("group", "sess", "dp")),
        P("group", None),
        P("group", None),
    )
    out_specs = (
        P(("group", "sess", "dp"), None, "head"),
        P(("group", "sess", "dp"), "head", None, None),
    )
    return jax.shard_map(
        per_device, mesh=mesh, in_specs=in_specs, out_specs=out_specs, check_vma=False
    )
```

```python
import functools

import jax
import jax.numpy as jnp
from jax import lax
from jax.experimental import pallas as pl
from jax.experimental.pallas import tpu as pltpu
from jax.sharding import PartitionSpec as P

F32 = jnp.float32
BF16 = jnp.bfloat16
HALF = 64
VMEM = pl.BlockSpec(memory_space=pltpu.VMEM)
SMEM = pl.BlockSpec(memory_space=pltpu.SMEM)
HBM = pl.BlockSpec(memory_space=pltpu.HBM)
ANY = pl.BlockSpec(memory_space=pl.ANY)


def dot(a, b, dims, precision=None):
    return lax.dot_general(
        a, b, ((dims[:1], dims[1:]), ((), ())), precision=precision, preferred_element_type=F32
    )


def iota(shape, dim):
    return lax.broadcasted_iota(jnp.int32, shape, dim)


def softplus(v):
    return jnp.maximum(v, 0.0) + jnp.log1p(jnp.exp(-jnp.abs(v)))


def running(v):
    rows = v.shape[1]
    upto = jnp.where(iota((rows, rows), 0) <= iota((rows, rows), 1), 1.0, 0.0).astype(F32)
    return dot(v, upto, (1, 0), lax.Precision.HIGHEST)


def silu(v):
    return v * (1.0 / (1.0 + jnp.exp(-v)))


def columns(params):
    heads = params.shape[1]
    eye = iota((heads, heads), 0) == iota((heads, heads), 1)
    return [
        jnp.sum(jnp.where(eye, params[i : i + 1], 0.0), axis=1, keepdims=True)
        for i in range(params.shape[0])
    ]


class Table:
    def __init__(self, tab, peers, slots):
        self.peers, self.slots = peers, slots
        self.me, self.odd, self.length = tab[0], tab[1], tab[2]
        count = peers * slots
        self.owner = lambda i: tab[3 + i]
        self.late = lambda i: tab[3 + count + i] % 2

    def far(self, j):
        return self.me ^ self.owner(self.me * self.slots + j)

    def slot(self, k):
        pick = jnp.int32(0)
        for j in range(1, self.slots):
            pick = jnp.where(self.far(j) == k, j, pick)
        return pick

    def holder(self, k, part):
        found = jnp.int32(0)
        for i in range(self.peers * self.slots):
            hit = (self.owner(i) == self.me ^ k) & (self.late(i) == part)
            found = jnp.where(hit, self.me ^ (i // self.slots), found)
        return found


class Copies:
    def __init__(self, sem):
        self.sem, self.count, self.started = sem, 0, []

    def __call__(self, src, dst, pred=None, again=False):
        self.count += not again
        copy = pltpu.make_async_copy(src, dst, self.sem.at[self.count - 1])
        if pred is None:
            copy.start()
        else:
            pl.when(pred)(copy.start)
        self.started.append((pred, copy))

    def wait(self):
        for pred, copy in self.started:
            if pred is None:
                copy.wait()
            else:
                pl.when(pred)(copy.wait)
        self.started = []


def gather(sem, dst, choices):
    for pred, pairs in choices:

        @pl.when(pred)
        def _():
            for src, part in pairs:
                pltpu.make_async_copy(src, part, sem).start()

    return pltpu.make_async_copy(dst, dst, sem).wait


def spans(width):
    return [slice(g * 256, (g + 1) * 256) for g in range(width // 256)]


def chunk(ref, index, width):
    size = width // 256 * HALF
    return ref.at[pl.ds(index * size, size)]


def from_rows(x, j, start, out):
    return [
        (x.at[j, pl.ds(start, HALF), lanes], out.at[pl.ds(g * HALF, HALF)])
        for g, lanes in enumerate(spans(x.shape[2]))
    ]


def tail_of(ref, size, start=0, count=None):
    return ref.at[pl.ds(ref.shape[0] - size + start, size if count is None else count)]


def send_part(peers, x_in, b, c, dt, owner, lens, own, near, *rest):
    smalls = (own, near, *rest[: peers - 2])
    outs = (own, near, *rest[peers - 2 : 2 * peers - 4])
    dtv, x, bc, table, length, sem = rest[2 * peers - 4 :]
    slots, rows, width = x.shape
    heads = dt.shape[1]
    dp = lax.axis_index("dp")
    odd = lax.axis_index("head") % 2
    copies = Copies(sem)
    copies(owner, table)
    copies(lens, length)
    copies(dt, dtv)
    copies(x_in, x)
    copies(b, bc, odd == 0)
    copies(c, bc, odd != 0, again=True)
    copies.wait()
    t = Table([lax.axis_index("sess"), odd, length[0]], peers, slots)
    t.owner = lambda i: table[dp, i]
    count = jnp.full((heads, rows), t.length.astype(F32)).astype(BF16)
    picks = [t.slot(k) for k in range(peers)]

    def put(out, index, j, start):
        for g, lanes in enumerate(spans(width)):
            at = (index * (width // 256) + g) * HALF
            out[at : at + HALF] = x[j, start : start + HALF, lanes]

    for k in list(range(2, peers)) + [1, 0]:
        out, j = smalls[k], picks[k]
        at = out.shape[0] - rows - 2 * heads
        out[at : at + rows] = bc[j]
        value = dtv[j]
        high = value.astype(BF16)
        value = value - high.astype(F32)
        middle = value.astype(BF16)
        low = (value - middle.astype(F32)).astype(BF16)
        out[at + rows : at + rows + heads] = jnp.concatenate([high, middle], axis=1)
        out[at + rows + heads :] = jnp.concatenate([low, count], axis=1)
        if k:
            put(outs[k], 0, j, 0)
    for m in range(peers // 2):
        put(near, m + 1, picks[1 ^ 2 * m], HALF)


def forward_part(peers, slots, tab, x, near, after, *rest):
    outs, sem = rest[:-1], rest[-1]
    rows, width = x.shape[1:]
    t = Table(tab, peers, slots)
    for m in range(1, peers // 2):
        out, at = outs[m - 1], t.holder(2 * m, 0)
        wait = gather(
            sem.at[m - 1],
            out,
            [
                (at == 0, from_rows(x, t.slot(2 * m), HALF, out)),
                (at == 1, [(chunk(near, m + 1, width), out)]),
            ],
        )
        pl.when(at < 2)(wait)


def pick_part(peers, slots, heads, tab, *rest):
    got = rest[:peers]
    mine, dts, lens, tails, counts, sem = rest[peers + 1 :]
    rows = mine.shape[0] - HALF
    size = rows + 2 * heads
    t = Table(tab, peers, slots)
    waits = []
    for part in range(2):
        at, out = t.holder(0, part), tails.at[part]
        choices = [(at == k, [(tail_of(got[k], size), out)]) for k in range(peers)]
        waits.append(gather(sem.at[part], out, choices))
    for j in range(slots):
        at, out = t.far(j), counts.at[j]
        choices = [
            (at == k, [(tail_of(got[k], size, rows + heads, heads), out)]) for k in range(peers)
        ]
        waits.append(gather(sem.at[2 + j], out, choices))
    for wait in waits:
        wait()
    mine[:rows] = tails[0, :rows]
    mine[rows:] = tails[1, :HALF]
    for part in range(2):
        first = tails[part, rows : rows + heads].astype(F32)
        second = tails[part, rows + heads :].astype(F32)
        dts[part] = first[:, :rows] + (first[:, rows:] + second[:, :rows])
    for j in range(slots):
        lens[j] = counts[j, :, rows:].astype(F32)


def touch_part(*refs):
    out = refs[-1]
    out[...] = jnp.zeros(out.shape, out.dtype)


def share_part(peers, slots, tab, dts, params, share0, share1, decays):
    parts, heads, rows = dts.shape
    width = share0.shape[1]
    size = width // heads
    per = 128 // size
    length = Table(tab, peers, slots).length
    alog, bias, _ = columns(params)
    rate = -jnp.exp(alog)
    col = iota((heads, rows), 1)
    lane = iota((rows, 128), 1) // size
    for part, out in ((0, share0), (1, share1)):
        step = jnp.where(col < length - part * rows, softplus(dts[part] + bias), 0.0)
        log_decay = running(rate * step)
        total = log_decay[:, rows - 1 :]
        share = jnp.transpose(jnp.exp(total - log_decay) * step)
        decays[part] = jnp.broadcast_to(jnp.exp(total).astype(BF16).astype(F32), (heads, 256))
        for p in range(width // 128):
            factor = jnp.broadcast_to(share[:, p * per : p * per + 1], (rows, 128))
            for q in range(1, per):
                factor = jnp.where(lane == q, share[:, p * per + q : p * per + q + 1], factor)
            out[:, p * 128 : (p + 1) * 128] = factor[: out.shape[0]]


def block_part(x_in, z_in, b_in, c_in, dt_in, params, yz, ez, x, z, b, c, dt, sem):
    slots, rows, width = x.shape
    heads = dt.shape[1]
    size = width // heads
    per = 128 // size
    waits = []
    for s in range(slots):
        copies = Copies(sem.at[s])
        for src, dst in ((dt_in, dt), (b_in, b), (c_in, c), (x_in, x), (z_in, z)):
            copies(src.at[s], dst.at[s])
        waits.append(copies)
    causal = iota((rows, rows), 0) >= iota((rows, rows), 1)
    lane = iota((rows, 128), 1) // size
    alog, bias, skip = columns(params)
    rate = -jnp.exp(alog)
    for s in range(slots):
        waits[s].wait()
        step = softplus(dt[s] + bias)
        log_decay = running(rate * step)
        log_col = jnp.transpose(log_decay)
        decay_col = jnp.exp(log_col)
        scores = jnp.where(causal, dot(c[s], b[s], (1, 1)), 0.0)
        for p in range(width // 128):
            lanes = slice(p * 128, (p + 1) * 128)
            xp = x[s, :, lanes]
            weights = []
            parts = []
            decay = decay_col[:, p * per : p * per + 1]
            own_skip = skip[p * per : p * per + 1]
            for q in range(per):
                h = p * per + q
                gap = jnp.minimum(log_col[:, h : h + 1] - log_decay[h : h + 1], 0.0)
                weights.append((jnp.exp(gap) * step[h : h + 1] * scores).astype(BF16))
                parts.append(jnp.where(lane == q, xp, jnp.zeros_like(xp)))
                if q:
                    decay = jnp.where(lane == q, decay_col[:, h : h + 1], decay)
                    own_skip = jnp.where(lane[:1] == q, skip[h : h + 1], own_skip)
            inner = dot(jnp.concatenate(weights, axis=1), jnp.concatenate(parts, axis=0), (1, 0))
            gate = silu(z[s, :, lanes].astype(F32))
            yz[s, :, lanes] = (inner + own_skip * xp.astype(F32)) * gate
            ez[s, :, lanes] = decay * gate


def early_part(peers, slots, tab, cache, mine, other, token, upper):
    def work(cs):
        for lanes in spans(cache.shape[0]):
            upper[:, lanes] = dot(cs[HALF : 2 * HALF], cache[lanes], (1, 1)).astype(BF16)

    odd = Table(tab, peers, slots).odd
    pl.when(odd == 0)(lambda: work(other))
    pl.when(odd != 0)(lambda: work(mine))


def late_part(peers, slots, tab, cache, mine, other, share, decays, x, near, *rest):
    half = peers // 2
    far, onward = rest[: peers - 2], rest[peers - 2 : peers - 3 + half]
    rest = rest[peers - 3 + half :]
    late, second, cars = rest[0], rest[1], rest[2 : peers + 2]
    low, high, car0, car1, bs, cs, sem = rest[peers + 2 :]
    rows, width = share.shape
    heads = decays.shape[1]
    size = width // heads
    t = Table(tab, peers, slots)
    k0, k1, j = t.holder(0, 0), t.holder(0, 1), t.slot(0)
    upper = (
        [(k0 == 0, from_rows(x, j, HALF, high)), (k0 == 1, [(chunk(near, 1, width), high)])]
        + [(k0 // 2 == m, [(onward[m - 1], high)]) for m in range(1, half)]
    )
    straight = [near] + list(far)

    def lower(at, out):
        return [(at == 0, from_rows(x, j, 0, out))] + [
            (at == k, [(chunk(straight[k - 1], 0, width), out)]) for k in range(1, peers)
        ]

    got_high = gather(sem.at[0], high, upper)
    got_low = gather(sem.at[1], low, lower(k0, low))
    got_second = gather(sem.at[2], second, lower(k1, second))

    @pl.when(t.odd == 0)
    def _():
        bs[...] = mine[:rows]
        cs[...] = other[...]

    @pl.when(t.odd != 0)
    def _():
        bs[...] = other[:rows]
        cs[...] = mine[...]

    for lanes in spans(width):
        car0[:, lanes] = dot(cs[:HALF], cache[lanes], (1, 1)).astype(BF16)
    got_low()
    got_high()
    for g, lanes in enumerate(spans(width)):
        at = slice(g * HALF, (g + 1) * HALF)
        xv = jnp.concatenate([low[at], high[at]], axis=0).astype(F32)
        local = dot((xv * share[:, lanes]).astype(BF16), bs[...], (0, 0)).astype(BF16).astype(F32)
        for q in range(256 // size):
            h = g * (256 // size) + q
            state = slice(h * size, (h + 1) * size)
            late[state] = (
                decays[0, h : h + 1] * cache[state].astype(F32)
                + local[q * size : (q + 1) * size]
            ).astype(BF16)
        car1[:, lanes] = dot(cs[rows:], late[lanes], (1, 1)).astype(BF16)
    got_second()
    waits = []
    for flag, at, src in ((0, k0, car0), (1, k1, car1)):
        choices = [(at == k, [(src, cars[k])]) for k in range(peers)]
        gather(sem.at[flag], src, choices)
        waits.append(pltpu.make_async_copy(src, cars[0], sem.at[flag]).wait)
    for wait in waits:
        wait()


def final_part(peers, slots, tab, mine, other, share, decays, late, second, final, bs):
    width = share.shape[1]
    heads = decays.shape[1]
    size = width // heads
    rows = mine.shape[0] - HALF
    odd = Table(tab, peers, slots).odd

    @pl.when(odd == 0)
    def _():
        bs[...] = mine[rows:]

    @pl.when(odd != 0)
    def _():
        bs[...] = other[rows:]

    for g, lanes in enumerate(spans(width)):
        xv = second[g * HALF : (g + 1) * HALF].astype(F32)
        local = dot((xv * share[:, lanes]).astype(BF16), bs[...], (0, 0)).astype(BF16).astype(F32)
        for q in range(256 // size):
            h = g * (256 // size) + q
            state = slice(h * size, (h + 1) * size)
            final[state] = (
                decays[1, h : h + 1] * late[state].astype(F32)
                + local[q * size : (q + 1) * size]
            ).astype(BF16)


def gate_part(peers, tab, yz, ez, *rest):
    cars, uppers = rest[:peers], rest[peers : 2 * peers]
    gated, squares = rest[2 * peers :]
    slots, rows, width = yz.shape
    t = Table(tab, peers, slots)

    def choose(at, refs, lanes):
        out = refs[0][:, lanes].astype(F32)
        for k in range(1, peers):
            out = jnp.where(at == k, refs[k][:, lanes].astype(F32), out)
        return out

    for j in range(slots):
        at = t.far(j)
        total = jnp.zeros((rows, 128), F32)
        for p in range(width // 128):
            lanes = slice(p * 128, (p + 1) * 128)
            got = jnp.concatenate([choose(at, cars, lanes), choose(at, uppers, lanes)], axis=0)
            value = yz[j, :, lanes] + ez[j, :, lanes] * got
            gated[j, :, lanes] = value
            total = total + value * value
        squares[j : j + 1] = jnp.sum(jnp.transpose(total), axis=0, keepdims=True)


def norm_part(peers, tab, gated, own, other, gain, lens, mixed, out, sem):
    slots, rows, width = gated.shape
    t = Table(tab, peers, slots)
    row = iota((rows, 128), 0).astype(F32)
    copies = Copies(sem)
    for j in range(slots):
        late = t.late(t.me * slots + j)
        live = row + (late * rows).astype(F32) < lens[j][:1]
        mean = (own[j : j + 1] + other[j : j + 1]) / (2.0 * width)
        inverse = jnp.transpose(jnp.broadcast_to(lax.rsqrt(mean + 1e-05), (rows, rows)))
        for p in range(width // 128):
            lanes = slice(p * 128, (p + 1) * 128)
            value = gated[j, :, lanes] * inverse * gain[:, lanes].astype(F32)
            out[j, :, lanes] = jnp.where(live, value, 0.0).astype(BF16)
        copies(out.at[j], mixed.at[j])
    copies.wait()


def call(kernel, outs, in_specs, out_specs=None, scratch=(), limit=24, cost=0):
    return pl.pallas_call(
        kernel,
        out_shape=outs,
        in_specs=in_specs,
        out_specs=out_specs if out_specs is not None else jax.tree.map(lambda _: VMEM, outs),
        scratch_shapes=scratch,
        compiler_params=pltpu.CompilerParams(vmem_limit_bytes=limit * 1024 * 1024),
        cost_estimate=pl.CostEstimate(flops=0, bytes_accessed=cost, transcendentals=0),
    )


def per_device(
    x_rows,
    z_rows,
    input_projection_matrix,
    c_rows,
    dt_raw,
    a_log,
    dt_bias,
    d_skip,
    norm_gain,
    cache_state,
    lengths,
    slot_owner,
    slot_task,
):
    slots, rows, width = x_rows.shape
    heads = dt_raw.shape[1]
    state = cache_state.shape[3]
    peers = lax.axis_size("sess")
    half = peers // 2
    head = lax.axis_index("head")
    groups = input_projection_matrix.shape[2] // state
    if groups > 1:
        at = head // 2 * state
        b = lax.dynamic_slice_in_dim(input_projection_matrix, at, state, 2)
        c = lax.dynamic_slice_in_dim(c_rows, at, state, 2)
    else:
        b, c = input_projection_matrix, c_rows

    def own_row(table):
        mine = iota(table.shape, 0) == lax.axis_index("dp")
        return jnp.sum(jnp.where(mine, table, 0), axis=0)

    ids = jnp.stack([lax.axis_index("sess"), head % 2]).astype(jnp.int32)
    tab = jnp.concatenate([ids, lengths, own_row(slot_owner), own_row(slot_task)])
    params = jnp.stack([a_log, dt_bias, d_skip])
    cache = cache_state.reshape(width, state)

    def far(value, k):
        return lax.ppermute(value, "sess", [(i, i ^ k) for i in range(peers)])

    def swapped(value):
        count = lax.axis_size("head")
        return lax.ppermute(value, "head", [(i, i ^ 1) for i in range(count)])

    def scratch(*sizes, dtype=BF16):
        return pltpu.VMEM(sizes, dtype)

    shape = jax.ShapeDtypeStruct
    dma = lambda *sizes: pltpu.SemaphoreType.DMA(sizes)
    bind = lambda kernel, *more: functools.partial(kernel, peers, *more)
    count = width // 256
    piece = count * HALF
    tail = rows + 2 * heads
    packed = lambda size: shape((size, 256), BF16)
    upper_rows = shape((HALF, width), BF16)
    own, near, *rest = call(
        bind(send_part),
        [packed(tail), packed((1 + half) * piece + tail)]
        + [packed(tail)] * (peers - 2)
        + [packed(piece)] * (peers - 2),
        [HBM] * 6,
        scratch=[
            scratch(*dt_raw.shape, dtype=F32),
            scratch(*x_rows.shape),
            scratch(*b.shape),
            pltpu.SMEM(slot_owner.shape, jnp.int32),
            pltpu.SMEM(lengths.shape, jnp.int32),
            dma(5),
        ],
        limit=60,
    )(x_rows, b, c, dt_raw, slot_owner, lengths)
    near = far(near, 1)
    smalls = [far(value, k + 2) for k, value in enumerate(rest[: peers - 2])]
    sends = [far(value, k + 2) for k, value in enumerate(rest[peers - 2 :])]
    yz, ez = call(
        block_part,
        [shape(x_rows.shape, F32)] * 2,
        [HBM] * 5 + [VMEM],
        scratch=[
            scratch(*x_rows.shape),
            scratch(*x_rows.shape),
            scratch(*b.shape),
            scratch(*b.shape),
            scratch(*dt_raw.shape, dtype=F32),
            dma(slots, 5),
        ],
    )(x_rows, z_rows, b, c, dt_raw, params)
    passing = call(
        bind(forward_part, slots),
        [packed(piece)] * (half - 1),
        [SMEM, HBM, ANY, ANY],
        [ANY] * (half - 1),
        [dma(half - 1)],
    )(tab, x_rows, near, ez)
    onward = [far(value, 2 * (m + 1)) for m, value in enumerate(passing)]
    mine, dts, lens = call(
        bind(pick_part, slots, heads),
        [
            shape((rows + HALF, state), BF16),
            shape((2, heads, rows), F32),
            shape((slots, heads, rows), F32),
        ],
        [SMEM] + [ANY] * (peers + 1),
        scratch=[scratch(2, tail, 256), scratch(slots, heads, 256), dma(2 + slots)],
    )(tab, own, near, *smalls, passing[0])
    other = swapped(mine)
    share0, share1, decays = call(
        bind(share_part, slots),
        [shape((rows, width), F32), shape((HALF, width), F32), shape((2, heads, 256), F32)],
        [SMEM, VMEM, VMEM],
    )(tab, dts, params)
    token = call(touch_part, shape((8, 128), F32), [ANY] * (peers - 2), cost=40_000_000)(*sends)
    upper = call(
        bind(early_part, slots), upper_rows, [SMEM, VMEM, VMEM, VMEM, ANY]
    )(tab, cache, mine, other, token)
    uppers = {2 * m: far(upper, 2 * m) if m else upper for m in range(half)}
    late, second, *cars = call(
        bind(late_part, slots),
        [shape((width, state), BF16), packed(piece)] + [upper_rows] * peers,
        [SMEM] + [VMEM] * 5 + [HBM] + [ANY] * (peers + half - 2),
        [VMEM, VMEM] + [ANY] * peers,
        [
            scratch(piece, 256),
            scratch(piece, 256),
            scratch(HALF, width),
            scratch(HALF, width),
            scratch(rows, state),
            scratch(rows + HALF, state),
            dma(3),
        ],
    )(tab, cache, mine, other, share0, decays, x_rows, near, *sends, *onward)
    cars = {0: cars[0]} | {k: far(cars[k], k) for k in list(range(2, peers)) + [1]}
    uppers |= {2 * m + 1: far(uppers[2 * m], 1) for m in range(half)}
    final = call(
        bind(final_part, slots),
        shape((width, state), BF16),
        [SMEM] + [VMEM] * 6,
        scratch=[scratch(HALF, state)],
    )(tab, mine, other, share1, decays, late, second)
    gated, squares = call(
        bind(gate_part),
        [shape(x_rows.shape, F32), shape((slots, rows), F32)],
        [SMEM] + [VMEM] * (2 + 2 * peers),
    )(
        tab,
        yz,
        ez,
        *[cars[k] for k in range(peers)],
        *[uppers[k] for k in range(peers)],
    )
    mixed_rows = call(bind(norm_part), shape(x_rows.shape, BF16), [SMEM] + [VMEM] * 5, ANY, [scratch(*x_rows.shape), dma(slots)])(
        tab, gated, squares, swapped(squares), norm_gain[None], lens
    )
    return (mixed_rows, final.reshape(cache_state.shape))


def solution(mesh):
    in_specs = (
        P(("group", "sess", "dp"), None, "head"),
        P(("group", "sess", "dp"), None, "head"),
        P(("group", "sess", "dp"), None, None),
        P(("group", "sess", "dp"), None, None),
        P(("group", "sess", "dp"), "head", None),
        P("head"),
        P("head"),
        P("head"),
        P("head"),
        P(("group", "sess", "dp"), "head", None, None),
        P(("group", "sess", "dp")),
        P("group", None),
        P("group", None),
    )
    out_specs = (
        P(("group", "sess", "dp"), None, "head"),
        P(("group", "sess", "dp"), "head", None, None),
    )
    return jax.shard_map(
        per_device, mesh=mesh, in_specs=in_specs, out_specs=out_specs, check_vma=False
    )
```

```python
import functools

import jax
import jax.numpy as jnp
from jax import lax
from jax.experimental import pallas as pl
from jax.experimental.pallas import tpu as pltpu
from jax.sharding import PartitionSpec as P

F32 = jnp.float32
BF16 = jnp.bfloat16
HALF = 64
VMEM = pl.BlockSpec(memory_space=pltpu.VMEM)
SMEM = pl.BlockSpec(memory_space=pltpu.SMEM)
HBM = pl.BlockSpec(memory_space=pltpu.HBM)
ANY = pl.BlockSpec(memory_space=pl.ANY)


def dot(a, b, dims, precision=None):
    return lax.dot_general(
        a, b, ((dims[:1], dims[1:]), ((), ())), precision=precision, preferred_element_type=F32
    )


def iota(shape, dim):
    return lax.broadcasted_iota(jnp.int32, shape, dim)


def softplus(v):
    return jnp.maximum(v, 0.0) + jnp.log1p(jnp.exp(-jnp.abs(v)))


def running(v):
    rows = v.shape[1]
    upto = jnp.where(iota((rows, rows), 0) <= iota((rows, rows), 1), 1.0, 0.0).astype(F32)
    return dot(v, upto, (1, 0), lax.Precision.HIGHEST)


def silu(v):
    return v * (1.0 / (1.0 + jnp.exp(-v)))


def columns(params):
    heads = params.shape[1]
    eye = iota((heads, heads), 0) == iota((heads, heads), 1)
    return [
        jnp.sum(jnp.where(eye, params[i : i + 1], 0.0), axis=1, keepdims=True)
        for i in range(params.shape[0])
    ]


class Table:
    def __init__(self, tab, peers, slots):
        self.peers, self.slots = peers, slots
        self.me, self.odd, self.length = tab[0], tab[1], tab[2]
        count = peers * slots
        self.owner = lambda i: tab[3 + i]
        self.late = lambda i: tab[3 + count + i] % 2

    def far(self, j):
        return self.me ^ self.owner(self.me * self.slots + j)

    def slot(self, k):
        pick = jnp.int32(0)
        for j in range(1, self.slots):
            pick = jnp.where(self.far(j) == k, j, pick)
        return pick

    def holder(self, k, part):
        found = jnp.int32(0)
        for i in range(self.peers * self.slots):
            hit = (self.owner(i) == self.me ^ k) & (self.late(i) == part)
            found = jnp.where(hit, self.me ^ (i // self.slots), found)
        return found


class Copies:
    def __init__(self, sem):
        self.sem, self.count, self.started = sem, 0, []

    def __call__(self, src, dst, pred=None, again=False):
        self.count += not again
        copy = pltpu.make_async_copy(src, dst, self.sem.at[self.count - 1])
        if pred is None:
            copy.start()
        else:
            pl.when(pred)(copy.start)
        self.started.append((pred, copy))

    def wait(self):
        for pred, copy in self.started:
            if pred is None:
                copy.wait()
            else:
                pl.when(pred)(copy.wait)
        self.started = []


def gather(sem, dst, choices):
    for pred, pairs in choices:

        @pl.when(pred)
        def _():
            for src, part in pairs:
                pltpu.make_async_copy(src, part, sem).start()

    return pltpu.make_async_copy(dst, dst, sem).wait


def spans(width):
    return [slice(g * 256, (g + 1) * 256) for g in range(width // 256)]


def chunk(ref, index, width):
    size = width // 256 * HALF
    return ref.at[pl.ds(index * size, size)]


def from_rows(x, j, start, out):
    return [
        (x.at[j, pl.ds(start, HALF), lanes], out.at[pl.ds(g * HALF, HALF)])
        for g, lanes in enumerate(spans(x.shape[2]))
    ]


def tail_of(ref, size, start=0, count=None):
    return ref.at[pl.ds(ref.shape[0] - size + start, size if count is None else count)]


def send_part(peers, x_in, b, c, dt, owner, lens, own, near, *rest):
    smalls = (own, near, *rest[: peers - 2])
    outs = (own, near, *rest[peers - 2 : 2 * peers - 4])
    dtv, x, bc, table, length, sem = rest[2 * peers - 4 :]
    slots, rows, width = x.shape
    heads = dt.shape[1]
    dp = lax.axis_index("dp")
    odd = lax.axis_index("head") % 2
    copies = Copies(sem)
    copies(owner, table)
    copies(lens, length)
    copies(dt, dtv)
    copies(x_in, x)
    copies(b, bc, odd == 0)
    copies(c, bc, odd != 0, again=True)
    copies.wait()
    t = Table([lax.axis_index("sess"), odd, length[0]], peers, slots)
    t.owner = lambda i: table[dp, i]
    count = jnp.full((heads, rows), t.length.astype(F32)).astype(BF16)
    picks = [t.slot(k) for k in range(peers)]

    def put(out, index, j, start):
        for g, lanes in enumerate(spans(width)):
            at = (index * (width // 256) + g) * HALF
            out[at : at + HALF] = x[j, start : start + HALF, lanes]

    for k in list(range(2, peers)) + [1, 0]:
        out, j = smalls[k], picks[k]
        at = out.shape[0] - rows - 2 * heads
        out[at : at + rows] = bc[j]
        value = dtv[j]
        high = value.astype(BF16)
        value = value - high.astype(F32)
        middle = value.astype(BF16)
        low = (value - middle.astype(F32)).astype(BF16)
        out[at + rows : at + rows + heads] = jnp.concatenate([high, middle], axis=1)
        out[at + rows + heads :] = jnp.concatenate([low, count], axis=1)
        if k:
            put(outs[k], 0, j, 0)
    for m in range(peers // 2):
        put(near, m + 1, picks[1 ^ 2 * m], HALF)


def forward_part(peers, slots, tab, x, near, after, *rest):
    outs, sem = rest[:-1], rest[-1]
    rows, width = x.shape[1:]
    t = Table(tab, peers, slots)
    for m in range(1, peers // 2):
        out, at = outs[m - 1], t.holder(2 * m, 0)
        wait = gather(
            sem.at[m - 1],
            out,
            [
                (at == 0, from_rows(x, t.slot(2 * m), HALF, out)),
                (at == 1, [(chunk(near, m + 1, width), out)]),
            ],
        )
        pl.when(at < 2)(wait)


def pick_part(peers, slots, heads, tab, *rest):
    got = rest[:peers]
    mine, dts, lens, tails, counts, sem = rest[peers + 1 :]
    rows = mine.shape[0] - HALF
    size = rows + 2 * heads
    t = Table(tab, peers, slots)
    waits = []
    for part in range(2):
        at, out = t.holder(0, part), tails.at[part]
        choices = [(at == k, [(tail_of(got[k], size), out)]) for k in range(peers)]
        waits.append(gather(sem.at[part], out, choices))
    for j in range(slots):
        at, out = t.far(j), counts.at[j]
        choices = [
            (at == k, [(tail_of(got[k], size, rows + heads, heads), out)]) for k in range(peers)
        ]
        waits.append(gather(sem.at[2 + j], out, choices))
    for wait in waits:
        wait()
    mine[:rows] = tails[0, :rows]
    mine[rows:] = tails[1, :HALF]
    for part in range(2):
        first = tails[part, rows : rows + heads].astype(F32)
        second = tails[part, rows + heads :].astype(F32)
        dts[part] = first[:, :rows] + (first[:, rows:] + second[:, :rows])
    for j in range(slots):
        lens[j] = counts[j, :, rows:].astype(F32)


def touch_part(*refs):
    out = refs[-1]
    out[...] = jnp.zeros(out.shape, out.dtype)


def share_part(peers, slots, tab, dts, params, share0, share1, decays):
    parts, heads, rows = dts.shape
    width = share0.shape[1]
    size = width // heads
    per = 128 // size
    length = Table(tab, peers, slots).length
    alog, bias, _ = columns(params)
    rate = -jnp.exp(alog)
    col = iota((heads, rows), 1)
    lane = iota((rows, 128), 1) // size
    for part, out in ((0, share0), (1, share1)):
        step = jnp.where(col < length - part * rows, softplus(dts[part] + bias), 0.0)
        log_decay = running(rate * step)
        total = log_decay[:, rows - 1 :]
        share = jnp.transpose(jnp.exp(total - log_decay) * step)
        decays[part] = jnp.broadcast_to(jnp.exp(total).astype(BF16).astype(F32), (heads, 256))
        for p in range(width // 128):
            factor = jnp.broadcast_to(share[:, p * per : p * per + 1], (rows, 128))
            for q in range(1, per):
                factor = jnp.where(lane == q, share[:, p * per + q : p * per + q + 1], factor)
            out[:, p * 128 : (p + 1) * 128] = factor[: out.shape[0]]


def block_part(x_in, z_in, b_in, c_in, dt_in, params, yz, ez, x, z, b, c, dt, sem):
    slots, rows, width = x.shape
    heads = dt.shape[1]
    size = width // heads
    per = 128 // size
    waits = []
    for s in range(slots):
        copies = Copies(sem.at[s])
        for src, dst in ((dt_in, dt), (b_in, b), (c_in, c), (x_in, x), (z_in, z)):
            copies(src.at[s], dst.at[s])
        waits.append(copies)
    causal = iota((rows, rows), 0) >= iota((rows, rows), 1)
    lane = iota((rows, 128), 1) // size
    alog, bias, skip = columns(params)
    rate = -jnp.exp(alog)
    for s in range(slots):
        waits[s].wait()
        step = softplus(dt[s] + bias)
        log_decay = running(rate * step)
        log_col = jnp.transpose(log_decay)
        decay_col = jnp.exp(log_col)
        scores = jnp.where(causal, dot(c[s], b[s], (1, 1)), 0.0)
        for p in range(width // 128):
            lanes = slice(p * 128, (p + 1) * 128)
            xp = x[s, :, lanes]
            weights = []
            parts = []
            decay = decay_col[:, p * per : p * per + 1]
            own_skip = skip[p * per : p * per + 1]
            for q in range(per):
                h = p * per + q
                gap = jnp.minimum(log_col[:, h : h + 1] - log_decay[h : h + 1], 0.0)
                weights.append((jnp.exp(gap) * step[h : h + 1] * scores).astype(BF16))
                parts.append(jnp.where(lane == q, xp, jnp.zeros_like(xp)))
                if q:
                    decay = jnp.where(lane == q, decay_col[:, h : h + 1], decay)
                    own_skip = jnp.where(lane[:1] == q, skip[h : h + 1], own_skip)
            inner = dot(jnp.concatenate(weights, axis=1), jnp.concatenate(parts, axis=0), (1, 0))
            gate = silu(z[s, :, lanes].astype(F32))
            yz[s, :, lanes] = (inner + own_skip * xp.astype(F32)) * gate
            ez[s, :, lanes] = decay * gate


def early_part(peers, slots, tab, cache, mine, other, token, upper):
    def work(cs):
        for lanes in spans(cache.shape[0]):
            upper[:, lanes] = dot(cs[HALF : 2 * HALF], cache[lanes], (1, 1)).astype(BF16)

    odd = Table(tab, peers, slots).odd
    pl.when(odd == 0)(lambda: work(other))
    pl.when(odd != 0)(lambda: work(mine))


def late_part(peers, slots, tab, cache, mine, other, share, decays, x, near, *rest):
    half = peers // 2
    far, onward = rest[: peers - 2], rest[peers - 2 : peers - 3 + half]
    rest = rest[peers - 3 + half :]
    late, second, cars = rest[0], rest[1], rest[2 : peers + 2]
    car0, car1, bs, cs, sem = rest[peers + 2 :]
    rows, width = share.shape
    heads = decays.shape[1]
    size = width // heads
    t = Table(tab, peers, slots)
    k0, k1, j = t.holder(0, 0), t.holder(0, 1), t.slot(0)
    straight = [near] + list(far)
    count = width // 256

    def one_of(values):
        out = values[0][1]
        for pred, value in values[1:]:
            out = jnp.where(pred, value, out)
        return out

    def low(at, g, lanes):
        rest = [(at == k, straight[k - 1][g * HALF : (g + 1) * HALF].astype(F32)) for k in range(1, peers)]
        return one_of([(None, x[j, :HALF, lanes].astype(F32))] + rest)

    def high(g, lanes):
        rest = [(k0 == 1, near[(count + g) * HALF : (count + g + 1) * HALF].astype(F32))]
        rest += [
            (k0 // 2 == m, onward[m - 1][g * HALF : (g + 1) * HALF].astype(F32))
            for m in range(1, half)
        ]
        return one_of([(None, x[j, HALF:, lanes].astype(F32))] + rest)

    @pl.when(t.odd == 0)
    def _():
        bs[...] = mine[:rows]
        cs[...] = other[...]

    @pl.when(t.odd != 0)
    def _():
        bs[...] = other[:rows]
        cs[...] = mine[...]

    for lanes in spans(width):
        car0[:, lanes] = dot(cs[:HALF], cache[lanes], (1, 1)).astype(BF16)
    for g, lanes in enumerate(spans(width)):
        second[g * HALF : (g + 1) * HALF] = low(k1, g, lanes).astype(BF16)
        xv = jnp.concatenate([low(k0, g, lanes), high(g, lanes)], axis=0)
        local = dot((xv * share[:, lanes]).astype(BF16), bs[...], (0, 0)).astype(BF16).astype(F32)
        for q in range(256 // size):
            h = g * (256 // size) + q
            state = slice(h * size, (h + 1) * size)
            late[state] = (
                decays[0, h : h + 1] * cache[state].astype(F32)
                + local[q * size : (q + 1) * size]
            ).astype(BF16)
        car1[:, lanes] = dot(cs[rows:], late[lanes], (1, 1)).astype(BF16)
    waits = []
    for flag, at, src in ((0, k0, car0), (1, k1, car1)):
        choices = [(at == k, [(src, cars[k])]) for k in range(peers)]
        gather(sem.at[flag], src, choices)
        waits.append(pltpu.make_async_copy(src, cars[0], sem.at[flag]).wait)
    for wait in waits:
        wait()


def final_part(peers, slots, tab, mine, other, share, decays, late, second, final, bs):
    width = share.shape[1]
    heads = decays.shape[1]
    size = width // heads
    rows = mine.shape[0] - HALF
    odd = Table(tab, peers, slots).odd

    @pl.when(odd == 0)
    def _():
        bs[...] = mine[rows:]

    @pl.when(odd != 0)
    def _():
        bs[...] = other[rows:]

    for g, lanes in enumerate(spans(width)):
        xv = second[g * HALF : (g + 1) * HALF].astype(F32)
        local = dot((xv * share[:, lanes]).astype(BF16), bs[...], (0, 0)).astype(BF16).astype(F32)
        for q in range(256 // size):
            h = g * (256 // size) + q
            state = slice(h * size, (h + 1) * size)
            final[state] = (
                decays[1, h : h + 1] * late[state].astype(F32)
                + local[q * size : (q + 1) * size]
            ).astype(BF16)


def gate_part(peers, tab, yz, ez, *rest):
    cars, uppers = rest[:peers], rest[peers : 2 * peers]
    gated, squares = rest[2 * peers :]
    slots, rows, width = yz.shape
    t = Table(tab, peers, slots)

    def choose(at, refs, lanes):
        out = refs[0][:, lanes].astype(F32)
        for k in range(1, peers):
            out = jnp.where(at == k, refs[k][:, lanes].astype(F32), out)
        return out

    for j in range(slots):
        at = t.far(j)
        total = jnp.zeros((rows, 128), F32)
        for p in range(width // 128):
            lanes = slice(p * 128, (p + 1) * 128)
            got = jnp.concatenate([choose(at, cars, lanes), choose(at, uppers, lanes)], axis=0)
            value = yz[j, :, lanes] + ez[j, :, lanes] * got
            gated[j, :, lanes] = value
            total = total + value * value
        squares[j : j + 1] = jnp.sum(jnp.transpose(total), axis=0, keepdims=True)


def norm_part(peers, tab, gated, own, other, gain, lens, mixed, out, sem):
    slots, rows, width = gated.shape
    t = Table(tab, peers, slots)
    row = iota((rows, 128), 0).astype(F32)
    copies = Copies(sem)
    for j in range(slots):
        late = t.late(t.me * slots + j)
        live = row + (late * rows).astype(F32) < lens[j][:1]
        mean = (own[j : j + 1] + other[j : j + 1]) / (2.0 * width)
        inverse = jnp.transpose(jnp.broadcast_to(lax.rsqrt(mean + 1e-05), (rows, rows)))
        for p in range(width // 128):
            lanes = slice(p * 128, (p + 1) * 128)
            value = gated[j, :, lanes] * inverse * gain[:, lanes].astype(F32)
            out[j, :, lanes] = jnp.where(live, value, 0.0).astype(BF16)
        copies(out.at[j], mixed.at[j])
    copies.wait()


def call(kernel, outs, in_specs, out_specs=None, scratch=(), limit=24, cost=0):
    return pl.pallas_call(
        kernel,
        out_shape=outs,
        in_specs=in_specs,
        out_specs=out_specs if out_specs is not None else jax.tree.map(lambda _: VMEM, outs),
        scratch_shapes=scratch,
        compiler_params=pltpu.CompilerParams(vmem_limit_bytes=limit * 1024 * 1024),
        cost_estimate=pl.CostEstimate(flops=0, bytes_accessed=cost, transcendentals=0),
    )


def per_device(
    x_rows,
    z_rows,
    input_projection_matrix,
    c_rows,
    dt_raw,
    a_log,
    dt_bias,
    d_skip,
    norm_gain,
    cache_state,
    lengths,
    slot_owner,
    slot_task,
):
    slots, rows, width = x_rows.shape
    heads = dt_raw.shape[1]
    state = cache_state.shape[3]
    peers = lax.axis_size("sess")
    half = peers // 2
    head = lax.axis_index("head")
    groups = input_projection_matrix.shape[2] // state
    if groups > 1:
        at = head // 2 * state
        b = lax.dynamic_slice_in_dim(input_projection_matrix, at, state, 2)
        c = lax.dynamic_slice_in_dim(c_rows, at, state, 2)
    else:
        b, c = input_projection_matrix, c_rows

    def own_row(table):
        mine = iota(table.shape, 0) == lax.axis_index("dp")
        return jnp.sum(jnp.where(mine, table, 0), axis=0)

    ids = jnp.stack([lax.axis_index("sess"), head % 2]).astype(jnp.int32)
    tab = jnp.concatenate([ids, lengths, own_row(slot_owner), own_row(slot_task)])
    params = jnp.stack([a_log, dt_bias, d_skip])
    cache = cache_state.reshape(width, state)

    def far(value, k):
        return lax.ppermute(value, "sess", [(i, i ^ k) for i in range(peers)])

    def swapped(value):
        count = lax.axis_size("head")
        return lax.ppermute(value, "head", [(i, i ^ 1) for i in range(count)])

    def scratch(*sizes, dtype=BF16):
        return pltpu.VMEM(sizes, dtype)

    shape = jax.ShapeDtypeStruct
    dma = lambda *sizes: pltpu.SemaphoreType.DMA(sizes)
    bind = lambda kernel, *more: functools.partial(kernel, peers, *more)
    count = width // 256
    piece = count * HALF
    tail = rows + 2 * heads
    packed = lambda size: shape((size, 256), BF16)
    upper_rows = shape((HALF, width), BF16)
    own, near, *rest = call(
        bind(send_part),
        [packed(tail), packed((1 + half) * piece + tail)]
        + [packed(tail)] * (peers - 2)
        + [packed(piece)] * (peers - 2),
        [HBM] * 6,
        scratch=[
            scratch(*dt_raw.shape, dtype=F32),
            scratch(*x_rows.shape),
            scratch(*b.shape),
            pltpu.SMEM(slot_owner.shape, jnp.int32),
            pltpu.SMEM(lengths.shape, jnp.int32),
            dma(5),
        ],
        limit=60,
    )(x_rows, b, c, dt_raw, slot_owner, lengths)
    near = far(near, 1)
    smalls = [far(value, k + 2) for k, value in enumerate(rest[: peers - 2])]
    sends = [far(value, k + 2) for k, value in enumerate(rest[peers - 2 :])]
    yz, ez = call(
        block_part,
        [shape(x_rows.shape, F32)] * 2,
        [HBM] * 5 + [VMEM],
        scratch=[
            scratch(*x_rows.shape),
            scratch(*x_rows.shape),
            scratch(*b.shape),
            scratch(*b.shape),
            scratch(*dt_raw.shape, dtype=F32),
            dma(slots, 5),
        ],
    )(x_rows, z_rows, b, c, dt_raw, params)
    passing = call(
        bind(forward_part, slots),
        [packed(piece)] * (half - 1),
        [SMEM, HBM, ANY, ANY],
        [ANY] * (half - 1),
        [dma(half - 1)],
    )(tab, x_rows, near, ez)
    onward = [far(value, 2 * (m + 1)) for m, value in enumerate(passing)]
    mine, dts, lens = call(
        bind(pick_part, slots, heads),
        [
            shape((rows + HALF, state), BF16),
            shape((2, heads, rows), F32),
            shape((slots, heads, rows), F32),
        ],
        [SMEM] + [ANY] * (peers + 1),
        scratch=[scratch(2, tail, 256), scratch(slots, heads, 256), dma(2 + slots)],
    )(tab, own, near, *smalls, passing[0])
    other = swapped(mine)
    share0, share1, decays = call(
        bind(share_part, slots),
        [shape((rows, width), F32), shape((HALF, width), F32), shape((2, heads, 256), F32)],
        [SMEM, VMEM, VMEM],
    )(tab, dts, params)
    token = call(touch_part, shape((8, 128), F32), [ANY] * (peers - 2), cost=40_000_000)(*sends)
    upper = call(
        bind(early_part, slots), upper_rows, [SMEM, VMEM, VMEM, VMEM, ANY]
    )(tab, cache, mine, other, token)
    uppers = {2 * m: far(upper, 2 * m) if m else upper for m in range(half)}
    late, second, *cars = call(
        bind(late_part, slots),
        [shape((width, state), BF16), packed(piece)] + [upper_rows] * peers,
        [SMEM] + [VMEM] * (5 + 1 + peers + half - 2),
        [VMEM, VMEM] + [ANY] * peers,
        [
            scratch(HALF, width),
            scratch(HALF, width),
            scratch(rows, state),
            scratch(rows + HALF, state),
            dma(3),
        ],
    )(tab, cache, mine, other, share0, decays, x_rows, near, *sends, *onward)
    cars = {0: cars[0]} | {k: far(cars[k], k) for k in list(range(2, peers)) + [1]}
    uppers |= {2 * m + 1: far(uppers[2 * m], 1) for m in range(half)}
    final = call(
        bind(final_part, slots),
        shape((width, state), BF16),
        [SMEM] + [VMEM] * 6,
        scratch=[scratch(HALF, state)],
    )(tab, mine, other, share1, decays, late, second)
    gated, squares = call(
        bind(gate_part),
        [shape(x_rows.shape, F32), shape((slots, rows), F32)],
        [SMEM] + [VMEM] * (2 + 2 * peers),
    )(
        tab,
        yz,
        ez,
        *[cars[k] for k in range(peers)],
        *[uppers[k] for k in range(peers)],
    )
    mixed_rows = call(bind(norm_part), shape(x_rows.shape, BF16), [SMEM] + [VMEM] * 5, ANY, [scratch(*x_rows.shape), dma(slots)])(
        tab, gated, squares, swapped(squares), norm_gain[None], lens
    )
    return (mixed_rows, final.reshape(cache_state.shape))


def solution(mesh):
    in_specs = (
        P(("group", "sess", "dp"), None, "head"),
        P(("group", "sess", "dp"), None, "head"),
        P(("group", "sess", "dp"), None, None),
        P(("group", "sess", "dp"), None, None),
        P(("group", "sess", "dp"), "head", None),
        P("head"),
        P("head"),
        P("head"),
        P("head"),
        P(("group", "sess", "dp"), "head", None, None),
        P(("group", "sess", "dp")),
        P("group", None),
        P("group", None),
    )
    out_specs = (
        P(("group", "sess", "dp"), None, "head"),
        P(("group", "sess", "dp"), "head", None, None),
    )
    return jax.shard_map(
        per_device, mesh=mesh, in_specs=in_specs, out_specs=out_specs, check_vma=False
    )
```

```python
import functools

import jax
import jax.numpy as jnp
from jax import lax
from jax.experimental import pallas as pl
from jax.experimental.pallas import tpu as pltpu
from jax.sharding import PartitionSpec as P

F32 = jnp.float32
BF16 = jnp.bfloat16
HALF = 64
VMEM = pl.BlockSpec(memory_space=pltpu.VMEM)
SMEM = pl.BlockSpec(memory_space=pltpu.SMEM)
HBM = pl.BlockSpec(memory_space=pltpu.HBM)
ANY = pl.BlockSpec(memory_space=pl.ANY)


def dot(a, b, dims, precision=None):
    return lax.dot_general(
        a, b, ((dims[:1], dims[1:]), ((), ())), precision=precision, preferred_element_type=F32
    )


def iota(shape, dim):
    return lax.broadcasted_iota(jnp.int32, shape, dim)


def softplus(v):
    return jnp.maximum(v, 0.0) + jnp.log1p(jnp.exp(-jnp.abs(v)))


def running(v):
    rows = v.shape[1]
    upto = jnp.where(iota((rows, rows), 0) <= iota((rows, rows), 1), 1.0, 0.0).astype(F32)
    return dot(v, upto, (1, 0), lax.Precision.HIGHEST)


def silu(v):
    return v * (1.0 / (1.0 + jnp.exp(-v)))


def columns(params):
    heads = params.shape[1]
    eye = iota((heads, heads), 0) == iota((heads, heads), 1)
    return [
        jnp.sum(jnp.where(eye, params[i : i + 1], 0.0), axis=1, keepdims=True)
        for i in range(params.shape[0])
    ]


class Table:
    def __init__(self, tab, peers, slots):
        self.peers, self.slots = peers, slots
        self.me, self.odd, self.length = tab[0], tab[1], tab[2]
        count = peers * slots
        self.owner = lambda i: tab[3 + i]
        self.late = lambda i: tab[3 + count + i] % 2

    def far(self, j):
        return self.me ^ self.owner(self.me * self.slots + j)

    def slot(self, k):
        pick = jnp.int32(0)
        for j in range(1, self.slots):
            pick = jnp.where(self.far(j) == k, j, pick)
        return pick

    def holder(self, k, part):
        found = jnp.int32(0)
        for i in range(self.peers * self.slots):
            hit = (self.owner(i) == self.me ^ k) & (self.late(i) == part)
            found = jnp.where(hit, self.me ^ (i // self.slots), found)
        return found


class Copies:
    def __init__(self, sem):
        self.sem, self.count, self.started = sem, 0, []

    def __call__(self, src, dst, pred=None, again=False):
        self.count += not again
        copy = pltpu.make_async_copy(src, dst, self.sem.at[self.count - 1])
        if pred is None:
            copy.start()
        else:
            pl.when(pred)(copy.start)
        self.started.append((pred, copy))

    def wait(self):
        for pred, copy in self.started:
            if pred is None:
                copy.wait()
            else:
                pl.when(pred)(copy.wait)
        self.started = []


def gather(sem, dst, choices):
    for pred, pairs in choices:

        @pl.when(pred)
        def _():
            for src, part in pairs:
                pltpu.make_async_copy(src, part, sem).start()

    return pltpu.make_async_copy(dst, dst, sem).wait


def spans(width):
    return [slice(g * 256, (g + 1) * 256) for g in range(width // 256)]


def chunk(ref, index, width):
    size = width // 256 * HALF
    return ref.at[pl.ds(index * size, size)]


def from_rows(x, j, start, out):
    return [
        (x.at[j, pl.ds(start, HALF), lanes], out.at[pl.ds(g * HALF, HALF)])
        for g, lanes in enumerate(spans(x.shape[2]))
    ]


def tail_of(ref, size, start=0, count=None):
    return ref.at[pl.ds(ref.shape[0] - size + start, size if count is None else count)]


def send_part(peers, x_in, b, c, dt, owner, lens, own, near, *rest):
    smalls = (own, near, *rest[: peers - 2])
    outs = (own, near, *rest[peers - 2 : 2 * peers - 4])
    dtv, x, bc, table, length, sem = rest[2 * peers - 4 :]
    slots, rows, width = x.shape
    heads = dt.shape[1]
    dp = lax.axis_index("dp")
    odd = lax.axis_index("head") % 2
    copies = Copies(sem)
    copies(owner, table)
    copies(lens, length)
    copies(dt, dtv)
    copies(x_in, x)
    copies(b, bc, odd == 0)
    copies(c, bc, odd != 0, again=True)
    copies.wait()
    t = Table([lax.axis_index("sess"), odd, length[0]], peers, slots)
    t.owner = lambda i: table[dp, i]
    count = jnp.full((heads, rows), t.length.astype(F32)).astype(BF16)
    picks = [t.slot(k) for k in range(peers)]

    def put(out, index, j, start):
        for g, lanes in enumerate(spans(width)):
            at = (index * (width // 256) + g) * HALF
            out[at : at + HALF] = x[j, start : start + HALF, lanes]

    for k in list(range(2, peers)) + [1, 0]:
        out, j = smalls[k], picks[k]
        at = out.shape[0] - rows - 2 * heads
        out[at : at + rows] = bc[j]
        value = dtv[j]
        high = value.astype(BF16)
        value = value - high.astype(F32)
        middle = value.astype(BF16)
        low = (value - middle.astype(F32)).astype(BF16)
        out[at + rows : at + rows + heads] = jnp.concatenate([high, middle], axis=1)
        out[at + rows + heads :] = jnp.concatenate([low, count], axis=1)
        if k:
            put(outs[k], 0, j, 0)
    for m in range(peers // 2):
        put(near, m + 1, picks[1 ^ 2 * m], HALF)


def forward_part(peers, slots, tab, x, near, after, *rest):
    outs, sem = rest[:-1], rest[-1]
    rows, width = x.shape[1:]
    t = Table(tab, peers, slots)
    for m in range(1, peers // 2):
        out, at = outs[m - 1], t.holder(2 * m, 0)
        wait = gather(
            sem.at[m - 1],
            out,
            [
                (at == 0, from_rows(x, t.slot(2 * m), HALF, out)),
                (at == 1, [(chunk(near, m + 1, width), out)]),
            ],
        )
        pl.when(at < 2)(wait)


def pick_part(peers, slots, heads, tab, *rest):
    got = rest[:peers]
    mine, dts, lens = rest[peers + 1 :]
    rows = mine.shape[0] - HALF
    size = rows + 2 * heads
    t = Table(tab, peers, slots)

    def choose(at, start, count):
        out = None
        for k in range(peers):
            base = got[k].shape[0] - size + start
            value = got[k][base : base + count].astype(F32)
            out = jnp.where(at == k, value, out) if k else value
        return out

    first, second = t.holder(0, 0), t.holder(0, 1)
    mine[:rows] = choose(first, 0, rows).astype(BF16)
    mine[rows:] = choose(second, 0, HALF).astype(BF16)
    for part, at in ((0, first), (1, second)):
        top = choose(at, rows, heads)
        low = choose(at, rows + heads, heads)
        dts[part] = top[:, :rows] + (top[:, rows:] + low[:, :rows])
    for j in range(slots):
        lens[j] = choose(t.far(j), rows + heads, heads)[:, rows:]


def touch_part(*refs):
    out = refs[-1]
    out[...] = jnp.zeros(out.shape, out.dtype)


def share_part(peers, slots, tab, dts, params, share0, share1, decays):
    parts, heads, rows = dts.shape
    width = share0.shape[1]
    size = width // heads
    per = 128 // size
    length = Table(tab, peers, slots).length
    alog, bias, _ = columns(params)
    rate = -jnp.exp(alog)
    col = iota((heads, rows), 1)
    lane = iota((rows, 128), 1) // size
    for part, out in ((0, share0), (1, share1)):
        step = jnp.where(col < length - part * rows, softplus(dts[part] + bias), 0.0)
        log_decay = running(rate * step)
        total = log_decay[:, rows - 1 :]
        share = jnp.transpose(jnp.exp(total - log_decay) * step)
        decays[part] = jnp.broadcast_to(jnp.exp(total).astype(BF16).astype(F32), (heads, 256))
        for p in range(width // 128):
            factor = jnp.broadcast_to(share[:, p * per : p * per + 1], (rows, 128))
            for q in range(1, per):
                factor = jnp.where(lane == q, share[:, p * per + q : p * per + q + 1], factor)
            out[:, p * 128 : (p + 1) * 128] = factor[: out.shape[0]]


def block_part(x_in, z_in, b_in, c_in, dt_in, params, yz, ez, x, z, b, c, dt, sem):
    slots, rows, width = x.shape
    heads = dt.shape[1]
    size = width // heads
    per = 128 // size
    waits = []
    for s in range(slots):
        copies = Copies(sem.at[s])
        for src, dst in ((dt_in, dt), (b_in, b), (c_in, c), (x_in, x), (z_in, z)):
            copies(src.at[s], dst.at[s])
        waits.append(copies)
    causal = iota((rows, rows), 0) >= iota((rows, rows), 1)
    lane = iota((rows, 128), 1) // size
    alog, bias, skip = columns(params)
    rate = -jnp.exp(alog)
    for s in range(slots):
        waits[s].wait()
        step = softplus(dt[s] + bias)
        log_decay = running(rate * step)
        log_col = jnp.transpose(log_decay)
        decay_col = jnp.exp(log_col)
        scores = jnp.where(causal, dot(c[s], b[s], (1, 1)), 0.0)
        for p in range(width // 128):
            lanes = slice(p * 128, (p + 1) * 128)
            xp = x[s, :, lanes]
            weights = []
            parts = []
            decay = decay_col[:, p * per : p * per + 1]
            own_skip = skip[p * per : p * per + 1]
            for q in range(per):
                h = p * per + q
                gap = jnp.minimum(log_col[:, h : h + 1] - log_decay[h : h + 1], 0.0)
                weights.append((jnp.exp(gap) * step[h : h + 1] * scores).astype(BF16))
                parts.append(jnp.where(lane == q, xp, jnp.zeros_like(xp)))
                if q:
                    decay = jnp.where(lane == q, decay_col[:, h : h + 1], decay)
                    own_skip = jnp.where(lane[:1] == q, skip[h : h + 1], own_skip)
            inner = dot(jnp.concatenate(weights, axis=1), jnp.concatenate(parts, axis=0), (1, 0))
            gate = silu(z[s, :, lanes].astype(F32))
            yz[s, :, lanes] = (inner + own_skip * xp.astype(F32)) * gate
            ez[s, :, lanes] = decay * gate


def early_part(peers, slots, tab, cache, mine, other, token, upper):
    def work(cs):
        for lanes in spans(cache.shape[0]):
            upper[:, lanes] = dot(cs[HALF : 2 * HALF], cache[lanes], (1, 1)).astype(BF16)

    odd = Table(tab, peers, slots).odd
    pl.when(odd == 0)(lambda: work(other))
    pl.when(odd != 0)(lambda: work(mine))


def late_part(peers, slots, tab, cache, mine, other, share, decays, x, near, *rest):
    half = peers // 2
    far, onward = rest[: peers - 2], rest[peers - 2 : peers - 3 + half]
    rest = rest[peers - 3 + half :]
    late, second, cars = rest[0], rest[1], rest[2 : peers + 2]
    car0, car1, bs, cs, sem = rest[peers + 2 :]
    rows, width = share.shape
    heads = decays.shape[1]
    size = width // heads
    t = Table(tab, peers, slots)
    k0, k1, j = t.holder(0, 0), t.holder(0, 1), t.slot(0)
    straight = [near] + list(far)
    count = width // 256

    def one_of(values):
        out = values[0][1]
        for pred, value in values[1:]:
            out = jnp.where(pred, value, out)
        return out

    def low(at, g, lanes):
        rest = [(at == k, straight[k - 1][g * HALF : (g + 1) * HALF].astype(F32)) for k in range(1, peers)]
        return one_of([(None, x[j, :HALF, lanes].astype(F32))] + rest)

    def high(g, lanes):
        rest = [(k0 == 1, near[(count + g) * HALF : (count + g + 1) * HALF].astype(F32))]
        rest += [
            (k0 // 2 == m, onward[m - 1][g * HALF : (g + 1) * HALF].astype(F32))
            for m in range(1, half)
        ]
        return one_of([(None, x[j, HALF:, lanes].astype(F32))] + rest)

    @pl.when(t.odd == 0)
    def _():
        bs[...] = mine[:rows]
        cs[...] = other[...]

    @pl.when(t.odd != 0)
    def _():
        bs[...] = other[:rows]
        cs[...] = mine[...]

    for lanes in spans(width):
        car0[:, lanes] = dot(cs[:HALF], cache[lanes], (1, 1)).astype(BF16)
    for g, lanes in enumerate(spans(width)):
        second[g * HALF : (g + 1) * HALF] = low(k1, g, lanes).astype(BF16)
        xv = jnp.concatenate([low(k0, g, lanes), high(g, lanes)], axis=0)
        local = dot((xv * share[:, lanes]).astype(BF16), bs[...], (0, 0)).astype(BF16).astype(F32)
        for q in range(256 // size):
            h = g * (256 // size) + q
            state = slice(h * size, (h + 1) * size)
            late[state] = (
                decays[0, h : h + 1] * cache[state].astype(F32)
                + local[q * size : (q + 1) * size]
            ).astype(BF16)
        car1[:, lanes] = dot(cs[rows:], late[lanes], (1, 1)).astype(BF16)
    waits = []
    for flag, at, src in ((0, k0, car0), (1, k1, car1)):
        choices = [(at == k, [(src, cars[k])]) for k in range(peers)]
        gather(sem.at[flag], src, choices)
        waits.append(pltpu.make_async_copy(src, cars[0], sem.at[flag]).wait)
    for wait in waits:
        wait()


def final_part(peers, slots, tab, mine, other, share, decays, late, second, final, bs):
    width = share.shape[1]
    heads = decays.shape[1]
    size = width // heads
    rows = mine.shape[0] - HALF
    odd = Table(tab, peers, slots).odd

    @pl.when(odd == 0)
    def _():
        bs[...] = mine[rows:]

    @pl.when(odd != 0)
    def _():
        bs[...] = other[rows:]

    for g, lanes in enumerate(spans(width)):
        xv = second[g * HALF : (g + 1) * HALF].astype(F32)
        local = dot((xv * share[:, lanes]).astype(BF16), bs[...], (0, 0)).astype(BF16).astype(F32)
        for q in range(256 // size):
            h = g * (256 // size) + q
            state = slice(h * size, (h + 1) * size)
            final[state] = (
                decays[1, h : h + 1] * late[state].astype(F32)
                + local[q * size : (q + 1) * size]
            ).astype(BF16)


def gate_part(peers, tab, yz, ez, *rest):
    cars, uppers = rest[:peers], rest[peers : 2 * peers]
    gated, squares = rest[2 * peers :]
    slots, rows, width = yz.shape
    t = Table(tab, peers, slots)

    def choose(at, refs, lanes):
        out = refs[0][:, lanes].astype(F32)
        for k in range(1, peers):
            out = jnp.where(at == k, refs[k][:, lanes].astype(F32), out)
        return out

    for j in range(slots):
        at = t.far(j)
        total = jnp.zeros((rows, 128), F32)
        for p in range(width // 128):
            lanes = slice(p * 128, (p + 1) * 128)
            got = jnp.concatenate([choose(at, cars, lanes), choose(at, uppers, lanes)], axis=0)
            value = yz[j, :, lanes] + ez[j, :, lanes] * got
            gated[j, :, lanes] = value
            total = total + value * value
        squares[j : j + 1] = jnp.sum(jnp.transpose(total), axis=0, keepdims=True)


def norm_part(peers, tab, gated, own, other, gain, lens, mixed, out, sem):
    slots, rows, width = gated.shape
    t = Table(tab, peers, slots)
    row = iota((rows, 128), 0).astype(F32)
    copies = Copies(sem)
    for j in range(slots):
        late = t.late(t.me * slots + j)
        live = row + (late * rows).astype(F32) < lens[j][:1]
        mean = (own[j : j + 1] + other[j : j + 1]) / (2.0 * width)
        inverse = jnp.transpose(jnp.broadcast_to(lax.rsqrt(mean + 1e-05), (rows, rows)))
        for p in range(width // 128):
            lanes = slice(p * 128, (p + 1) * 128)
            value = gated[j, :, lanes] * inverse * gain[:, lanes].astype(F32)
            out[j, :, lanes] = jnp.where(live, value, 0.0).astype(BF16)
        copies(out.at[j], mixed.at[j])
    copies.wait()


def call(kernel, outs, in_specs, out_specs=None, scratch=(), limit=24, cost=0):
    return pl.pallas_call(
        kernel,
        out_shape=outs,
        in_specs=in_specs,
        out_specs=out_specs if out_specs is not None else jax.tree.map(lambda _: VMEM, outs),
        scratch_shapes=scratch,
        compiler_params=pltpu.CompilerParams(vmem_limit_bytes=limit * 1024 * 1024),
        cost_estimate=pl.CostEstimate(flops=0, bytes_accessed=cost, transcendentals=0),
    )


def per_device(
    x_rows,
    z_rows,
    input_projection_matrix,
    c_rows,
    dt_raw,
    a_log,
    dt_bias,
    d_skip,
    norm_gain,
    cache_state,
    lengths,
    slot_owner,
    slot_task,
):
    slots, rows, width = x_rows.shape
    heads = dt_raw.shape[1]
    state = cache_state.shape[3]
    peers = lax.axis_size("sess")
    half = peers // 2
    head = lax.axis_index("head")
    groups = input_projection_matrix.shape[2] // state
    if groups > 1:
        at = head // 2 * state
        b = lax.dynamic_slice_in_dim(input_projection_matrix, at, state, 2)
        c = lax.dynamic_slice_in_dim(c_rows, at, state, 2)
    else:
        b, c = input_projection_matrix, c_rows

    def own_row(table):
        mine = iota(table.shape, 0) == lax.axis_index("dp")
        return jnp.sum(jnp.where(mine, table, 0), axis=0)

    ids = jnp.stack([lax.axis_index("sess"), head % 2]).astype(jnp.int32)
    tab = jnp.concatenate([ids, lengths, own_row(slot_owner), own_row(slot_task)])
    params = jnp.stack([a_log, dt_bias, d_skip])
    cache = cache_state.reshape(width, state)

    def far(value, k):
        return lax.ppermute(value, "sess", [(i, i ^ k) for i in range(peers)])

    def swapped(value):
        count = lax.axis_size("head")
        return lax.ppermute(value, "head", [(i, i ^ 1) for i in range(count)])

    def scratch(*sizes, dtype=BF16):
        return pltpu.VMEM(sizes, dtype)

    shape = jax.ShapeDtypeStruct
    dma = lambda *sizes: pltpu.SemaphoreType.DMA(sizes)
    bind = lambda kernel, *more: functools.partial(kernel, peers, *more)
    count = width // 256
    piece = count * HALF
    tail = rows + 2 * heads
    packed = lambda size: shape((size, 256), BF16)
    upper_rows = shape((HALF, width), BF16)
    own, near, *rest = call(
        bind(send_part),
        [packed(tail), packed((1 + half) * piece + tail)]
        + [packed(tail)] * (peers - 2)
        + [packed(piece)] * (peers - 2),
        [HBM] * 6,
        scratch=[
            scratch(*dt_raw.shape, dtype=F32),
            scratch(*x_rows.shape),
            scratch(*b.shape),
            pltpu.SMEM(slot_owner.shape, jnp.int32),
            pltpu.SMEM(lengths.shape, jnp.int32),
            dma(5),
        ],
        limit=60,
    )(x_rows, b, c, dt_raw, slot_owner, lengths)
    near = far(near, 1)
    smalls = [far(value, k + 2) for k, value in enumerate(rest[: peers - 2])]
    sends = [far(value, k + 2) for k, value in enumerate(rest[peers - 2 :])]
    yz, ez = call(
        block_part,
        [shape(x_rows.shape, F32)] * 2,
        [HBM] * 5 + [VMEM],
        scratch=[
            scratch(*x_rows.shape),
            scratch(*x_rows.shape),
            scratch(*b.shape),
            scratch(*b.shape),
            scratch(*dt_raw.shape, dtype=F32),
            dma(slots, 5),
        ],
    )(x_rows, z_rows, b, c, dt_raw, params)
    passing = call(
        bind(forward_part, slots),
        [packed(piece)] * (half - 1),
        [SMEM, HBM, ANY, ANY],
        [ANY] * (half - 1),
        [dma(half - 1)],
    )(tab, x_rows, near, ez)
    onward = [far(value, 2 * (m + 1)) for m, value in enumerate(passing)]
    mine, dts, lens = call(
        bind(pick_part, slots, heads),
        [
            shape((rows + HALF, state), BF16),
            shape((2, heads, rows), F32),
            shape((slots, heads, rows), F32),
        ],
        [SMEM] + [VMEM] * peers + [ANY],
    )(tab, own, near, *smalls, passing[0])
    other = swapped(mine)
    share0, share1, decays = call(
        bind(share_part, slots),
        [shape((rows, width), F32), shape((HALF, width), F32), shape((2, heads, 256), F32)],
        [SMEM, VMEM, VMEM],
    )(tab, dts, params)
    token = call(touch_part, shape((8, 128), F32), [ANY] * (peers - 2), cost=40_000_000)(*sends)
    upper = call(
        bind(early_part, slots), upper_rows, [SMEM, VMEM, VMEM, VMEM, ANY]
    )(tab, cache, mine, other, token)
    uppers = {2 * m: far(upper, 2 * m) if m else upper for m in range(half)}
    late, second, *cars = call(
        bind(late_part, slots),
        [shape((width, state), BF16), packed(piece)] + [upper_rows] * peers,
        [SMEM] + [VMEM] * (5 + 1 + peers + half - 2),
        [VMEM, VMEM] + [ANY] * peers,
        [
            scratch(HALF, width),
            scratch(HALF, width),
            scratch(rows, state),
            scratch(rows + HALF, state),
            dma(3),
        ],
    )(tab, cache, mine, other, share0, decays, x_rows, near, *sends, *onward)
    cars = {0: cars[0]} | {k: far(cars[k], k) for k in list(range(2, peers)) + [1]}
    uppers |= {2 * m + 1: far(uppers[2 * m], 1) for m in range(half)}
    final = call(
        bind(final_part, slots),
        shape((width, state), BF16),
        [SMEM] + [VMEM] * 6,
        scratch=[scratch(HALF, state)],
    )(tab, mine, other, share1, decays, late, second)
    gated, squares = call(
        bind(gate_part),
        [shape(x_rows.shape, F32), shape((slots, rows), F32)],
        [SMEM] + [VMEM] * (2 + 2 * peers),
    )(
        tab,
        yz,
        ez,
        *[cars[k] for k in range(peers)],
        *[uppers[k] for k in range(peers)],
    )
    mixed_rows = call(bind(norm_part), shape(x_rows.shape, BF16), [SMEM] + [VMEM] * 5, ANY, [scratch(*x_rows.shape), dma(slots)])(
        tab, gated, squares, swapped(squares), norm_gain[None], lens
    )
    return (mixed_rows, final.reshape(cache_state.shape))


def solution(mesh):
    in_specs = (
        P(("group", "sess", "dp"), None, "head"),
        P(("group", "sess", "dp"), None, "head"),
        P(("group", "sess", "dp"), None, None),
        P(("group", "sess", "dp"), None, None),
        P(("group", "sess", "dp"), "head", None),
        P("head"),
        P("head"),
        P("head"),
        P("head"),
        P(("group", "sess", "dp"), "head", None, None),
        P(("group", "sess", "dp")),
        P("group", None),
        P("group", None),
    )
    out_specs = (
        P(("group", "sess", "dp"), None, "head"),
        P(("group", "sess", "dp"), "head", None, None),
    )
    return jax.shard_map(
        per_device, mesh=mesh, in_specs=in_specs, out_specs=out_specs, check_vma=False
    )
```
